512 devices in a mesh: row: 16 (over z_hi, x, core), col: 32 (over y, z_lo).
Axes of the slice: x: 4, y: 4, z: 16 (z_hi: 2, z_lo: 8; z = z_hi * 8 + z_lo), core: 2. Of those that a mesh axis runs over, the one named last changes fastest.
Arguments:
- volt_init: float32 [128, 512, 400], P('row', 'col'), may hold values from -6 to 6
- curr_init: float32 [128, 512, 400], P('row', 'col'), may hold values from -6 to 6
- local_inverse: bfloat16 [128, 400, 400], P('row'), may hold values from -1 to 2, as said below
- schur_inverse: bfloat16 [4096, 4096], P('row', 'col'), may hold values from -1 to 2, as said below
- ind_gain: float32 [128, 400], P('row'), may hold values from 0.05 to 0.5
- tie: float32 [128, 64], P('row'), may hold values from 0.3 to 3
- port_map: int32 [128, 64], P('row'), may hold values from 0 to 4095
- breaker: int32 [128, 512, 400], P('row', 'col'), may hold values 0 or 1
- fault_time: int32 [512], P('col'), may hold values from 0 to 2
- fault_node: int32 [512], P('col'), may hold values from 0 to 51199
Outputs:
- volt_final: float32 [128, 512, 400], P('row', 'col')
- curr_final: float32 [128, 512, 400], P('row', 'col')
- iface_volt: float32 [512, 4096], P('col', 'row')
The draws below stay inside these ranges and needn't reach their ends.
Inputs may be any that keep to these rules, and one draw needn't show every extreme that they name: `local_inverse`: diagonal entries between 0.5 and 1.5; off-diagonal entries independent. `schur_inverse`: diagonal entries between 0.5 and 1.5; off-diagonal entries independent.
All inputs are finite; a program needn't handle non-finite values. No bound on the sum of `breaker` on one device may be relied on, other than what follows from the above.
Results may differ from the reference program's by a relative error of at most 0.0068.
Values may be sent and summed in bfloat16 or wider, within the bound.
No kernel may reach another device: no remote copies, remote signals or barrier semaphores. Data moves between devices by JAX's collectives and lax.ppermute only.
A program may use at most 64 MiB of HBM per device.

```python
import math
import jax
import jax.numpy as jnp
from jax import lax

NODES = 400
PORTS = 64
NI = 4096
STEPS = 2
SUBNETS = 128
SCEN = 512


def dominant(key, count, order):
    first, second = jax.random.split(key)
    diag = jax.random.uniform(first, (count, order), jnp.float32, 0.5, 1.5)
    return (diag, second)


def draw_local_inverse(key, part):
    key = jax.random.fold_in(key, 11)
    diag, second = dominant(key, SUBNETS, NODES)
    shape = (SUBNETS, NODES, NODES)
    off_diag = jnp.clip(jax.random.normal(second, shape, jnp.float32), -5.0, 5.0)
    off_diag = off_diag * (0.6 / math.sqrt(NODES))
    rows = lax.broadcasted_iota(jnp.int32, shape, 1)
    cols = lax.broadcasted_iota(jnp.int32, shape, 2)
    full = jnp.where(rows == cols, diag[:, :, None], off_diag)
    return full.astype(jnp.bfloat16)


def draw_schur_inverse(key, part):
    key = jax.random.fold_in(key, 12)
    diag, second = dominant(key, 1, NI)
    shape = (NI, NI)
    off_diag = jnp.clip(jax.random.normal(second, shape, jnp.float32), -5.0, 5.0)
    off_diag = off_diag * (0.6 / math.sqrt(NI))
    rows = lax.broadcasted_iota(jnp.int32, shape, 0)
    cols = lax.broadcasted_iota(jnp.int32, shape, 1)
    full = jnp.where(rows == cols, diag[0][:, None], off_diag)
    return full.astype(jnp.bfloat16)


def set_ends(values, stream_key, low, largest):
    place = [jax.random.randint(jax.random.fold_in(stream_key, axis), (), 0, length) for axis, length in enumerate(values.shape)]
    longest = values.shape.index(max(values.shape))
    next_to = place[:longest] + [(place[longest] + 1) % values.shape[longest]] + place[longest + 1:]
    return values.at[tuple(place)].set(low).at[tuple(next_to)].set(largest)


def steps_of(rng, dims, cuts, low, top_value):
    loudness = 1.0
    for position, shards_of in cuts:
        draws = jax.random.uniform(jax.random.fold_in(jax.random.fold_in(rng, 6), position), (shards_of,), jnp.float32, low / len(cuts), top_value / len(cuts))
        loudness = loudness * jnp.repeat(jnp.exp(draws), dims[position] // shards_of).reshape((-1,) + (1,) * (len(dims) - 1 - position))
    return loudness


def bell_draw(key, dims, width, bound, cuts=(), kind=jnp.bfloat16):
    level = steps_of(key, dims, cuts, -0.22, 0.18) if cuts else 1.0
    values = jax.random.normal(key, dims, jnp.float32) * width * level
    return jnp.minimum(jnp.maximum(values, -bound), bound).astype(kind)


def setup_inputs(seed: int = 0) -> dict:
    key_of = jax.random.split(jax.random.key(seed), 11)
    volt_init = bell_draw(key_of[0], (SUBNETS, SCEN, NODES), 1.0, 6.0, ((0, 16), (1, 32)), jnp.float32)
    curr_init = bell_draw(key_of[1], (SUBNETS, SCEN, NODES), 1.0, 6.0, ((0, 16), (1, 32)), jnp.float32)
    local_inverse = draw_local_inverse(jax.random.fold_in(key_of[10], 71), 0)
    schur_inverse = draw_schur_inverse(jax.random.fold_in(key_of[10], 71), 0)
    ind_gain = jnp.clip(jnp.exp(math.log(0.5) - 2.3025851 * jax.random.uniform(key_of[4], (SUBNETS, NODES), jnp.float32) ** steps_of(key_of[4], (SUBNETS, NODES), ((0, 16),), -0.2, 0.2)), 0.05, 0.5)
    tie = jnp.clip(jnp.exp(math.log(3.0) - 2.3025851 * jax.random.uniform(key_of[5], (SUBNETS, PORTS), jnp.float32) ** steps_of(key_of[5], (SUBNETS, PORTS), ((0, 16),), -0.2, 0.2)), 0.3, 3.0)
    port_map = set_ends(jax.random.randint(key_of[6], (SUBNETS, PORTS), 0, NI), jax.random.fold_in(key_of[6], 1), 0, NI - 1).astype(jnp.int32)
    breaker = set_ends((jax.random.randint(key_of[7], (SUBNETS, SCEN, NODES), 0, 8) < 7).astype(jnp.int32), jax.random.fold_in(key_of[7], 1), 0, 1)
    fault_time = set_ends(jax.random.randint(key_of[8], (SCEN,), 0, STEPS + 1), jax.random.fold_in(key_of[8], 1), 0, STEPS).astype(jnp.int32)
    fault_node = set_ends(jax.random.randint(key_of[9], (SCEN,), 0, SUBNETS * NODES), jax.random.fold_in(key_of[9], 1), 0, (SUBNETS * NODES) - 1).astype(jnp.int32)
    return {"volt_init": volt_init, "curr_init": curr_init, "local_inverse": local_inverse, "schur_inverse": schur_inverse, "ind_gain": ind_gain, "tie": tie, "port_map": port_map, "breaker": breaker, "fault_time": fault_time, "fault_node": fault_node}


def reference(volt_init, curr_init, local_inverse, schur_inverse, ind_gain, tie, port_map, breaker, fault_time, fault_node):
    volt = volt_init
    curr = curr_init
    closed = breaker.astype(jnp.float32)
    inverse_wide = local_inverse.astype(jnp.float32)
    schur_wide = schur_inverse.astype(jnp.float32)
    node_ids = (jnp.arange(SUBNETS, dtype=jnp.int32)[:, None] * NODES + jnp.arange(NODES, dtype=jnp.int32)[None, :])
    hits = (node_ids[:, None, :] == fault_node[None, :, None])
    flat_map = port_map.reshape(-1)
    iface_volt = jnp.zeros((SCEN, NI), jnp.float32)
    for step in range(STEPS):
        hist = closed * (curr + ind_gain[:, None, :] * volt)
        active = (step >= fault_time)[None, :, None]
        fault_on = jnp.where(hits & active, 1.0, 0.0).astype(jnp.float32)
        inject = (-hist - 2.0 * fault_on * volt).astype(jnp.bfloat16)
        open_volt = jnp.einsum("ksn,knm->ksm", inject.astype(jnp.float32), inverse_wide, precision=lax.Precision.HIGHEST)
        values = tie[:, None, :] * open_volt[:, :, :PORTS]
        flat_values = jnp.transpose(values, (0, 2, 1)).reshape(SUBNETS * PORTS, SCEN)
        iface_rhs = jax.ops.segment_sum(flat_values, flat_map, NI).T
        rhs_half = iface_rhs.astype(jnp.bfloat16)
        iface_volt = lax.dot_general(rhs_half.astype(jnp.float32), schur_wide, (((1,), (1,)), ((), ())), precision=lax.Precision.HIGHEST)
        picked = jnp.take(iface_volt, flat_map, axis=1).reshape(SCEN, SUBNETS, PORTS)
        drive = (tie[:, None, :] * jnp.transpose(picked, (1, 0, 2))).astype(jnp.bfloat16)
        volt_next = open_volt + jnp.einsum("ksp,kpn->ksn", drive.astype(jnp.float32), inverse_wide[:, :PORTS, :], precision=lax.Precision.HIGHEST)
        curr = closed * (curr + ind_gain[:, None, :] * (volt_next + volt))
        volt = volt_next
    return volt, curr, iface_volt
```

```python
import functools

import jax
import jax.numpy as jnp
from jax import lax
from jax.experimental import pallas as pl
from jax.experimental.pallas import tpu as pltpu
from jax.sharding import PartitionSpec as P

ROWS = 16
COLS = 32
SUBS = 8
SCEN = 16
NODES = 400
PORTS = 64
OWN = SUBS * PORTS
BLOCK = 256
LANES = 128
TILES = OWN // LANES
VALUE_ROWS = TILES * SCEN
Z_GROUPS = [[8 * y + z for z in range(8)] for y in range(4)]
Y_GROUPS = [[8 * y + z for y in range(4)] for z in range(8)]
VMEM_BYTES = 40 << 20

NN = (((1,), (0,)), ((), ()))
NT = (((1,), (1,)), ((), ()))


def dot(a, b, dims=NN):
    return lax.dot_general(a, b, dims, preferred_element_type=jnp.float32)


def flat_row(ref):
    return jnp.concatenate([ref[k : k + 1, :] for k in range(SUBS)], axis=1)


def column(ref):
    place = lax.broadcasted_iota(jnp.int32, (SCEN, 1), 0)
    out = jnp.zeros((SCEN, 1), jnp.int32)
    for s in range(SCEN):
        out = jnp.where(place == s, ref[s], out)
    return out


def open_circuit(step, volts, currs, closed, gain_ref, inv_wait, inv_ref, time_ref, node_ref, tie_ref, open_ref, send_ref):
    fault_node = column(node_ref)
    active = step >= column(time_ref)
    fault_node = jnp.where(active, fault_node, -1)
    first = lax.axis_index("row") * SUBS
    lane = lax.broadcasted_iota(jnp.int32, (SCEN, NODES), 1)
    parts = []
    for k in range(SUBS):
        volt = volts(k)
        hist = closed(k) * (currs(k) + gain_ref[k : k + 1, :] * volt)
        hit = lane + (first + k) * NODES == fault_node
        inject = (-hist - jnp.where(hit, 2.0 * volt, 0.0)).astype(jnp.bfloat16)
        inv_wait(k)
        open_k = dot(inject, inv_ref[k])
        open_ref[k] = open_k
        parts.append(tie_ref[k : k + 1, :] * open_k[:, :PORTS])
    values = jnp.concatenate(parts, axis=1).astype(jnp.bfloat16)
    for r in range(ROWS):
        for t in range(TILES):
            send_ref[r, t * SCEN : (t + 1) * SCEN, :] = values[:, t * LANES : (t + 1) * LANES]


def inverse_copies(inv_hbm, inv_ref, sems):
    copies = [pltpu.make_async_copy(inv_hbm.at[k], inv_ref.at[k], sems.at[k]) for k in range(SUBS)]
    for copy in copies:
        copy.start()
    return copies


def first_kernel(time_ref, node_ref, volt_ref, curr_ref, breaker_ref, gain_ref, tie_ref, map_ref, inv_hbm, open_ref, send_ref, inv_ref, sems):
    copies = inverse_copies(inv_hbm, inv_ref, sems)
    mapped = flat_row(map_ref)
    rows = [(mapped // BLOCK).astype(jnp.float32), (mapped % BLOCK).astype(jnp.float32)]
    rows = [row[:, t * LANES : (t + 1) * LANES] for row in rows for t in range(TILES)]
    tail = jnp.concatenate(rows + [jnp.zeros((16 - len(rows), LANES), jnp.float32)], axis=0).astype(jnp.bfloat16)
    for r in range(ROWS):
        send_ref[r, VALUE_ROWS : VALUE_ROWS + 16, :] = tail
    open_circuit(
        0,
        lambda k: volt_ref[k],
        lambda k: curr_ref[k],
        lambda k: breaker_ref[k].astype(jnp.float32),
        gain_ref,
        lambda k: copies[k].wait(),
        inv_ref,
        time_ref,
        node_ref,
        tie_ref,
        open_ref,
        send_ref,
    )


def interface_kernel(recv_ref, map_ref, schur_hbm, iface_ref, send_ref, schur_ref, sems):
    copies = [pltpu.make_async_copy(schur_hbm.at[y], schur_ref.at[y], sems.at[y]) for y in range(4)]
    for copy in copies:
        copy.start()
    low = lax.broadcasted_iota(jnp.int32, (BLOCK, OWN), 0)
    rhs = jnp.zeros((ROWS * SCEN, BLOCK), jnp.float32)
    for r in range(ROWS):
        tail = map_ref[r, VALUE_ROWS : VALUE_ROWS + 16, :].astype(jnp.float32)
        hi = jnp.concatenate([tail[t : t + 1] for t in range(TILES)], axis=1).astype(jnp.int32)
        lo = jnp.concatenate([tail[TILES + t : TILES + t + 1] for t in range(TILES)], axis=1).astype(jnp.int32)
        values = jnp.concatenate([recv_ref[r, t * SCEN : (t + 1) * SCEN, :] for t in range(TILES)], axis=1)
        values = values.astype(jnp.float32)
        left = jnp.concatenate([jnp.where(hi == h, values, 0.0) for h in range(ROWS)], axis=0).astype(jnp.bfloat16)
        right = jnp.where(low == lo, 1.0, 0.0).astype(jnp.bfloat16)
        rhs += dot(left, right, NT)
    rhs = rhs.astype(jnp.bfloat16)
    total = jnp.zeros((SCEN, BLOCK), jnp.float32)
    for h in range(ROWS):
        if h % 4 == 0:
            copies[h // 4].wait()
        pair = schur_ref[h // 4, 2 * (h % 4)], schur_ref[h // 4, 2 * (h % 4) + 1]
        total += dot(rhs[h * SCEN : (h + 1) * SCEN, :], jnp.concatenate(pair, axis=1), NT)
    iface_ref[...] = total
    half = total.astype(jnp.bfloat16)
    for r in range(ROWS):
        send_ref[r] = half


def driven(recv_ref, map_ref, tie_ref):
    mapped = flat_row(map_ref)
    hi = mapped // BLOCK
    low = lax.broadcasted_iota(jnp.int32, (BLOCK, OWN), 0)
    right = jnp.where(low == mapped % BLOCK, 1.0, 0.0).astype(jnp.bfloat16)
    found = dot(recv_ref[...].reshape(ROWS * SCEN, BLOCK), right)
    picked = jnp.zeros((SCEN, OWN), jnp.float32)
    for r in range(ROWS):
        picked += jnp.where(hi == r, found[r * SCEN : (r + 1) * SCEN, :], 0.0)
    return (flat_row(tie_ref) * picked).astype(jnp.bfloat16)


def update(k, drive, open_ref, inv, volt, curr_ref, breaker_ref, gain_ref):
    volt_next = open_ref[k] + dot(drive[:, k * PORTS : (k + 1) * PORTS], inv)
    closed = breaker_ref[k].astype(jnp.float32)
    curr = closed * (curr_ref[k] + gain_ref[k : k + 1, :] * (volt_next + volt))
    return volt_next, curr


def middle_kernel(time_ref, node_ref, recv_ref, open_prev_ref, volt_ref, curr_ref, breaker_ref, gain_ref, tie_ref, map_ref, inv_hbm, volt_out, curr_out, open_ref, send_ref, inv_ref, sems):
    copies = inverse_copies(inv_hbm, inv_ref, sems)
    drive = driven(recv_ref, map_ref, tie_ref)
    for k in range(SUBS):
        copies[k].wait()
        volt_out[k], curr_out[k] = update(k, drive, open_prev_ref, inv_ref[k, :PORTS, :], volt_ref[k], curr_ref, breaker_ref, gain_ref)
    open_circuit(
        1,
        lambda k: volt_out[k],
        lambda k: curr_out[k],
        lambda k: breaker_ref[k].astype(jnp.float32),
        gain_ref,
        lambda k: None,
        inv_ref,
        time_ref,
        node_ref,
        tie_ref,
        open_ref,
        send_ref,
    )


def last_kernel(recv_ref, open_prev_ref, volt_ref, curr_ref, breaker_ref, gain_ref, tie_ref, map_ref, inv_hbm, volt_out, curr_out, inv_ref, sems):
    copies = [pltpu.make_async_copy(inv_hbm.at[k, :PORTS], inv_ref.at[k], sems.at[k]) for k in range(SUBS)]
    for copy in copies:
        copy.start()
    drive = driven(recv_ref, map_ref, tie_ref)
    for k in range(SUBS):
        copies[k].wait()
        volt_out[k], curr_out[k] = update(k, drive, open_prev_ref, inv_ref[k], volt_ref[k], curr_ref, breaker_ref, gain_ref)


SMEM = pl.BlockSpec(memory_space=pltpu.SMEM)
VMEM = pl.BlockSpec(memory_space=pltpu.VMEM)
ANY = pl.BlockSpec(memory_space=pl.ANY)


def call(body, ins, outs, scratch, flops, moved):
    return pl.pallas_call(
        body,
        out_shape=[jax.ShapeDtypeStruct(shape, kind) for shape, kind in outs],
        in_specs=ins,
        out_specs=[VMEM] * len(outs),
        scratch_shapes=scratch,
        compiler_params=pltpu.CompilerParams(vmem_limit_bytes=VMEM_BYTES),
        cost_estimate=pl.CostEstimate(flops=flops, bytes_accessed=moved, transcendentals=0),
    )


STATE = ((SUBS, SCEN, NODES), jnp.float32)
INVERSE = [pltpu.VMEM((SUBS, NODES, NODES), jnp.bfloat16), pltpu.SemaphoreType.DMA((SUBS,))]
OPEN_FLOPS = 2 * SUBS * SCEN * NODES * NODES


def local(volt, curr, local_inverse, schur_inverse, ind_gain, tie, port_map, breaker, fault_time, fault_node):
    with jax.named_scope("schur_rows"):
        blocks = jnp.broadcast_to(schur_inverse[None], (8, BLOCK, LANES))
        blocks = lax.all_to_all(blocks, "col", 0, 0, axis_index_groups=Z_GROUPS)
        blocks = jnp.broadcast_to(blocks[None], (4, 8, BLOCK, LANES))
        schur_rows = lax.all_to_all(blocks, "col", 0, 0, axis_index_groups=Y_GROUPS)

    first = call(
        first_kernel,
        [SMEM] * 2 + [VMEM] * 6 + [ANY],
        [STATE, ((ROWS, VALUE_ROWS + 16, LANES), jnp.bfloat16)],
        INVERSE,
        OPEN_FLOPS,
        4 << 20,
    )
    interface = call(
        interface_kernel,
        [VMEM] * 2 + [ANY],
        [((SCEN, BLOCK), jnp.float32), ((ROWS, SCEN, BLOCK), jnp.bfloat16)],
        [pltpu.VMEM((4, 8, BLOCK, LANES), jnp.bfloat16), pltpu.SemaphoreType.DMA((4,))],
        2 * 256 * 256 * 8192,
        3 << 20,
    )
    middle = call(
        middle_kernel,
        [SMEM] * 2 + [VMEM] * 8 + [ANY],
        [STATE, STATE, STATE, ((ROWS, VALUE_ROWS, LANES), jnp.bfloat16)],
        INVERSE,
        OPEN_FLOPS,
        4 << 20,
    )
    last = call(
        last_kernel,
        [VMEM] * 8 + [ANY],
        [STATE, STATE],
        [pltpu.VMEM((SUBS, PORTS, NODES), jnp.bfloat16), pltpu.SemaphoreType.DMA((SUBS,))],
        OPEN_FLOPS // 8,
        2 << 20,
    )

    exchange = functools.partial(lax.all_to_all, axis_name="row", split_axis=0, concat_axis=0)
    opened, send = first(fault_time, fault_node, volt, curr, breaker, ind_gain, tie, port_map, local_inverse)
    maps = exchange(send)
    _, send = interface(maps, maps, schur_rows)
    volt, curr, opened, send = middle(fault_time, fault_node, exchange(send), opened, volt, curr, breaker, ind_gain, tie, port_map, local_inverse)
    iface_block, send = interface(exchange(send), maps, schur_rows)
    volt, curr = last(exchange(send), opened, volt, curr, breaker, ind_gain, tie, port_map, local_inverse)
    return volt, curr, iface_block


def solution(mesh):
    placed = (
        P("row", "col", None),
        P("row", "col", None),
        P("row", None, None),
        P("row", "col"),
        P("row", None),
        P("row", None),
        P("row", None),
        P("row", "col", None),
        P("col"),
        P("col"),
    )
    return jax.shard_map(
        local,
        mesh=mesh,
        in_specs=placed,
        out_specs=(P("row", "col", None), P("row", "col", None), P("col", "row")),
        check_vma=False,
    )
```

```python
import functools

import jax
import jax.numpy as jnp
from jax import lax
from jax.experimental import pallas as pl
from jax.experimental.pallas import tpu as pltpu
from jax.sharding import PartitionSpec as P

ROWS = 16
COLS = 32
SUBS = 8
SCEN = 16
NODES = 400
PORTS = 64
OWN = SUBS * PORTS
BLOCK = 256
LANES = 128
TILES = OWN // LANES
VALUE_ROWS = TILES * SCEN
QUADS = [[4 * q + z for z in range(4)] for q in range(8)]
VMEM_BYTES = 40 << 20
ALL_VMEM = 60 << 20

NN = (((1,), (0,)), ((), ()))
NT = (((1,), (1,)), ((), ()))


def dot(a, b, dims=NN):
    return lax.dot_general(a, b, dims, preferred_element_type=jnp.float32)


def flat_row(ref):
    return jnp.concatenate([ref[k : k + 1, :] for k in range(SUBS)], axis=1)


def column(ref):
    place = lax.broadcasted_iota(jnp.int32, (SCEN, 1), 0)
    out = jnp.zeros((SCEN, 1), jnp.int32)
    for s in range(SCEN):
        out = jnp.where(place == s, ref[s], out)
    return out


def open_circuit(step, volts, currs, closed, gain_ref, inv_wait, inv_ref, time_ref, node_ref, tie_ref, open_ref, send_ref):
    fault_node = column(node_ref)
    active = step >= column(time_ref)
    fault_node = jnp.where(active, fault_node, -1)
    first = lax.axis_index("row") * SUBS
    lane = lax.broadcasted_iota(jnp.int32, (SCEN, NODES), 1)
    parts = []
    for k in range(SUBS):
        volt = volts(k)
        hist = closed(k) * (currs(k) + gain_ref[k : k + 1, :] * volt)
        hit = lane + (first + k) * NODES == fault_node
        inject = (-hist - jnp.where(hit, 2.0 * volt, 0.0)).astype(jnp.bfloat16)
        inv_wait(k)
        open_k = dot(inject, inv_ref[k])
        open_ref[k] = open_k
        parts.append(tie_ref[k : k + 1, :] * open_k[:, :PORTS])
    values = jnp.concatenate(parts, axis=1).astype(jnp.bfloat16)
    for r in range(ROWS):
        for t in range(TILES):
            send_ref[r, t * SCEN : (t + 1) * SCEN, :] = values[:, t * LANES : (t + 1) * LANES]


def inverse_copies(inv_hbm, inv_ref, sems):
    copies = [pltpu.make_async_copy(inv_hbm.at[k], inv_ref.at[k], sems.at[k]) for k in range(SUBS)]
    for copy in copies:
        copy.start()
    return copies


def first_kernel(time_ref, node_ref, volt_ref, curr_ref, breaker_ref, gain_ref, tie_ref, map_ref, inv_hbm, open_ref, send_ref, inv_ref, sems):
    copies = inverse_copies(inv_hbm, inv_ref, sems)
    mapped = flat_row(map_ref)
    rows = [(mapped // BLOCK).astype(jnp.float32), (mapped % BLOCK).astype(jnp.float32)]
    rows = [row[:, t * LANES : (t + 1) * LANES] for row in rows for t in range(TILES)]
    tail = jnp.concatenate(rows + [jnp.zeros((16 - len(rows), LANES), jnp.float32)], axis=0).astype(jnp.bfloat16)
    for r in range(ROWS):
        send_ref[r, VALUE_ROWS : VALUE_ROWS + 16, :] = tail
    open_circuit(
        0,
        lambda k: volt_ref[k],
        lambda k: curr_ref[k],
        lambda k: breaker_ref[k].astype(jnp.float32),
        gain_ref,
        lambda k: copies[k].wait(),
        inv_ref,
        time_ref,
        node_ref,
        tie_ref,
        open_ref,
        send_ref,
    )


def interface_kernel(recv_ref, map_ref, *refs):
    parts, (iface_ref, send_ref, schur_ref, rhs_ref, sems) = refs[:4], refs[4:]
    copies = [pltpu.make_async_copy(parts[n], schur_ref.at[n], sems.at[n]) for n in range(4)]
    for copy in copies:
        copy.start()
    low = lax.broadcasted_iota(jnp.int32, (BLOCK, OWN), 0)
    rhs = jnp.zeros((ROWS * SCEN, BLOCK), jnp.float32)
    for r in range(ROWS):
        tail = map_ref[r, VALUE_ROWS : VALUE_ROWS + 16, :].astype(jnp.float32)
        hi = jnp.concatenate([tail[t : t + 1] for t in range(TILES)], axis=1).astype(jnp.int32)
        lo = jnp.concatenate([tail[TILES + t : TILES + t + 1] for t in range(TILES)], axis=1).astype(jnp.int32)
        values = jnp.concatenate([recv_ref[r, t * SCEN : (t + 1) * SCEN, :] for t in range(TILES)], axis=1)
        values = values.astype(jnp.float32)
        left = jnp.concatenate([jnp.where(hi == h, values, 0.0) for h in range(ROWS)], axis=0).astype(jnp.bfloat16)
        right = jnp.where(low == lo, 1.0, 0.0).astype(jnp.bfloat16)
        rhs += dot(left, right, NT)
    rhs_ref[...] = rhs.astype(jnp.bfloat16).reshape(ROWS, SCEN, BLOCK)
    col = lax.axis_index("col")
    own_y, own_half = col // 8, (col // 4) % 2
    total = jnp.zeros((SCEN, BLOCK), jnp.float32)
    for n in range(4):
        copies[n].wait()
        for other in range(2):
            first = 4 * ((own_y + 4 - n) % 4) + 2 * ((own_half + other) % 2)
            for p in range(2):
                pair = schur_ref[n, 2 * p, other], schur_ref[n, 2 * p + 1, other]
                total += dot(rhs_ref[first + p], jnp.concatenate(pair, axis=1), NT)
    iface_ref[...] = total
    half = total.astype(jnp.bfloat16)
    for r in range(ROWS):
        send_ref[r] = half


def driven(recv_ref, map_ref, tie_ref):
    mapped = flat_row(map_ref)
    hi = mapped // BLOCK
    low = lax.broadcasted_iota(jnp.int32, (BLOCK, OWN), 0)
    right = jnp.where(low == mapped % BLOCK, 1.0, 0.0).astype(jnp.bfloat16)
    found = dot(recv_ref[...].reshape(ROWS * SCEN, BLOCK), right)
    picked = jnp.zeros((SCEN, OWN), jnp.float32)
    for r in range(ROWS):
        picked += jnp.where(hi == r, found[r * SCEN : (r + 1) * SCEN, :], 0.0)
    return (flat_row(tie_ref) * picked).astype(jnp.bfloat16)


def update(k, drive, open_ref, inv, volt, curr_ref, breaker_ref, gain_ref):
    volt_next = open_ref[k] + dot(drive[:, k * PORTS : (k + 1) * PORTS], inv)
    closed = breaker_ref[k].astype(jnp.float32)
    curr = closed * (curr_ref[k] + gain_ref[k : k + 1, :] * (volt_next + volt))
    return volt_next, curr


def middle_kernel(time_ref, node_ref, recv_ref, open_prev_ref, volt_ref, curr_ref, breaker_ref, gain_ref, tie_ref, map_ref, inv_hbm, volt_out, curr_out, open_ref, send_ref, inv_ref, sems):
    copies = inverse_copies(inv_hbm, inv_ref, sems)
    drive = driven(recv_ref, map_ref, tie_ref)
    for k in range(SUBS):
        copies[k].wait()
        volt_out[k], curr_out[k] = update(k, drive, open_prev_ref, inv_ref[k, :PORTS, :], volt_ref[k], curr_ref, breaker_ref, gain_ref)
    open_circuit(
        1,
        lambda k: volt_out[k],
        lambda k: curr_out[k],
        lambda k: breaker_ref[k].astype(jnp.float32),
        gain_ref,
        lambda k: None,
        inv_ref,
        time_ref,
        node_ref,
        tie_ref,
        open_ref,
        send_ref,
    )


def last_kernel(recv_ref, open_prev_ref, volt_ref, curr_ref, breaker_ref, gain_ref, tie_ref, map_ref, inv_hbm, volt_out, curr_out, inv_ref, sems):
    copies = [pltpu.make_async_copy(inv_hbm.at[k, :PORTS], inv_ref.at[k], sems.at[k]) for k in range(SUBS)]
    for copy in copies:
        copy.start()
    drive = driven(recv_ref, map_ref, tie_ref)
    for k in range(SUBS):
        copies[k].wait()
        volt_out[k], curr_out[k] = update(k, drive, open_prev_ref, inv_ref[k], volt_ref[k], curr_ref, breaker_ref, gain_ref)


SMEM = pl.BlockSpec(memory_space=pltpu.SMEM)
VMEM = pl.BlockSpec(memory_space=pltpu.VMEM)
ANY = pl.BlockSpec(memory_space=pl.ANY)


def call(body, ins, outs, scratch, flops, moved, vmem=VMEM_BYTES):
    return pl.pallas_call(
        body,
        out_shape=[jax.ShapeDtypeStruct(shape, kind) for shape, kind in outs],
        in_specs=ins,
        out_specs=[VMEM] * len(outs),
        scratch_shapes=scratch,
        compiler_params=pltpu.CompilerParams(vmem_limit_bytes=vmem),
        cost_estimate=pl.CostEstimate(flops=flops, bytes_accessed=moved, transcendentals=0),
    )


STATE = ((SUBS, SCEN, NODES), jnp.float32)
INVERSE = [pltpu.VMEM((SUBS, NODES, NODES), jnp.bfloat16), pltpu.SemaphoreType.DMA((SUBS,))]
OPEN_FLOPS = 2 * SUBS * SCEN * NODES * NODES


def local(volt, curr, local_inverse, schur_inverse, ind_gain, tie, port_map, breaker, fault_time, fault_node):
    first = call(
        first_kernel,
        [SMEM] * 2 + [VMEM] * 6 + [ANY],
        [STATE, ((ROWS, VALUE_ROWS + 16, LANES), jnp.bfloat16)],
        INVERSE,
        OPEN_FLOPS,
        4 << 20,
        ALL_VMEM,
    )
    interface = call(
        interface_kernel,
        [VMEM] * 2 + [ANY] * 4,
        [((SCEN, BLOCK), jnp.float32), ((ROWS, SCEN, BLOCK), jnp.bfloat16)],
        [pltpu.VMEM((4, 4, 2, BLOCK, LANES), jnp.bfloat16), pltpu.VMEM((ROWS, SCEN, BLOCK), jnp.bfloat16), pltpu.SemaphoreType.DMA((4,))],
        2 * 256 * 256 * 8192,
        3 << 20,
    )
    middle = call(
        middle_kernel,
        [SMEM] * 2 + [VMEM] * 8 + [ANY],
        [STATE, STATE, STATE, ((ROWS, VALUE_ROWS, LANES), jnp.bfloat16)],
        INVERSE,
        OPEN_FLOPS,
        4 << 20,
    )
    last = call(
        last_kernel,
        [VMEM] * 8 + [ANY],
        [STATE, STATE],
        [pltpu.VMEM((SUBS, PORTS, NODES), jnp.bfloat16), pltpu.SemaphoreType.DMA((SUBS,))],
        OPEN_FLOPS // 8,
        2 << 20,
    )

    exchange = functools.partial(lax.all_to_all, axis_name="row", split_axis=0, concat_axis=0)
    with jax.named_scope("schur_z"):
        across = lax.ppermute(schur_inverse, "col", [(c, c ^ 4) for c in range(COLS)])
    opened, send = first(fault_time, fault_node, volt, curr, breaker, ind_gain, tie, port_map, local_inverse)
    across, send = lax.optimization_barrier((across, send))
    with jax.named_scope("schur_z"):
        blocks = jnp.broadcast_to(jnp.stack([schur_inverse, across])[None], (4, 2, BLOCK, LANES))
        blocks = lax.all_to_all(blocks, "col", 0, 0, axis_index_groups=QUADS)
    blocks, send = lax.optimization_barrier((blocks, send))
    with jax.named_scope("schur_y"):
        schur_rows = [blocks] + [lax.ppermute(blocks, "col", [(c, (c + 8 * n) % COLS) for c in range(COLS)]) for n in (1, 2, 3)]
    maps = exchange(send)
    _, send = interface(maps, maps, *schur_rows)
    volt, curr, opened, send = middle(fault_time, fault_node, exchange(send), opened, volt, curr, breaker, ind_gain, tie, port_map, local_inverse)
    iface_block, send = interface(exchange(send), maps, *schur_rows)
    volt, curr = last(exchange(send), opened, volt, curr, breaker, ind_gain, tie, port_map, local_inverse)
    return volt, curr, iface_block


def solution(mesh):
    placed = (
        P("row", "col", None),
        P("row", "col", None),
        P("row", None, None),
        P("row", "col"),
        P("row", None),
        P("row", None),
        P("row", None),
        P("row", "col", None),
        P("col"),
        P("col"),
    )
    return jax.shard_map(
        local,
        mesh=mesh,
        in_specs=placed,
        out_specs=(P("row", "col", None), P("row", "col", None), P("col", "row")),
        check_vma=False,
    )
```

```python
import functools

import jax
import jax.numpy as jnp
from jax import lax
from jax.experimental import pallas as pl
from jax.experimental.pallas import tpu as pltpu
from jax.sharding import PartitionSpec as P

ROWS = 16
COLS = 32
SUBS = 8
SCEN = 16
NODES = 400
PORTS = 64
OWN = SUBS * PORTS
BLOCK = 256
LANES = 128
TILES = OWN // LANES
VALUE_ROWS = TILES * SCEN
Y_GROUPS = [[8 * y + z for y in range(4)] for z in range(8)]
VMEM_BYTES = 40 << 20
ALL_VMEM = 60 << 20

NN = (((1,), (0,)), ((), ()))
NT = (((1,), (1,)), ((), ()))


def dot(a, b, dims=NN):
    return lax.dot_general(a, b, dims, preferred_element_type=jnp.float32)


def flat_row(ref):
    return jnp.concatenate([ref[k : k + 1, :] for k in range(SUBS)], axis=1)


def column(ref):
    place = lax.broadcasted_iota(jnp.int32, (SCEN, 1), 0)
    out = jnp.zeros((SCEN, 1), jnp.int32)
    for s in range(SCEN):
        out = jnp.where(place == s, ref[s], out)
    return out


def open_circuit(step, volts, currs, closed, gain_ref, inv_wait, inv_ref, time_ref, node_ref, tie_ref, open_ref, send_ref):
    fault_node = column(node_ref)
    active = step >= column(time_ref)
    fault_node = jnp.where(active, fault_node, -1)
    first = lax.axis_index("row") * SUBS
    lane = lax.broadcasted_iota(jnp.int32, (SCEN, NODES), 1)
    parts = []
    for k in range(SUBS):
        volt = volts(k)
        hist = closed(k) * (currs(k) + gain_ref[k : k + 1, :] * volt)
        hit = lane + (first + k) * NODES == fault_node
        inject = (-hist - jnp.where(hit, 2.0 * volt, 0.0)).astype(jnp.bfloat16)
        inv_wait(k)
        open_k = dot(inject, inv_ref[k])
        open_ref[k] = open_k
        parts.append(tie_ref[k : k + 1, :] * open_k[:, :PORTS])
    values = jnp.concatenate(parts, axis=1).astype(jnp.bfloat16)
    for r in range(ROWS):
        for t in range(TILES):
            send_ref[r, t * SCEN : (t + 1) * SCEN, :] = values[:, t * LANES : (t + 1) * LANES]


def inverse_copies(inv_hbm, inv_ref, sems):
    copies = [pltpu.make_async_copy(inv_hbm.at[k], inv_ref.at[k], sems.at[k]) for k in range(SUBS)]
    for copy in copies:
        copy.start()
    return copies


def first_kernel(time_ref, node_ref, volt_ref, curr_ref, breaker_ref, gain_ref, tie_ref, map_ref, inv_hbm, open_ref, send_ref, inv_ref, sems):
    copies = inverse_copies(inv_hbm, inv_ref, sems)
    mapped = flat_row(map_ref)
    rows = [(mapped // BLOCK).astype(jnp.float32), (mapped % BLOCK).astype(jnp.float32)]
    rows = [row[:, t * LANES : (t + 1) * LANES] for row in rows for t in range(TILES)]
    tail = jnp.concatenate(rows + [jnp.zeros((16 - len(rows), LANES), jnp.float32)], axis=0).astype(jnp.bfloat16)
    for r in range(ROWS):
        send_ref[r, VALUE_ROWS : VALUE_ROWS + 16, :] = tail
    open_circuit(
        0,
        lambda k: volt_ref[k],
        lambda k: curr_ref[k],
        lambda k: breaker_ref[k].astype(jnp.float32),
        gain_ref,
        lambda k: copies[k].wait(),
        inv_ref,
        time_ref,
        node_ref,
        tie_ref,
        open_ref,
        send_ref,
    )


def right_hand_side(recv_ref, map_ref, rhs_ref):
    low = lax.broadcasted_iota(jnp.int32, (BLOCK, OWN), 0)
    rhs = jnp.zeros((ROWS * SCEN, BLOCK), jnp.float32)
    for r in range(ROWS):
        tail = map_ref[r, VALUE_ROWS : VALUE_ROWS + 16, :].astype(jnp.float32)
        hi = jnp.concatenate([tail[t : t + 1] for t in range(TILES)], axis=1).astype(jnp.int32)
        lo = jnp.concatenate([tail[TILES + t : TILES + t + 1] for t in range(TILES)], axis=1).astype(jnp.int32)
        values = jnp.concatenate([recv_ref[r, t * SCEN : (t + 1) * SCEN, :] for t in range(TILES)], axis=1)
        values = values.astype(jnp.float32)
        left = jnp.concatenate([jnp.where(hi == h, values, 0.0) for h in range(ROWS)], axis=0).astype(jnp.bfloat16)
        right = jnp.where(low == lo, 1.0, 0.0).astype(jnp.bfloat16)
        rhs += dot(left, right, NT)
    rhs = rhs.astype(jnp.bfloat16)
    for h in range(ROWS):
        for side in range(2):
            rhs_ref[2 * h + side] = rhs[h * SCEN : (h + 1) * SCEN, side * LANES : (side + 1) * LANES]


def schur_copies(schur_hbm, schur_ref, sems):
    copies = [pltpu.make_async_copy(schur_hbm.at[y], schur_ref.at[y], sems.at[y]) for y in range(4)]
    for copy in copies:
        copy.start()
    return copies


def schur_product(rhs_ref, schur_ref, copies, iface_ref, send_ref):
    own_z = lax.axis_index("col") % 8
    total = jnp.zeros((SCEN, BLOCK), jnp.float32)
    for y in range(4):
        copies[y].wait()
        for x in (0, 2):
            for o in range(2):
                col = 8 * y + jnp.bitwise_xor(own_z, x + 4 * o)
                left = jnp.concatenate([rhs_ref[col], rhs_ref[jnp.bitwise_xor(col, 1)]], axis=1)
                right = jnp.concatenate([schur_ref[y, x, o], schur_ref[y, x + 1, o]], axis=1)
                total += dot(left, right, NT)
    iface_ref[...] = total
    half = total.astype(jnp.bfloat16)
    for r in range(ROWS):
        send_ref[r] = half


def rhs_kernel(recv_ref, rhs_ref):
    right_hand_side(recv_ref, recv_ref, rhs_ref)


def product_kernel(rhs_ref, schur_hbm, iface_ref, send_ref, schur_ref, sems):
    copies = schur_copies(schur_hbm, schur_ref, sems)
    schur_product(rhs_ref, schur_ref, copies, iface_ref, send_ref)


def interface_kernel(recv_ref, map_ref, schur_hbm, iface_ref, send_ref, schur_ref, rhs_ref, sems):
    copies = schur_copies(schur_hbm, schur_ref, sems)
    right_hand_side(recv_ref, map_ref, rhs_ref)
    schur_product(rhs_ref, schur_ref, copies, iface_ref, send_ref)


def driven(recv_ref, map_ref, tie_ref):
    mapped = flat_row(map_ref)
    hi = mapped // BLOCK
    low = lax.broadcasted_iota(jnp.int32, (BLOCK, OWN), 0)
    right = jnp.where(low == mapped % BLOCK, 1.0, 0.0).astype(jnp.bfloat16)
    found = dot(recv_ref[...].reshape(ROWS * SCEN, BLOCK), right)
    picked = jnp.zeros((SCEN, OWN), jnp.float32)
    for r in range(ROWS):
        picked += jnp.where(hi == r, found[r * SCEN : (r + 1) * SCEN, :], 0.0)
    return (flat_row(tie_ref) * picked).astype(jnp.bfloat16)


def update(k, drive, open_ref, inv, volt, curr_ref, breaker_ref, gain_ref):
    volt_next = open_ref[k] + dot(drive[:, k * PORTS : (k + 1) * PORTS], inv)
    closed = breaker_ref[k].astype(jnp.float32)
    curr = closed * (curr_ref[k] + gain_ref[k : k + 1, :] * (volt_next + volt))
    return volt_next, curr


def middle_kernel(time_ref, node_ref, recv_ref, open_prev_ref, volt_ref, curr_ref, breaker_ref, gain_ref, tie_ref, map_ref, inv_hbm, volt_out, curr_out, open_ref, send_ref, inv_ref, sems):
    copies = inverse_copies(inv_hbm, inv_ref, sems)
    drive = driven(recv_ref, map_ref, tie_ref)
    for k in range(SUBS):
        copies[k].wait()
        volt_out[k], curr_out[k] = update(k, drive, open_prev_ref, inv_ref[k, :PORTS, :], volt_ref[k], curr_ref, breaker_ref, gain_ref)
    open_circuit(
        1,
        lambda k: volt_out[k],
        lambda k: curr_out[k],
        lambda k: breaker_ref[k].astype(jnp.float32),
        gain_ref,
        lambda k: None,
        inv_ref,
        time_ref,
        node_ref,
        tie_ref,
        open_ref,
        send_ref,
    )


def last_kernel(recv_ref, open_prev_ref, volt_ref, curr_ref, breaker_ref, gain_ref, tie_ref, map_ref, inv_hbm, volt_out, curr_out, inv_ref, sems):
    copies = [pltpu.make_async_copy(inv_hbm.at[k, :PORTS], inv_ref.at[k], sems.at[k]) for k in range(SUBS)]
    for copy in copies:
        copy.start()
    drive = driven(recv_ref, map_ref, tie_ref)
    for k in range(SUBS):
        copies[k].wait()
        volt_out[k], curr_out[k] = update(k, drive, open_prev_ref, inv_ref[k], volt_ref[k], curr_ref, breaker_ref, gain_ref)


SMEM = pl.BlockSpec(memory_space=pltpu.SMEM)
VMEM = pl.BlockSpec(memory_space=pltpu.VMEM)
ANY = pl.BlockSpec(memory_space=pl.ANY)


def call(body, ins, outs, scratch, flops, moved, vmem=VMEM_BYTES):
    return pl.pallas_call(
        body,
        out_shape=[jax.ShapeDtypeStruct(shape, kind) for shape, kind in outs],
        in_specs=ins,
        out_specs=[VMEM] * len(outs),
        scratch_shapes=scratch,
        compiler_params=pltpu.CompilerParams(vmem_limit_bytes=vmem),
        cost_estimate=pl.CostEstimate(flops=flops, bytes_accessed=moved, transcendentals=0),
    )


STATE = ((SUBS, SCEN, NODES), jnp.float32)
INVERSE = [pltpu.VMEM((SUBS, NODES, NODES), jnp.bfloat16), pltpu.SemaphoreType.DMA((SUBS,))]
OPEN_FLOPS = 2 * SUBS * SCEN * NODES * NODES


def local(volt, curr, local_inverse, schur_inverse, ind_gain, tie, port_map, breaker, fault_time, fault_node):
    first = call(
        first_kernel,
        [SMEM] * 2 + [VMEM] * 6 + [ANY],
        [STATE, ((ROWS, VALUE_ROWS + 16, LANES), jnp.bfloat16)],
        INVERSE,
        OPEN_FLOPS,
        4 << 20,
        ALL_VMEM,
    )
    faces = [((SCEN, BLOCK), jnp.float32), ((ROWS, SCEN, BLOCK), jnp.bfloat16)]
    schur_scratch = pltpu.VMEM((4, 4, 2, BLOCK, LANES), jnp.bfloat16)
    rhs_shape = ((COLS, SCEN, LANES), jnp.bfloat16)
    summed = call(rhs_kernel, [VMEM], [rhs_shape], [], 2 * 256 * 256 * 8192, 1 << 20)
    product = call(
        product_kernel,
        [VMEM, ANY],
        faces,
        [schur_scratch, pltpu.SemaphoreType.DMA((4,))],
        2 * 16 * 256 * 4096,
        3 << 20,
    )
    interface = call(
        interface_kernel,
        [VMEM] * 2 + [ANY],
        faces,
        [schur_scratch, pltpu.VMEM(*rhs_shape), pltpu.SemaphoreType.DMA((4,))],
        2 * 256 * 256 * 8192,
        3 << 20,
    )
    middle = call(
        middle_kernel,
        [SMEM] * 2 + [VMEM] * 8 + [ANY],
        [STATE, STATE, STATE, ((ROWS, VALUE_ROWS, LANES), jnp.bfloat16)],
        INVERSE,
        OPEN_FLOPS,
        4 << 20,
    )
    last = call(
        last_kernel,
        [VMEM] * 8 + [ANY],
        [STATE, STATE],
        [pltpu.VMEM((SUBS, PORTS, NODES), jnp.bfloat16), pltpu.SemaphoreType.DMA((SUBS,))],
        OPEN_FLOPS // 8,
        2 << 20,
    )

    exchange = functools.partial(lax.all_to_all, axis_name="row", split_axis=0, concat_axis=0)
    with jax.named_scope("schur_z"):
        across = lax.ppermute(schur_inverse, "col", [(c, c ^ 4) for c in range(COLS)])
    opened, send = first(fault_time, fault_node, volt, curr, breaker, ind_gain, tie, port_map, local_inverse)
    across, send = lax.optimization_barrier((across, send))
    maps = exchange(send)
    with jax.named_scope("schur_z"):
        pair = jnp.stack([schur_inverse, across])
        quad = [pair] + [lax.ppermute(pair, "col", [(c, c ^ n) for c in range(COLS)]) for n in (1, 2, 3)]
    quad, maps = lax.optimization_barrier((quad, maps))
    with jax.named_scope("schur_y"):
        blocks = jnp.broadcast_to(jnp.stack(quad)[None], (4, 4, 2, BLOCK, LANES))
        schur_rows = lax.all_to_all(blocks, "col", 0, 0, axis_index_groups=Y_GROUPS)
    (rhs,) = summed(maps)
    _, send = product(rhs, schur_rows)
    volt, curr, opened, send = middle(fault_time, fault_node, exchange(send), opened, volt, curr, breaker, ind_gain, tie, port_map, local_inverse)
    iface_block, send = interface(exchange(send), maps, schur_rows)
    volt, curr = last(exchange(send), opened, volt, curr, breaker, ind_gain, tie, port_map, local_inverse)
    return volt, curr, iface_block


def solution(mesh):
    placed = (
        P("row", "col", None),
        P("row", "col", None),
        P("row", None, None),
        P("row", "col"),
        P("row", None),
        P("row", None),
        P("row", None),
        P("row", "col", None),
        P("col"),
        P("col"),
    )
    return jax.shard_map(
        local,
        mesh=mesh,
        in_specs=placed,
        out_specs=(P("row", "col", None), P("row", "col", None), P("col", "row")),
        check_vma=False,
    )
```

```python
import functools

import jax
import jax.numpy as jnp
from jax import lax
from jax.experimental import pallas as pl
from jax.experimental.pallas import tpu as pltpu
from jax.sharding import PartitionSpec as P

ROWS = 16
COLS = 32
SUBS = 8
SCEN = 16
NODES = 400
PORTS = 64
OWN = SUBS * PORTS
BLOCK = 256
LANES = 128
TILES = OWN // LANES
VALUE_ROWS = TILES * SCEN
QUADS = [[4 * q + z for z in range(4)] for q in range(8)]
VMEM_BYTES = 60 << 20

NN = (((1,), (0,)), ((), ()))
NT = (((1,), (1,)), ((), ()))


def dot(a, b, dims=NN):
    return lax.dot_general(a, b, dims, preferred_element_type=jnp.float32)


def flat_row(ref):
    return jnp.concatenate([ref[k : k + 1, :] for k in range(SUBS)], axis=1)


def column(ref):
    place = lax.broadcasted_iota(jnp.int32, (SCEN, 1), 0)
    out = jnp.zeros((SCEN, 1), jnp.int32)
    for s in range(SCEN):
        out = jnp.where(place == s, ref[s], out)
    return out


def open_circuit(step, volts, currs, breaker_ref, gain_ref, inv_copies, inv_ref, time_ref, node_ref, tie_ref, open_ref, send_ref):
    fault_node = jnp.where(step >= column(time_ref), column(node_ref), -1)
    first = lax.axis_index("row") * SUBS
    lane = lax.broadcasted_iota(jnp.int32, (SCEN, NODES), 1)
    parts = []
    for k in range(SUBS):
        volt = volts[k]
        hist = breaker_ref[k].astype(jnp.float32) * (currs[k] + gain_ref[k : k + 1, :] * volt)
        hit = lane + (first + k) * NODES == fault_node
        inject = (-hist - jnp.where(hit, 2.0 * volt, 0.0)).astype(jnp.bfloat16)
        if inv_copies:
            inv_copies[k].wait()
        open_k = dot(inject, inv_ref[k])
        open_ref[k] = open_k
        parts.append(tie_ref[k : k + 1, :] * open_k[:, :PORTS])
    values = jnp.concatenate(parts, axis=1).astype(jnp.bfloat16)
    for r in range(ROWS):
        for t in range(TILES):
            send_ref[r, t * SCEN : (t + 1) * SCEN, :] = values[:, t * LANES : (t + 1) * LANES]


def fetch(sources, targets, sems):
    copies = [pltpu.make_async_copy(a, b, sems.at[n]) for n, (a, b) in enumerate(zip(sources, targets))]
    for copy in copies:
        copy.start()
    return copies


def by_subnetwork(ref, rows=None):
    return [ref.at[k] if rows is None else ref.at[k, pl.ds(0, rows)] for k in range(SUBS)]


def first_kernel(time_ref, node_ref, volt_hbm, curr_hbm, breaker_hbm, gain_hbm, tie_hbm, map_hbm, inv_hbm, open_ref, send_ref, map_ref, gain_ref, tie_ref, volt_ref, curr_ref, breaker_ref, inv_ref, sems):
    copies = fetch(
        [map_hbm, gain_hbm, tie_hbm, volt_hbm, curr_hbm, breaker_hbm] + by_subnetwork(inv_hbm),
        [map_ref, gain_ref, tie_ref, volt_ref, curr_ref, breaker_ref] + by_subnetwork(inv_ref),
        sems,
    )
    copies[0].wait()
    mapped = flat_row(map_ref)
    rows = [(mapped // BLOCK).astype(jnp.float32), (mapped % BLOCK).astype(jnp.float32)]
    rows = [row[:, t * LANES : (t + 1) * LANES] for row in rows for t in range(TILES)]
    tail = jnp.concatenate(rows + [jnp.zeros((16 - len(rows), LANES), jnp.float32)], axis=0).astype(jnp.bfloat16)
    for r in range(ROWS):
        send_ref[r, VALUE_ROWS : VALUE_ROWS + 16, :] = tail
    for copy in copies[1:6]:
        copy.wait()
    open_circuit(0, volt_ref, curr_ref, breaker_ref, gain_ref, copies[6:], inv_ref, time_ref, node_ref, tie_ref, open_ref, send_ref)


def right_hand_side(recv_ref, map_ref, rhs_ref):
    low = lax.broadcasted_iota(jnp.int32, (BLOCK, OWN), 0)
    rhs = jnp.zeros((ROWS * SCEN, BLOCK), jnp.float32)
    for r in range(ROWS):
        tail = map_ref[r, VALUE_ROWS : VALUE_ROWS + 16, :].astype(jnp.float32)
        hi = jnp.concatenate([tail[t : t + 1] for t in range(TILES)], axis=1).astype(jnp.int32)
        lo = jnp.concatenate([tail[TILES + t : TILES + t + 1] for t in range(TILES)], axis=1).astype(jnp.int32)
        values = jnp.concatenate([recv_ref[r, t * SCEN : (t + 1) * SCEN, :] for t in range(TILES)], axis=1)
        values = values.astype(jnp.float32)
        left = jnp.concatenate([jnp.where(hi == h, values, 0.0) for h in range(ROWS)], axis=0).astype(jnp.bfloat16)
        right = jnp.where(low == lo, 1.0, 0.0).astype(jnp.bfloat16)
        rhs += dot(left, right, NT)
    rhs_ref[...] = rhs.astype(jnp.bfloat16).reshape(ROWS, SCEN, BLOCK)


def schur_copies(parts, schur_ref, sems):
    own, back, ahead, far_low, far_high = parts
    low, high = schur_ref.at[2, pl.ds(0, 2)], schur_ref.at[2, pl.ds(2, 2)]
    return fetch([own, back, ahead, far_low, far_high], [schur_ref.at[0], schur_ref.at[1], schur_ref.at[3], low, high], sems)


def schur_product(rhs_ref, schur_ref, copies, iface_ref, send_ref):
    col = lax.axis_index("col")
    own_y, own_half = col // 8, (col // 4) % 2
    total = jnp.zeros((SCEN, BLOCK), jnp.float32)
    for n, waits in ((0, copies[:1]), (1, copies[1:2]), (3, copies[2:3]), (2, copies[3:])):
        for copy in waits:
            copy.wait()
        for other in range(2):
            first = 4 * ((own_y + 4 - n) % 4) + 2 * ((own_half + other) % 2)
            for p in range(2):
                pair = schur_ref[n, 2 * p, other], schur_ref[n, 2 * p + 1, other]
                total += dot(rhs_ref[first + p], jnp.concatenate(pair, axis=1), NT)
    iface_ref[...] = total
    for r in range(ROWS):
        send_ref[r] = total


def rhs_kernel(recv_ref, rhs_ref):
    right_hand_side(recv_ref, recv_ref, rhs_ref)


def product_kernel(rhs_ref, *refs):
    parts, (iface_ref, send_ref, schur_ref, sems) = refs[:5], refs[5:]
    copies = schur_copies(parts, schur_ref, sems)
    schur_product(rhs_ref, schur_ref, copies, iface_ref, send_ref)


def interface_kernel(recv_ref, map_ref, *refs):
    parts, (iface_ref, send_ref, schur_ref, rhs_ref, sems) = refs[:5], refs[5:]
    copies = schur_copies(parts, schur_ref, sems)
    right_hand_side(recv_ref, map_ref, rhs_ref)
    schur_product(rhs_ref, schur_ref, copies, iface_ref, send_ref)


def port_kernel(map_ref, tie_ref, out_ref):
    mapped = flat_row(map_ref)
    rows = [(mapped // BLOCK).astype(jnp.float32), (mapped % BLOCK).astype(jnp.float32), flat_row(tie_ref)]
    out_ref[...] = jnp.concatenate(rows + [jnp.zeros((8 - len(rows), OWN), jnp.float32)], axis=0)


def driven(recv_ref, ports):
    hi, lo = ports[0:1].astype(jnp.int32), ports[1:2].astype(jnp.int32)
    low = lax.broadcasted_iota(jnp.int32, (BLOCK, OWN), 0)
    right = jnp.where(low == lo, 1.0, 0.0).astype(jnp.bfloat16)
    volts = recv_ref[...].reshape(ROWS * SCEN, BLOCK)
    coarse = volts.astype(jnp.bfloat16)
    found = dot(coarse, right) + dot((volts - coarse.astype(jnp.float32)).astype(jnp.bfloat16), right)
    picked = jnp.zeros((SCEN, OWN), jnp.float32)
    for r in range(ROWS):
        picked += jnp.where(hi == r, found[r * SCEN : (r + 1) * SCEN, :], 0.0)
    return (ports[2:3] * picked).astype(jnp.bfloat16)


def update(k, drive, open_ref, inv, volt, curr, breaker_ref, gain_ref):
    volt_next = open_ref[k] + dot(drive[:, k * PORTS : (k + 1) * PORTS], inv)
    closed = breaker_ref[k].astype(jnp.float32)
    return volt_next, closed * (curr + gain_ref[k : k + 1, :] * (volt_next + volt))


def middle_kernel(time_ref, node_ref, recv_ref, open_prev_ref, volt_hbm, curr_hbm, breaker_hbm, gain_hbm, tie_hbm, ports_hbm, inv_hbm, volt_out, curr_out, open_ref, send_ref, ports_ref, gain_ref, tie_ref, volt_ref, curr_ref, breaker_ref, inv_ref, sems):
    copies = fetch(
        [ports_hbm, tie_hbm, gain_hbm, volt_hbm, curr_hbm, breaker_hbm] + by_subnetwork(inv_hbm),
        [ports_ref, tie_ref, gain_ref, volt_ref, curr_ref, breaker_ref] + by_subnetwork(inv_ref),
        sems,
    )
    copies[0].wait()
    drive = driven(recv_ref, ports_ref[...])
    for copy in copies[1:6]:
        copy.wait()
    for k in range(SUBS):
        copies[6 + k].wait()
        volt_out[k], curr_out[k] = update(k, drive, open_prev_ref, inv_ref[k, :PORTS, :], volt_ref[k], curr_ref[k], breaker_ref, gain_ref)
    open_circuit(1, volt_out, curr_out, breaker_ref, gain_ref, None, inv_ref, time_ref, node_ref, tie_ref, open_ref, send_ref)


def last_kernel(recv_ref, open_prev_ref, volt_ref, curr_ref, breaker_hbm, gain_hbm, ports_hbm, inv_hbm, volt_out, curr_out, ports_ref, gain_ref, breaker_ref, inv_ref, sems):
    copies = fetch(
        [ports_hbm, gain_hbm, breaker_hbm] + by_subnetwork(inv_hbm, PORTS),
        [ports_ref, gain_ref, breaker_ref] + by_subnetwork(inv_ref),
        sems,
    )
    copies[0].wait()
    drive = driven(recv_ref, ports_ref[...])
    for copy in copies[1:3]:
        copy.wait()
    for k in range(SUBS):
        copies[3 + k].wait()
        volt_out[k], curr_out[k] = update(k, drive, open_prev_ref, inv_ref[k], volt_ref[k], curr_ref[k], breaker_ref, gain_ref)


SMEM = pl.BlockSpec(memory_space=pltpu.SMEM)
VMEM = pl.BlockSpec(memory_space=pltpu.VMEM)
HBM = pl.BlockSpec(memory_space=pltpu.HBM)


def call(body, ins, outs, scratch, flops, moved):
    return pl.pallas_call(
        body,
        out_shape=[jax.ShapeDtypeStruct(shape, kind) for shape, kind in outs],
        in_specs=ins,
        out_specs=[VMEM] * len(outs),
        scratch_shapes=scratch,
        compiler_params=pltpu.CompilerParams(vmem_limit_bytes=VMEM_BYTES),
        cost_estimate=pl.CostEstimate(flops=flops, bytes_accessed=moved, transcendentals=0),
    )


STATE = ((SUBS, SCEN, NODES), jnp.float32)
PREP_FLOPS = 100_000_000_000_000
OPEN_FLOPS = 2 * SUBS * SCEN * NODES * NODES
SMALL = [
    pltpu.VMEM((SUBS, PORTS), jnp.int32),
    pltpu.VMEM((SUBS, NODES), jnp.float32),
    pltpu.VMEM((SUBS, PORTS), jnp.float32),
]
PORT_ROWS = pltpu.VMEM((8, OWN), jnp.float32)
BREAKER = pltpu.VMEM((SUBS, SCEN, NODES), jnp.int32)
INVERSE = pltpu.VMEM((SUBS, NODES, NODES), jnp.bfloat16)


def local(volt, curr, local_inverse, schur_inverse, ind_gain, tie, port_map, breaker, fault_time, fault_node):
    first = call(
        first_kernel,
        [SMEM] * 2 + [HBM] * 7,
        [STATE, ((ROWS, VALUE_ROWS + 16, LANES), jnp.bfloat16)],
        SMALL + [pltpu.VMEM(*STATE)] * 2 + [BREAKER, INVERSE, pltpu.SemaphoreType.DMA((6 + SUBS,))],
        OPEN_FLOPS,
        4 << 20,
    )
    faces = [((SCEN, BLOCK), jnp.float32), ((ROWS, SCEN, BLOCK), jnp.float32)]
    schur_scratch = pltpu.VMEM((4, 4, 2, BLOCK, LANES), jnp.bfloat16)
    rhs_shape = ((ROWS, SCEN, BLOCK), jnp.bfloat16)
    summed = call(rhs_kernel, [VMEM], [rhs_shape], [], 2 * 256 * 256 * 8192, 1 << 20)
    product = call(
        product_kernel,
        [VMEM] + [HBM] * 5,
        faces,
        [schur_scratch, pltpu.SemaphoreType.DMA((5,))],
        2 * 16 * 256 * 4096,
        3 << 20,
    )
    interface = call(
        interface_kernel,
        [VMEM] * 2 + [HBM] * 5,
        faces,
        [schur_scratch, pltpu.VMEM(*rhs_shape), pltpu.SemaphoreType.DMA((5,))],
        2 * 256 * 256 * 8192,
        3 << 20,
    )
    middle = call(
        middle_kernel,
        [SMEM] * 2 + [VMEM] * 2 + [HBM] * 7,
        [STATE, STATE, STATE, ((ROWS, VALUE_ROWS, LANES), jnp.bfloat16)],
        [PORT_ROWS] + SMALL[1:] + [pltpu.VMEM(*STATE)] * 2 + [BREAKER, INVERSE, pltpu.SemaphoreType.DMA((6 + SUBS,))],
        OPEN_FLOPS,
        4 << 20,
    )
    last = call(
        last_kernel,
        [VMEM] * 4 + [HBM] * 4,
        [STATE, STATE],
        [PORT_ROWS, SMALL[1], BREAKER, pltpu.VMEM((SUBS, PORTS, NODES), jnp.bfloat16), pltpu.SemaphoreType.DMA((3 + SUBS,))],
        OPEN_FLOPS // 8,
        2 << 20,
    )

    described = call(port_kernel, [VMEM] * 2, [((8, OWN), jnp.float32)], [], PREP_FLOPS, 1 << 20)

    exchange = functools.partial(lax.all_to_all, axis_name="row", split_axis=0, concat_axis=0)
    def along_y(block, steps):
        return lax.ppermute(block, "col", [(c, (c + 8 * steps) % COLS) for c in range(COLS)])

    with jax.named_scope("schur_z"):
        across = lax.ppermute(schur_inverse, "col", [(c, c ^ 4) for c in range(COLS)])
    opened, send = first(fault_time, fault_node, volt, curr, breaker, ind_gain, tie, port_map, local_inverse)
    across, send = lax.optimization_barrier((across, send))
    with jax.named_scope("schur_z"):
        own = jnp.broadcast_to(jnp.stack([schur_inverse, across])[None], (4, 2, BLOCK, LANES))
        own = lax.all_to_all(own, "col", 0, 0, axis_index_groups=QUADS)
    own, send, own_ports = lax.optimization_barrier((own, send, port_map))
    with jax.named_scope("schur_y"):
        back, ahead = along_y(own, 1), along_y(own, -1)
        schur_rows = own, back, ahead, along_y(back[:2], 1), along_y(ahead[2:], -1)
    maps = exchange(send)
    (ports,) = described(own_ports, tie)
    (rhs,) = summed(maps)
    rhs, ports = lax.optimization_barrier((rhs, ports))
    _, send = product(rhs, *schur_rows)
    volt, curr, opened, send = middle(fault_time, fault_node, exchange(send), opened, volt, curr, breaker, ind_gain, tie, ports, local_inverse)
    iface_block, send = interface(exchange(send), maps, *schur_rows)
    volt, curr = last(exchange(send), opened, volt, curr, breaker, ind_gain, ports, local_inverse)
    return volt, curr, iface_block


def solution(mesh):
    placed = (
        P("row", "col", None),
        P("row", "col", None),
        P("row", None, None),
        P("row", "col"),
        P("row", None),
        P("row", None),
        P("row", None),
        P("row", "col", None),
        P("col"),
        P("col"),
    )
    return jax.shard_map(
        local,
        mesh=mesh,
        in_specs=placed,
        out_specs=(P("row", "col", None), P("row", "col", None), P("col", "row")),
        check_vma=False,
    )
```

```python
import functools

import jax
import jax.numpy as jnp
from jax import lax
from jax.experimental import pallas as pl
from jax.experimental.pallas import tpu as pltpu
from jax.sharding import PartitionSpec as P

ROWS = 16
COLS = 32
SUBS = 8
SCEN = 16
NODES = 400
PORTS = 64
OWN = SUBS * PORTS
BLOCK = 256
LANES = 128
TILES = OWN // LANES
VALUE_ROWS = TILES * SCEN
MAP_ROWS = 2 * TILES
VMEM_BYTES = 60 << 20
BF16, F32 = jnp.bfloat16, jnp.float32

NN = (((1,), (0,)), ((), ()))
NT = (((1,), (1,)), ((), ()))


def dot(a, b, dims=NN):
    return lax.dot_general(a, b, dims, preferred_element_type=F32)


def halves(x):
    coarse = x.astype(BF16)
    return coarse, (x - coarse.astype(F32)).astype(BF16)


def fetch(sources, targets, sems):
    copies = [pltpu.make_async_copy(a, b, sems.at[n]) for n, (a, b) in enumerate(zip(sources, targets))]
    for copy in copies:
        copy.start()
    return copies


def wait_for(copies):
    for copy in copies:
        copy.wait()


def each(ref, count):
    return [ref.at[k] for k in range(count)]


def flat_row(ref):
    return jnp.concatenate([ref[k : k + 1, :] for k in range(SUBS)], axis=1)


def tiles_of(row):
    return [row[:, t * LANES : (t + 1) * LANES] for t in range(TILES)]


def column(ref):
    place = lax.broadcasted_iota(jnp.int32, (SCEN, 1), 0)
    out = jnp.zeros((SCEN, 1), jnp.int32)
    for s in range(SCEN):
        out = jnp.where(place == s, ref[s], out)
    return out


def open_circuit(step, volts, currs, breaker_ref, gain_ref, inv_copies, inv_ref, time_ref, node_ref, tie_ref, open_ref, send_ref):
    fault_node = jnp.where(step >= column(time_ref), column(node_ref), -1)
    first = lax.axis_index("row") * SUBS
    lane = lax.broadcasted_iota(jnp.int32, (SCEN, NODES), 1)
    parts = []
    for k in range(SUBS):
        volt = volts[k]
        hist = breaker_ref[k].astype(F32) * (currs[k] + gain_ref[k : k + 1, :] * volt)
        hit = lane + (first + k) * NODES == fault_node
        inject = (-hist - jnp.where(hit, 2.0 * volt, 0.0)).astype(BF16)
        if inv_copies:
            inv_copies[k].wait()
        open_k = dot(inject, inv_ref[k])
        open_ref[k] = open_k
        parts.append(tie_ref[k : k + 1, :] * open_k[:, :PORTS])
    values = jnp.concatenate(parts, axis=1).astype(send_ref.dtype)
    for t, tile in enumerate(tiles_of(values)):
        for r in range(ROWS):
            send_ref[r, t * SCEN : (t + 1) * SCEN, :] = tile


def first_kernel(time_ref, node_ref, volt_hbm, curr_hbm, breaker_hbm, gain_hbm, tie_hbm, map_hbm, inv_hbm, open_ref, send_ref, map_ref, gain_ref, tie_ref, volt_ref, curr_ref, breaker_ref, inv_ref, sems):
    copies = fetch(
        [map_hbm, gain_hbm, tie_hbm, volt_hbm, curr_hbm, breaker_hbm] + each(inv_hbm, SUBS),
        [map_ref, gain_ref, tie_ref, volt_ref, curr_ref, breaker_ref] + each(inv_ref, SUBS),
        sems,
    )
    copies[0].wait()
    mapped = flat_row(map_ref)
    rows = tiles_of((mapped // BLOCK).astype(F32)) + tiles_of((mapped % BLOCK).astype(F32))
    tail = jnp.concatenate(rows, axis=0)
    for r in range(ROWS):
        send_ref[r, VALUE_ROWS:, :] = tail
    wait_for(copies[1:6])
    open_circuit(0, volt_ref, curr_ref, breaker_ref, gain_ref, copies[6:], inv_ref, time_ref, node_ref, tie_ref, open_ref, send_ref)


def right_hand_side(recv_ref, map_ref, ready):
    low = lax.broadcasted_iota(jnp.int32, (BLOCK, OWN), 0)
    rhs = jnp.zeros((ROWS * SCEN, BLOCK), F32)
    for r in range(ROWS):
        wait_for(ready(r))
        tail = map_ref[r].astype(jnp.int32)
        hi = jnp.concatenate([tail[t : t + 1] for t in range(TILES)], axis=1)
        lo = jnp.concatenate([tail[TILES + t : TILES + t + 1] for t in range(TILES)], axis=1)
        right = jnp.where(low == lo, 1.0, 0.0).astype(BF16)
        values = jnp.concatenate([recv_ref[r, t * SCEN : (t + 1) * SCEN, :] for t in range(TILES)], axis=1)
        for part in halves(values) if values.dtype == F32 else (values,):
            part = part.astype(F32)
            left = jnp.concatenate([jnp.where(hi == h, part, 0.0) for h in range(ROWS)], axis=0).astype(BF16)
            rhs += dot(left, right, NT)
    return rhs.astype(BF16).reshape(ROWS, SCEN, BLOCK)


def join_kernel(own_hbm, across_hbm, *refs):
    quads, (out_hbm, sems) = refs[:3], refs[3:]
    wait_for(fetch([own_hbm, across_hbm, *quads], [out_hbm.at[0, 0], out_hbm.at[0, 1]] + [out_hbm.at[x] for x in (1, 2, 3)], sems))


def schur_copies(parts, schur_ref, sems):
    own, back, ahead, far_low, far_high = parts
    low, high = schur_ref.at[2, pl.ds(0, 2)], schur_ref.at[2, pl.ds(2, 2)]
    return fetch([own, back, ahead, far_low, far_high], [schur_ref.at[0], schur_ref.at[1], schur_ref.at[3], low, high], sems)


def schur_product(rhs_ref, schur_ref, copies):
    col = lax.axis_index("col")
    own_y, own_z = col // 8, col % 8
    total = jnp.zeros((SCEN, BLOCK), F32)
    for n, waits in ((0, copies[:1]), (1, copies[1:2]), (3, copies[2:3]), (2, copies[3:])):
        wait_for(waits)
        for x in (0, 2):
            for o in range(2):
                place = 8 * ((own_y + 4 - n) % 4) + jnp.bitwise_xor(own_z, x + 4 * o)
                left = jnp.concatenate([rhs_ref[place], rhs_ref[jnp.bitwise_xor(place, 1)]], axis=1)
                right = jnp.concatenate([schur_ref[n, x, o], schur_ref[n, x + 1, o]], axis=1)
                total += dot(left, right, NT)
    return total


def keep(rhs, rhs_ref):
    for h in range(ROWS):
        for side in range(2):
            rhs_ref[2 * h + side] = rhs[h, :, side * LANES : (side + 1) * LANES]


def rhs_kernel(recv_hbm, rhs_ref, map_out, recv_ref, map_ref, sems):
    copies = fetch(
        [recv_hbm.at[r, pl.ds(0, VALUE_ROWS)] for r in range(ROWS)] + [recv_hbm.at[r, pl.ds(VALUE_ROWS, MAP_ROWS)] for r in range(ROWS)],
        each(recv_ref, ROWS) + each(map_ref, ROWS),
        sems,
    )
    keep(right_hand_side(recv_ref, map_ref, lambda r: (copies[r], copies[ROWS + r])), rhs_ref)
    map_out[...] = map_ref[...]


def product_kernel(rhs_hbm, *refs):
    parts, (send_ref, schur_ref, rhs_ref, sems, rhs_sem) = refs[:5], refs[5:]
    copies = schur_copies(parts, schur_ref, sems)
    wait_for(fetch([rhs_hbm], [rhs_ref], rhs_sem))
    total = schur_product(rhs_ref, schur_ref, copies)
    for r in range(ROWS):
        send_ref[r] = total


def interface_kernel(recv_hbm, map_hbm, *refs):
    parts, (iface_ref, send_ref, schur_ref, rhs_ref, recv_ref, map_ref, sems, recv_sems) = refs[:5], refs[5:]
    arrived = fetch([map_hbm] + each(recv_hbm, ROWS), [map_ref] + each(recv_ref, ROWS), recv_sems)
    copies = schur_copies(parts, schur_ref, sems)
    arrived[0].wait()
    keep(right_hand_side(recv_ref, map_ref, lambda r: (arrived[1 + r],)), rhs_ref)
    total = schur_product(rhs_ref, schur_ref, copies)
    iface_ref[...] = total
    half = total.astype(BF16)
    for r in range(ROWS):
        send_ref[r] = half


def driven(recv_ref, map_ref, tie_ref):
    mapped = flat_row(map_ref)
    hi = mapped // BLOCK
    low = lax.broadcasted_iota(jnp.int32, (BLOCK, OWN), 0)
    right = jnp.where(low == mapped % BLOCK, 1.0, 0.0).astype(BF16)
    volts = recv_ref[...].reshape(ROWS * SCEN, BLOCK)
    found = sum(dot(part, right) for part in (halves(volts) if volts.dtype == F32 else (volts,)))
    picked = jnp.zeros((SCEN, OWN), F32)
    for r in range(ROWS):
        picked += jnp.where(hi == r, found[r * SCEN : (r + 1) * SCEN, :], 0.0)
    return (flat_row(tie_ref) * picked).astype(BF16)


def update(k, drive, open_ref, inv, volt, curr, breaker_ref, gain_ref):
    volt_next = open_ref[k] + dot(drive[:, k * PORTS : (k + 1) * PORTS], inv)
    closed = breaker_ref[k].astype(F32)
    return volt_next, closed * (curr + gain_ref[k : k + 1, :] * (volt_next + volt))


def middle_kernel(time_ref, node_ref, recv_hbm, prev_hbm, volt_hbm, curr_hbm, breaker_hbm, gain_hbm, tie_hbm, map_hbm, inv_hbm, volt_out, curr_out, open_ref, send_ref, recv_ref, prev_ref, map_ref, gain_ref, tie_ref, volt_ref, curr_ref, breaker_ref, inv_ref, sems):
    copies = fetch(
        [map_hbm, tie_hbm, recv_hbm, gain_hbm, prev_hbm, volt_hbm, curr_hbm, breaker_hbm] + each(inv_hbm, SUBS),
        [map_ref, tie_ref, recv_ref, gain_ref, prev_ref, volt_ref, curr_ref, breaker_ref] + each(inv_ref, SUBS),
        sems,
    )
    wait_for(copies[:3])
    drive = driven(recv_ref, map_ref, tie_ref)
    wait_for(copies[3:8])
    for k in range(SUBS):
        copies[8 + k].wait()
        volt_out[k], curr_out[k] = update(k, drive, prev_ref, inv_ref[k, :PORTS, :], volt_ref[k], curr_ref[k], breaker_ref, gain_ref)
    open_circuit(1, volt_out, curr_out, breaker_ref, gain_ref, None, inv_ref, time_ref, node_ref, tie_ref, open_ref, send_ref)


def last_kernel(recv_hbm, prev_hbm, volt_hbm, curr_hbm, breaker_hbm, gain_hbm, tie_hbm, map_hbm, inv_hbm, volt_out, curr_out, recv_ref, prev_ref, map_ref, gain_ref, tie_ref, volt_ref, curr_ref, breaker_ref, inv_ref, sems):
    copies = fetch(
        [map_hbm, tie_hbm, recv_hbm, gain_hbm, prev_hbm, volt_hbm, curr_hbm, breaker_hbm] + [inv_hbm.at[k, pl.ds(0, PORTS)] for k in range(SUBS)],
        [map_ref, tie_ref, recv_ref, gain_ref, prev_ref, volt_ref, curr_ref, breaker_ref] + each(inv_ref, SUBS),
        sems,
    )
    wait_for(copies[:3])
    drive = driven(recv_ref, map_ref, tie_ref)
    wait_for(copies[3:])
    for k in range(SUBS):
        volt_out[k], curr_out[k] = update(k, drive, prev_ref, inv_ref[k], volt_ref[k], curr_ref[k], breaker_ref, gain_ref)


SMEM = pl.BlockSpec(memory_space=pltpu.SMEM)
VMEM = pl.BlockSpec(memory_space=pltpu.VMEM)
HBM = pl.BlockSpec(memory_space=pltpu.HBM)

STATE = ((SUBS, SCEN, NODES), F32)
SCHUR = ((4, 4, 2, BLOCK, LANES), BF16)
RHS = ((COLS, SCEN, LANES), BF16)
MAPS = ((ROWS, MAP_ROWS, LANES), F32)
FACE = (ROWS, SCEN, BLOCK)
GIGA = 1_000_000_000


def held(*shapes):
    return [pltpu.VMEM(*shape) for shape in shapes]


def copies_of(count):
    return [pltpu.SemaphoreType.DMA((count,))]


SMALL = held(((SUBS, PORTS), jnp.int32), ((SUBS, NODES), F32), ((SUBS, PORTS), F32))
BREAKER = held(((SUBS, SCEN, NODES), jnp.int32))


def call(body, ins, outs, scratch, flops, moved, out_specs=None):
    return pl.pallas_call(
        body,
        out_shape=[jax.ShapeDtypeStruct(shape, kind) for shape, kind in outs],
        in_specs=ins,
        out_specs=out_specs or [VMEM] * len(outs),
        scratch_shapes=scratch,
        compiler_params=pltpu.CompilerParams(vmem_limit_bytes=VMEM_BYTES),
        cost_estimate=pl.CostEstimate(flops=flops, bytes_accessed=moved, transcendentals=0),
    )


first = call(
    first_kernel,
    [SMEM] * 2 + [HBM] * 7,
    [STATE, ((ROWS, VALUE_ROWS + MAP_ROWS, LANES), F32)],
    SMALL + held(STATE, STATE) + BREAKER + held(((SUBS, NODES, NODES), BF16)) + copies_of(6 + SUBS),
    GIGA,
    4 << 20,
)
join = call(join_kernel, [HBM] * 5, [((4, 2, BLOCK, LANES), BF16)], copies_of(5), 100_000 * GIGA, 1 << 20, [HBM])
summed = call(
    rhs_kernel,
    [HBM],
    [RHS, MAPS],
    held(((ROWS, VALUE_ROWS, LANES), F32), MAPS) + copies_of(2 * ROWS),
    GIGA,
    1 << 20,
)
product = call(product_kernel, [HBM] * 6, [(FACE, F32)], held(SCHUR, RHS) + copies_of(5) + copies_of(1), GIGA, 3 << 20)
interface = call(
    interface_kernel,
    [HBM] * 7,
    [(FACE[1:], F32), (FACE, BF16)],
    held(SCHUR, RHS, ((ROWS, VALUE_ROWS, LANES), BF16), MAPS) + copies_of(5) + copies_of(1 + ROWS),
    GIGA,
    3 << 20,
)
middle = call(
    middle_kernel,
    [SMEM] * 2 + [HBM] * 9,
    [STATE, STATE, STATE, ((ROWS, VALUE_ROWS, LANES), BF16)],
    held((FACE, F32), STATE) + SMALL + held(STATE, STATE) + BREAKER + held(((SUBS, NODES, NODES), BF16)) + copies_of(8 + SUBS),
    GIGA,
    4 << 20,
)
last = call(
    last_kernel,
    [HBM] * 9,
    [STATE, STATE],
    held((FACE, BF16), STATE) + SMALL + held(STATE, STATE) + BREAKER + held(((SUBS, PORTS, NODES), BF16)) + copies_of(8 + SUBS),
    GIGA,
    2 << 20,
)


def along_z(block, flip):
    return lax.ppermute(block, "col", [(c, c ^ flip) for c in range(COLS)])


def along_y(block, steps):
    return lax.ppermute(block, "col", [(c, (c + 8 * steps) % COLS) for c in range(COLS)])


def local(volt, curr, local_inverse, schur_inverse, ind_gain, tie, port_map, breaker, fault_time, fault_node):
    exchange = functools.partial(lax.all_to_all, axis_name="row", split_axis=0, concat_axis=0)
    fixed = breaker, ind_gain, tie, port_map, local_inverse
    with jax.named_scope("schur_z"):
        across = along_z(schur_inverse, 4)
    opened, send = first(fault_time, fault_node, volt, curr, *fixed)
    across, send = lax.optimization_barrier((across, send))
    with jax.named_scope("schur_z"):
        pair = jnp.stack([schur_inverse, across])
        (own,) = join(schur_inverse, across, *(along_z(pair, x) for x in (1, 2, 3)))
    with jax.named_scope("schur_y"):
        back, ahead = along_y(own, 1), along_y(own, -1)
        schur_rows = own, back, ahead, along_y(back[:2], 1), along_y(ahead[2:], -1)
    rhs, maps = summed(exchange(send))
    (send,) = product(rhs, *schur_rows)
    volt, curr, opened, send = middle(fault_time, fault_node, exchange(send), opened, volt, curr, *fixed)
    iface_block, send = interface(exchange(send), maps, *schur_rows)
    volt, curr = last(exchange(send), opened, volt, curr, *fixed)
    return volt, curr, iface_block


def solution(mesh):
    placed = (
        P("row", "col", None),
        P("row", "col", None),
        P("row", None, None),
        P("row", "col"),
        P("row", None),
        P("row", None),
        P("row", None),
        P("row", "col", None),
        P("col"),
        P("col"),
    )
    return jax.shard_map(
        local,
        mesh=mesh,
        in_specs=placed,
        out_specs=(P("row", "col", None), P("row", "col", None), P("col", "row")),
        check_vma=False,
    )
```

```python
import functools

import jax
import jax.numpy as jnp
from jax import lax
from jax.experimental import pallas as pl
from jax.experimental.pallas import tpu as pltpu
from jax.sharding import PartitionSpec as P

ROWS = 16
COLS = 32
SUBS = 8
SCEN = 16
NODES = 400
PORTS = 64
OWN = SUBS * PORTS
BLOCK = 256
LANES = 128
TILES = OWN // LANES
VALUE_ROWS = TILES * SCEN
MAP_ROWS = 2 * TILES
CORES = [[2 * n + core for n in range(ROWS // 2)] for core in range(2)]
VMEM_BYTES = 16 << 20
ALL_VMEM = 60 << 20
BF16, F32 = jnp.bfloat16, jnp.float32

NN = (((1,), (0,)), ((), ()))
NT = (((1,), (1,)), ((), ()))


def dot(a, b, dims=NN):
    return lax.dot_general(a, b, dims, preferred_element_type=F32)


def halves(x):
    coarse = x.astype(BF16)
    return coarse, (x - coarse.astype(F32)).astype(BF16)


def fetch(sources, targets, sems):
    copies = [pltpu.make_async_copy(a, b, sems.at[n]) for n, (a, b) in enumerate(zip(sources, targets))]
    for copy in copies:
        copy.start()
    return copies


def wait_for(copies):
    for copy in copies:
        copy.wait()


def each(ref, count):
    return [ref.at[k] for k in range(count)]


def flat_row(ref):
    return jnp.concatenate([ref[k : k + 1, :] for k in range(SUBS)], axis=1)


def tiles_of(row):
    return [row[:, t * LANES : (t + 1) * LANES] for t in range(TILES)]


def column(ref):
    place = lax.broadcasted_iota(jnp.int32, (SCEN, 1), 0)
    out = jnp.zeros((SCEN, 1), jnp.int32)
    for s in range(SCEN):
        out = jnp.where(place == s, ref[s], out)
    return out


def open_circuit(step, volts, currs, breaker_ref, gain_ref, inv_copies, inv_ref, time_ref, node_ref, tie_ref, open_ref, send_ref):
    fault_node = jnp.where(step >= column(time_ref), column(node_ref), -1)
    first = lax.axis_index("row") * SUBS
    lane = lax.broadcasted_iota(jnp.int32, (SCEN, NODES), 1)
    parts = []
    for k in range(SUBS):
        volt = volts[k]
        hist = breaker_ref[k].astype(F32) * (currs[k] + gain_ref[k : k + 1, :] * volt)
        hit = lane + (first + k) * NODES == fault_node
        inject = (-hist - jnp.where(hit, 2.0 * volt, 0.0)).astype(BF16)
        if inv_copies:
            inv_copies[k].wait()
        open_k = dot(inject, inv_ref[k])
        open_ref[k] = open_k
        parts.append(tie_ref[k : k + 1, :] * open_k[:, :PORTS])
    values = jnp.concatenate(parts, axis=1).astype(send_ref.dtype)
    for t, tile in enumerate(tiles_of(values)):
        for r in range(send_ref.shape[0]):
            send_ref[r, t * SCEN : (t + 1) * SCEN, :] = tile


def first_kernel(time_ref, node_ref, volt_hbm, curr_hbm, breaker_hbm, gain_hbm, tie_hbm, map_hbm, inv_hbm, open_ref, send_ref, map_ref, gain_ref, tie_ref, volt_ref, curr_ref, breaker_ref, inv_ref, sems):
    copies = fetch(
        [map_hbm, gain_hbm, tie_hbm, volt_hbm, curr_hbm, breaker_hbm] + each(inv_hbm, SUBS),
        [map_ref, gain_ref, tie_ref, volt_ref, curr_ref, breaker_ref] + each(inv_ref, SUBS),
        sems,
    )
    copies[0].wait()
    mapped = flat_row(map_ref)
    rows = tiles_of((mapped // BLOCK).astype(F32)) + tiles_of((mapped % BLOCK).astype(F32))
    tail = jnp.concatenate(rows, axis=0)
    for r in range(send_ref.shape[0]):
        send_ref[r, VALUE_ROWS:, :] = tail
    wait_for(copies[1:6])
    open_circuit(0, volt_ref, curr_ref, breaker_ref, gain_ref, copies[6:], inv_ref, time_ref, node_ref, tie_ref, open_ref, send_ref)


def right_hand_side(recv_ref, map_ref):
    low = lax.broadcasted_iota(jnp.int32, (BLOCK, OWN), 0).astype(F32).astype(BF16)
    one, zero = jnp.ones((), BF16), jnp.zeros((), BF16)
    rhs = jnp.zeros((ROWS * SCEN, BLOCK), F32)
    for r in range(ROWS):
        tail = map_ref[r]
        hi = jnp.concatenate([tail[t : t + 1] for t in range(TILES)], axis=1)
        lo = jnp.concatenate([tail[TILES + t : TILES + t + 1] for t in range(TILES)], axis=1)
        hi = jnp.broadcast_to(hi, (SCEN, OWN)).astype(BF16)
        right = jnp.where(low == lo.astype(BF16), one, zero)
        values = jnp.concatenate([recv_ref[r, t * SCEN : (t + 1) * SCEN, :] for t in range(TILES)], axis=1)
        for part in halves(values) if values.dtype == F32 else (values,):
            left = jnp.concatenate([jnp.where(hi == h, part, zero) for h in range(ROWS)], axis=0)
            rhs += dot(left, right, NT)
    return rhs.astype(BF16).reshape(ROWS, SCEN, BLOCK)


def join_kernel(own_ref, across_ref, *refs):
    quads, (out_ref,) = refs[:3], refs[3:]
    out_ref[0, 0] = own_ref[...]
    out_ref[0, 1] = across_ref[...]
    for x in (1, 2, 3):
        out_ref[x] = quads[x - 1][...]


def schur_copies(parts, schur_ref, sems):
    own, back, ahead, far_low, far_high = parts
    low, high = schur_ref.at[2, pl.ds(0, 2)], schur_ref.at[2, pl.ds(2, 2)]
    return fetch([own, back, ahead, far_low, far_high], [schur_ref.at[0], schur_ref.at[1], schur_ref.at[3], low, high], sems)


def schur_product(rhs_ref, schur_ref, copies):
    col = lax.axis_index("col")
    own_y, own_z = col // 8, col % 8
    wait_for(copies)
    left, right = [], []
    for n in range(4):
        for x in range(4):
            for o in range(2):
                left.append(rhs_ref[8 * ((own_y + 4 - n) % 4) + jnp.bitwise_xor(own_z, x + 4 * o)])
                right.append(schur_ref[n, x, o])
    return dot(jnp.concatenate(left, axis=1), jnp.concatenate(right, axis=1), NT)


def keep(rhs, rhs_ref):
    for h in range(ROWS):
        for side in range(2):
            rhs_ref[2 * h + side] = rhs[h, :, side * LANES : (side + 1) * LANES]


def two_parts(same, other, ref):
    half = ROWS // 2
    return [same, other], [ref.at[pl.ds(0, half)], ref.at[pl.ds(half, half)]]


def rhs_kernel(same_hbm, other_hbm, rhs_ref, map_out, recv_ref, sems):
    wait_for(fetch(*two_parts(same_hbm, other_hbm, recv_ref), sems))
    map_out[...] = recv_ref[:, VALUE_ROWS:, :]
    keep(right_hand_side(recv_ref, map_out), rhs_ref)


def product_kernel(rhs_hbm, *refs):
    parts, (send_ref, schur_ref, rhs_ref, sems, rhs_sem) = refs[:5], refs[5:]
    copies = schur_copies(parts, schur_ref, sems)
    wait_for(fetch([rhs_hbm], [rhs_ref], rhs_sem))
    total = schur_product(rhs_ref, schur_ref, copies)
    for r in range(send_ref.shape[0]):
        send_ref[r] = total


def interface_kernel(same_hbm, other_hbm, map_hbm, *refs):
    parts, (iface_ref, send_ref, schur_ref, rhs_ref, recv_ref, map_ref, sems, recv_sems) = refs[:5], refs[5:]
    sources, targets = two_parts(same_hbm, other_hbm, recv_ref)
    arrived = fetch([map_hbm] + sources, [map_ref] + targets, recv_sems)
    copies = schur_copies(parts, schur_ref, sems)
    wait_for(arrived)
    keep(right_hand_side(recv_ref, map_ref), rhs_ref)
    total = schur_product(rhs_ref, schur_ref, copies)
    iface_ref[...] = total
    half = total.astype(BF16)
    for r in range(ROWS):
        send_ref[r] = half


def driven(recv_ref, map_ref, tie_ref, sender):
    mapped = flat_row(map_ref)
    hi = mapped // BLOCK
    low = lax.broadcasted_iota(jnp.int32, (BLOCK, OWN), 0)
    right = jnp.where(low == mapped % BLOCK, 1.0, 0.0).astype(BF16)
    volts = recv_ref[...].reshape(ROWS * SCEN, BLOCK)
    found = sum(dot(part, right) for part in (halves(volts) if volts.dtype == F32 else (volts,)))
    picked = jnp.zeros((SCEN, OWN), F32)
    for r in range(ROWS):
        picked += jnp.where(hi == sender(r), found[r * SCEN : (r + 1) * SCEN, :], 0.0)
    return (flat_row(tie_ref) * picked).astype(BF16)


def update(k, drive, open_ref, inv, volt, curr, breaker_ref, gain_ref):
    volt_next = open_ref[k] + dot(drive[:, k * PORTS : (k + 1) * PORTS], inv)
    closed = breaker_ref[k].astype(F32)
    return volt_next, closed * (curr + gain_ref[k : k + 1, :] * (volt_next + volt))


def paired_sender(place):
    core = lax.axis_index("row") % 2
    half = ROWS // 2
    return 2 * place + core if place < half else 2 * (place - half) + 1 - core


def middle_kernel(time_ref, node_ref, same_hbm, other_hbm, prev_hbm, volt_hbm, curr_hbm, breaker_hbm, gain_hbm, tie_hbm, map_hbm, inv_hbm, volt_out, curr_out, open_ref, send_ref, recv_ref, prev_ref, map_ref, gain_ref, tie_ref, volt_ref, curr_ref, breaker_ref, inv_ref, sems):
    sources, targets = two_parts(same_hbm, other_hbm, recv_ref)
    copies = fetch(
        [map_hbm, tie_hbm] + sources + [gain_hbm, prev_hbm, volt_hbm, curr_hbm, breaker_hbm] + each(inv_hbm, SUBS),
        [map_ref, tie_ref] + targets + [gain_ref, prev_ref, volt_ref, curr_ref, breaker_ref] + each(inv_ref, SUBS),
        sems,
    )
    wait_for(copies[:4])
    drive = driven(recv_ref, map_ref, tie_ref, paired_sender)
    wait_for(copies[4:9])
    for k in range(SUBS):
        copies[9 + k].wait()
        volt_out[k], curr_out[k] = update(k, drive, prev_ref, inv_ref[k, :PORTS, :], volt_ref[k], curr_ref[k], breaker_ref, gain_ref)
    open_circuit(1, volt_out, curr_out, breaker_ref, gain_ref, None, inv_ref, time_ref, node_ref, tie_ref, open_ref, send_ref)


def last_kernel(recv_hbm, prev_hbm, volt_hbm, curr_hbm, breaker_hbm, gain_hbm, tie_hbm, map_hbm, inv_hbm, volt_out, curr_out, recv_ref, prev_ref, map_ref, gain_ref, tie_ref, volt_ref, curr_ref, breaker_ref, inv_ref, sems):
    copies = fetch(
        [map_hbm, tie_hbm, recv_hbm, gain_hbm, prev_hbm, volt_hbm, curr_hbm, breaker_hbm] + [inv_hbm.at[k, pl.ds(0, PORTS)] for k in range(SUBS)],
        [map_ref, tie_ref, recv_ref, gain_ref, prev_ref, volt_ref, curr_ref, breaker_ref] + each(inv_ref, SUBS),
        sems,
    )
    wait_for(copies[:3])
    drive = driven(recv_ref, map_ref, tie_ref, lambda place: place)
    wait_for(copies[3:])
    for k in range(SUBS):
        volt_out[k], curr_out[k] = update(k, drive, prev_ref, inv_ref[k], volt_ref[k], curr_ref[k], breaker_ref, gain_ref)


SMEM = pl.BlockSpec(memory_space=pltpu.SMEM)
VMEM = pl.BlockSpec(memory_space=pltpu.VMEM)
HBM = pl.BlockSpec(memory_space=pltpu.HBM)

STATE = ((SUBS, SCEN, NODES), F32)
SCHUR = ((4, 4, 2, BLOCK, LANES), BF16)
RHS = ((COLS, SCEN, LANES), BF16)
MAPS = ((ROWS, MAP_ROWS, LANES), F32)
FACE = (ROWS, SCEN, BLOCK)
GIGA = 1_000_000_000


def held(*shapes):
    return [pltpu.VMEM(*shape) for shape in shapes]


def copies_of(count):
    return [pltpu.SemaphoreType.DMA((count,))]


SMALL = held(((SUBS, PORTS), jnp.int32), ((SUBS, NODES), F32), ((SUBS, PORTS), F32))
BREAKER = held(((SUBS, SCEN, NODES), jnp.int32))


def call(body, ins, outs, scratch, flops, moved, vmem=VMEM_BYTES):
    return pl.pallas_call(
        body,
        out_shape=[jax.ShapeDtypeStruct(shape, kind) for shape, kind in outs],
        in_specs=ins,
        out_specs=[VMEM] * len(outs),
        scratch_shapes=scratch,
        compiler_params=pltpu.CompilerParams(vmem_limit_bytes=vmem),
        cost_estimate=pl.CostEstimate(flops=flops, bytes_accessed=moved, transcendentals=0),
    )


first = call(
    first_kernel,
    [SMEM] * 2 + [HBM] * 7,
    [STATE, ((ROWS // 2, VALUE_ROWS + MAP_ROWS, LANES), F32)],
    SMALL + held(STATE, STATE) + BREAKER + held(((SUBS, NODES, NODES), BF16)) + copies_of(6 + SUBS),
    GIGA,
    4 << 20,
    ALL_VMEM,
)
join = call(join_kernel, [VMEM] * 5, [((4, 2, BLOCK, LANES), BF16)], [], 100_000 * GIGA, 1 << 20, 8 << 20)
summed = call(rhs_kernel, [HBM] * 2, [RHS, MAPS], held(((ROWS, VALUE_ROWS + MAP_ROWS, LANES), F32)) + copies_of(2), GIGA, 1 << 20)
product = call(product_kernel, [HBM] * 6, [((ROWS // 2, SCEN, BLOCK), F32)], held(SCHUR, RHS) + copies_of(5) + copies_of(1), GIGA, 3 << 20)
interface = call(
    interface_kernel,
    [HBM] * 8,
    [(FACE[1:], F32), (FACE, BF16)],
    held(SCHUR, RHS, ((ROWS, VALUE_ROWS, LANES), BF16), MAPS) + copies_of(5) + copies_of(3),
    GIGA,
    3 << 20,
)
middle = call(
    middle_kernel,
    [SMEM] * 2 + [HBM] * 10,
    [STATE, STATE, STATE, ((ROWS // 2, VALUE_ROWS, LANES), BF16)],
    held((FACE, F32), STATE) + SMALL + held(STATE, STATE) + BREAKER + held(((SUBS, NODES, NODES), BF16)) + copies_of(9 + SUBS),
    GIGA,
    4 << 20,
)
last = call(
    last_kernel,
    [HBM] * 9,
    [STATE, STATE],
    held((FACE, BF16), STATE) + SMALL + held(STATE, STATE) + BREAKER + held(((SUBS, PORTS, NODES), BF16)) + copies_of(8 + SUBS),
    GIGA,
    2 << 20,
)


def along_z(block, flip):
    return lax.ppermute(block, "col", [(c, c ^ flip) for c in range(COLS)])


def along_y(block, steps):
    return lax.ppermute(block, "col", [(c, (c + 8 * steps) % COLS) for c in range(COLS)])


def local(volt, curr, local_inverse, schur_inverse, ind_gain, tie, port_map, breaker, fault_time, fault_node):
    exchange = functools.partial(lax.all_to_all, axis_name="row", split_axis=0, concat_axis=0)

    def paired_exchange(send):
        same = exchange(send, axis_index_groups=CORES)
        return same, lax.ppermute(same, "row", [(r, r ^ 1) for r in range(ROWS)])

    fixed = breaker, ind_gain, tie, port_map, local_inverse
    with jax.named_scope("schur_z"):
        across = along_z(schur_inverse, 4)
    opened, send = first(fault_time, fault_node, volt, curr, *fixed)
    across, send = lax.optimization_barrier((across, send))
    with jax.named_scope("schur_z"):
        pair = jnp.stack([schur_inverse, across])
        (own,) = join(schur_inverse, across, *(along_z(pair, x) for x in (1, 2, 3)))
    with jax.named_scope("schur_y"):
        back, ahead = along_y(own, 1), along_y(own, -1)
        schur_rows = own, back, ahead, along_y(back[:2], 1), along_y(ahead[2:], -1)
    rhs, maps = summed(*paired_exchange(send))
    (send,) = product(rhs, *schur_rows)
    volt, curr, opened, send = middle(fault_time, fault_node, *paired_exchange(send), opened, volt, curr, *fixed)
    iface_block, send = interface(*paired_exchange(send), maps, *schur_rows)
    volt, curr = last(exchange(send), opened, volt, curr, *fixed)
    return volt, curr, iface_block


def solution(mesh):
    placed = (
        P("row", "col", None),
        P("row", "col", None),
        P("row", None, None),
        P("row", "col"),
        P("row", None),
        P("row", None),
        P("row", None),
        P("row", "col", None),
        P("col"),
        P("col"),
    )
    return jax.shard_map(
        local,
        mesh=mesh,
        in_specs=placed,
        out_specs=(P("row", "col", None), P("row", "col", None), P("col", "row")),
        check_vma=False,
    )
```

```python
import jax
import jax.numpy as jnp
from jax import lax
from jax.experimental import pallas as pl
from jax.experimental.pallas import tpu as pltpu
from jax.sharding import PartitionSpec as P

ROWS = 16
COLS = 32
SUBS = 8
SCEN = 16
NODES = 400
PORTS = 64
OWN = SUBS * PORTS
BLOCK = 256
LANES = 128
TILES = OWN // LANES
VALUE_ROWS = TILES * SCEN
MAP_ROWS = 2 * TILES
CORES = [[2 * n + core for n in range(ROWS // 2)] for core in range(2)]
PAIRS = [[2 * n, 2 * n + 1] for n in range(ROWS // 2)]
VMEM_BYTES = 16 << 20
ALL_VMEM = 60 << 20
BF16, F32 = jnp.bfloat16, jnp.float32

NN = (((1,), (0,)), ((), ()))
NT = (((1,), (1,)), ((), ()))


def dot(a, b, dims=NN):
    return lax.dot_general(a, b, dims, preferred_element_type=F32)


def halves(x):
    coarse = x.astype(BF16)
    return coarse, (x - coarse.astype(F32)).astype(BF16)


def fetch(sources, targets, sems):
    copies = [pltpu.make_async_copy(a, b, sems.at[n]) for n, (a, b) in enumerate(zip(sources, targets))]
    for copy in copies:
        copy.start()
    return copies


def wait_for(copies):
    for copy in copies:
        copy.wait()


def each(ref, count):
    return [ref.at[k] for k in range(count)]


def flat_row(ref):
    return jnp.concatenate([ref[k : k + 1, :] for k in range(SUBS)], axis=1)


def tiles_of(row):
    return [row[:, t * LANES : (t + 1) * LANES] for t in range(TILES)]


def column(ref):
    place = lax.broadcasted_iota(jnp.int32, (SCEN, 1), 0)
    out = jnp.zeros((SCEN, 1), jnp.int32)
    for s in range(SCEN):
        out = jnp.where(place == s, ref[s], out)
    return out


def open_circuit(step, volts, currs, breaker_ref, gain_ref, inv_copies, inv_ref, time_ref, node_ref, tie_ref, open_ref, send_ref):
    fault_node = jnp.where(step >= column(time_ref), column(node_ref), -1)
    first = lax.axis_index("row") * SUBS
    lane = lax.broadcasted_iota(jnp.int32, (SCEN, NODES), 1)
    parts = []
    for k in range(SUBS):
        volt = volts[k]
        hist = breaker_ref[k].astype(F32) * (currs[k] + gain_ref[k : k + 1, :] * volt)
        hit = lane + (first + k) * NODES == fault_node
        inject = (-hist - jnp.where(hit, 2.0 * volt, 0.0)).astype(BF16)
        if inv_copies:
            inv_copies[k].wait()
        open_k = dot(inject, inv_ref[k])
        open_ref[k] = open_k
        parts.append(tie_ref[k : k + 1, :] * open_k[:, :PORTS])
    values = jnp.concatenate(parts, axis=1).astype(send_ref.dtype)
    for t, tile in enumerate(tiles_of(values)):
        for r in range(send_ref.shape[0]):
            send_ref[r, t * SCEN : (t + 1) * SCEN, :] = tile


def first_kernel(time_ref, node_ref, volt_hbm, curr_hbm, breaker_hbm, gain_hbm, tie_hbm, map_hbm, inv_hbm, open_ref, send_ref, right_ref, rows_ref, map_ref, gain_ref, tie_ref, volt_ref, curr_ref, breaker_ref, inv_ref, sems):
    copies = fetch(
        [map_hbm, gain_hbm, tie_hbm, volt_hbm, curr_hbm, breaker_hbm] + each(inv_hbm, SUBS),
        [map_ref, gain_ref, tie_ref, volt_ref, curr_ref, breaker_ref] + each(inv_ref, SUBS),
        sems,
    )
    copies[0].wait()
    mapped = flat_row(map_ref)
    rows = tiles_of((mapped // BLOCK).astype(F32)) + tiles_of((mapped % BLOCK).astype(F32))
    tail = jnp.concatenate(rows, axis=0)
    for r in range(send_ref.shape[0]):
        send_ref[r, VALUE_ROWS:, :] = tail
    wait_for(copies[1:6])
    low = lax.broadcasted_iota(jnp.int32, (BLOCK, OWN), 0)
    right_ref[...] = jnp.where(low == mapped % BLOCK, 1.0, 0.0).astype(BF16)
    rows_ref[...] = jnp.concatenate([(mapped // BLOCK).astype(F32), flat_row(tie_ref), jnp.zeros((6, OWN), F32)], axis=0)
    open_circuit(0, volt_ref, curr_ref, breaker_ref, gain_ref, copies[6:], inv_ref, time_ref, node_ref, tie_ref, open_ref, send_ref)


def right_hand_side(recv_ref, map_ref):
    low = lax.broadcasted_iota(jnp.int32, (BLOCK, OWN), 0).astype(F32).astype(BF16)
    one, zero = jnp.ones((), BF16), jnp.zeros((), BF16)
    rhs = jnp.zeros((ROWS * SCEN, BLOCK), F32)
    for r in range(ROWS):
        tail = map_ref[r]
        hi = jnp.concatenate([tail[t : t + 1] for t in range(TILES)], axis=1)
        lo = jnp.concatenate([tail[TILES + t : TILES + t + 1] for t in range(TILES)], axis=1)
        hi = jnp.broadcast_to(hi, (SCEN, OWN)).astype(BF16)
        right = jnp.where(low == lo.astype(BF16), one, zero)
        values = jnp.concatenate([recv_ref[r, t * SCEN : (t + 1) * SCEN, :] for t in range(TILES)], axis=1)
        for part in halves(values) if values.dtype == F32 else (values,):
            left = jnp.concatenate([jnp.where(hi == h, part, zero) for h in range(ROWS)], axis=0)
            rhs += dot(left, right, NT)
    return rhs.astype(BF16).reshape(ROWS, SCEN, BLOCK)


def join_kernel(own_ref, across_ref, *refs):
    quads, (out_ref,) = refs[:3], refs[3:]
    out_ref[0, 0] = own_ref[...]
    out_ref[0, 1] = across_ref[...]
    for x in (1, 2, 3):
        out_ref[x] = quads[x - 1][...]


def schur_copies(parts, schur_ref, sems):
    own, back, ahead, far_low, far_high = parts
    low, high = schur_ref.at[2, pl.ds(0, 2)], schur_ref.at[2, pl.ds(2, 2)]
    return fetch([own, back, ahead, far_low, far_high], [schur_ref.at[0], schur_ref.at[1], schur_ref.at[3], low, high], sems)


def schur_product(rhs_ref, schur_ref, copies):
    col = lax.axis_index("col")
    own_y, own_z = col // 8, col % 8
    wait_for(copies)
    left, right = [], []
    for n in range(4):
        for x in range(4):
            for o in range(2):
                left.append(rhs_ref[8 * ((own_y + 4 - n) % 4) + jnp.bitwise_xor(own_z, x + 4 * o)])
                right.append(schur_ref[n, x, o])
    return dot(jnp.concatenate(left, axis=1), jnp.concatenate(right, axis=1), NT)


def keep(rhs, rhs_ref):
    for h in range(ROWS):
        for side in range(2):
            rhs_ref[2 * h + side] = rhs[h, :, side * LANES : (side + 1) * LANES]


def rhs_kernel(recv_hbm, rhs_ref, map_out, recv_ref, sems):
    wait_for(fetch([recv_hbm], [recv_ref], sems))
    map_out[...] = recv_ref[:, VALUE_ROWS:, :]
    keep(right_hand_side(recv_ref, map_out), rhs_ref)


def product_kernel(rhs_hbm, *refs):
    parts, (send_ref, schur_ref, rhs_ref, sems, rhs_sem) = refs[:5], refs[5:]
    copies = schur_copies(parts, schur_ref, sems)
    wait_for(fetch([rhs_hbm], [rhs_ref], rhs_sem))
    total = schur_product(rhs_ref, schur_ref, copies)
    for r in range(send_ref.shape[0]):
        send_ref[r] = total


def interface_kernel(recv_hbm, map_hbm, *refs):
    parts, (iface_ref, send_ref, schur_ref, rhs_ref, recv_ref, map_ref, sems, recv_sems) = refs[:5], refs[5:]
    arrived = fetch([map_hbm, recv_hbm], [map_ref, recv_ref], recv_sems)
    copies = schur_copies(parts, schur_ref, sems)
    wait_for(arrived)
    keep(right_hand_side(recv_ref, map_ref), rhs_ref)
    total = schur_product(rhs_ref, schur_ref, copies)
    iface_ref[...] = total
    half = total.astype(BF16)
    for r in range(ROWS):
        send_ref[r] = half


def driven(recv_ref, right_ref, rows_ref, sender):
    hi = rows_ref[0:1, :].astype(jnp.int32)
    volts = recv_ref[...].reshape(ROWS * SCEN, BLOCK)
    found = sum(dot(part, right_ref[...]) for part in (halves(volts) if volts.dtype == F32 else (volts,)))
    picked = jnp.zeros((SCEN, OWN), F32)
    for n in range(ROWS):
        picked += jnp.where(hi == sender(n), found[n * SCEN : (n + 1) * SCEN, :], 0.0)
    return (rows_ref[1:2, :] * picked).astype(BF16)


def update(k, drive, open_ref, inv, volt, curr, breaker_ref, gain_ref):
    volt_next = open_ref[k] + dot(drive[:, k * PORTS : (k + 1) * PORTS], inv)
    closed = breaker_ref[k].astype(F32)
    return volt_next, closed * (curr + gain_ref[k : k + 1, :] * (volt_next + volt))


def paired_sender(place):
    return 2 * (place % (ROWS // 2)) + place // (ROWS // 2)


def middle_kernel(time_ref, node_ref, recv_hbm, prev_hbm, volt_hbm, curr_hbm, breaker_hbm, gain_hbm, tie_hbm, right_hbm, rows_hbm, inv_hbm, volt_out, curr_out, open_ref, send_ref, recv_ref, prev_ref, right_ref, rows_ref, gain_ref, tie_ref, volt_ref, curr_ref, breaker_ref, inv_ref, sems):
    copies = fetch(
        [right_hbm, rows_hbm, recv_hbm, prev_hbm, volt_hbm, curr_hbm, breaker_hbm, gain_hbm, tie_hbm] + each(inv_hbm, SUBS),
        [right_ref, rows_ref, recv_ref, prev_ref, volt_ref, curr_ref, breaker_ref, gain_ref, tie_ref] + each(inv_ref, SUBS),
        sems,
    )
    wait_for(copies[:3])
    drive = driven(recv_ref, right_ref, rows_ref, paired_sender)
    wait_for(copies[3:9])
    for k in range(SUBS):
        copies[9 + k].wait()
        volt_out[k], curr_out[k] = update(k, drive, prev_ref, inv_ref[k, :PORTS, :], volt_ref[k], curr_ref[k], breaker_ref, gain_ref)
    open_circuit(1, volt_out, curr_out, breaker_ref, gain_ref, None, inv_ref, time_ref, node_ref, tie_ref, open_ref, send_ref)


def last_kernel(recv_hbm, prev_hbm, volt_hbm, curr_hbm, breaker_hbm, gain_hbm, right_hbm, rows_hbm, inv_hbm, volt_out, curr_out, recv_ref, prev_ref, right_ref, rows_ref, gain_ref, volt_ref, curr_ref, breaker_ref, inv_ref, sems):
    copies = fetch(
        [right_hbm, rows_hbm, recv_hbm, prev_hbm, volt_hbm, curr_hbm, breaker_hbm, gain_hbm] + [inv_hbm.at[k, pl.ds(0, PORTS)] for k in range(SUBS)],
        [right_ref, rows_ref, recv_ref, prev_ref, volt_ref, curr_ref, breaker_ref, gain_ref] + each(inv_ref, SUBS),
        sems,
    )
    wait_for(copies[:3])
    drive = driven(recv_ref, right_ref, rows_ref, lambda place: place)
    wait_for(copies[3:])
    for k in range(SUBS):
        volt_out[k], curr_out[k] = update(k, drive, prev_ref, inv_ref[k], volt_ref[k], curr_ref[k], breaker_ref, gain_ref)


SMEM = pl.BlockSpec(memory_space=pltpu.SMEM)
VMEM = pl.BlockSpec(memory_space=pltpu.VMEM)
HBM = pl.BlockSpec(memory_space=pltpu.HBM)

STATE = ((SUBS, SCEN, NODES), F32)
SCHUR = ((4, 4, 2, BLOCK, LANES), BF16)
RHS = ((COLS, SCEN, LANES), BF16)
MAPS = ((ROWS, MAP_ROWS, LANES), F32)
FACE = (ROWS, SCEN, BLOCK)
GIGA = 1_000_000_000


def held(*shapes):
    return [pltpu.VMEM(*shape) for shape in shapes]


def copies_of(count):
    return [pltpu.SemaphoreType.DMA((count,))]


GAIN, TIE = held(((SUBS, NODES), F32), ((SUBS, PORTS), F32))
BREAKER = held(((SUBS, SCEN, NODES), jnp.int32))
INVERSE = held(((SUBS, NODES, NODES), BF16))
PICK = [((BLOCK, OWN), BF16), ((8, OWN), F32)]


def call(body, ins, outs, scratch, flops, moved, vmem=VMEM_BYTES):
    return pl.pallas_call(
        body,
        out_shape=[jax.ShapeDtypeStruct(shape, kind) for shape, kind in outs],
        in_specs=ins,
        out_specs=[VMEM] * len(outs),
        scratch_shapes=scratch,
        compiler_params=pltpu.CompilerParams(vmem_limit_bytes=vmem),
        cost_estimate=pl.CostEstimate(flops=flops, bytes_accessed=moved, transcendentals=0),
    )


first = call(
    first_kernel,
    [SMEM] * 2 + [HBM] * 7,
    [STATE, ((ROWS // 2, VALUE_ROWS + MAP_ROWS, LANES), F32)] + PICK,
    held(((SUBS, PORTS), jnp.int32)) + [GAIN, TIE] + held(STATE, STATE) + BREAKER + INVERSE + copies_of(6 + SUBS),
    GIGA,
    4 << 20,
    ALL_VMEM,
)
join = call(join_kernel, [VMEM] * 5, [((4, 2, BLOCK, LANES), BF16)], [], 100_000 * GIGA, 1 << 20, 8 << 20)
summed = call(rhs_kernel, [HBM], [RHS, MAPS], held(((ROWS, VALUE_ROWS + MAP_ROWS, LANES), F32)) + copies_of(1), GIGA, 1 << 20)
product = call(product_kernel, [HBM] * 6, [((ROWS // 2, SCEN, BLOCK), F32)], held(SCHUR, RHS) + copies_of(5) + copies_of(1), GIGA, 3 << 20)
interface = call(
    interface_kernel,
    [HBM] * 7,
    [(FACE[1:], F32), (FACE, BF16)],
    held(SCHUR, RHS, ((ROWS, VALUE_ROWS, LANES), BF16), MAPS) + copies_of(5) + copies_of(2),
    GIGA,
    3 << 20,
)
middle = call(
    middle_kernel,
    [SMEM] * 2 + [HBM] * 10,
    [STATE, STATE, STATE, ((ROWS // 2, VALUE_ROWS, LANES), BF16)],
    held((FACE, F32), STATE, *PICK) + [GAIN, TIE] + held(STATE, STATE) + BREAKER + INVERSE + copies_of(9 + SUBS),
    GIGA,
    4 << 20,
)
last = call(
    last_kernel,
    [HBM] * 9,
    [STATE, STATE],
    held((FACE, BF16), STATE, *PICK) + [GAIN] + held(STATE, STATE) + BREAKER + held(((SUBS, PORTS, NODES), BF16)) + copies_of(8 + SUBS),
    GIGA,
    2 << 20,
)


def along_z(block, flip):
    return lax.ppermute(block, "col", [(c, c ^ flip) for c in range(COLS)])


def along_y(block, steps):
    return lax.ppermute(block, "col", [(c, (c + 8 * steps) % COLS) for c in range(COLS)])


def exchange(send, groups=None):
    return lax.all_to_all(send, "row", 0, 0, axis_index_groups=groups)


def paired_exchange(send):
    both = lax.all_gather(exchange(send, CORES), "row", axis_index_groups=PAIRS)
    return both.reshape(ROWS, *send.shape[1:])


def local(volt, curr, local_inverse, schur_inverse, ind_gain, tie, port_map, breaker, fault_time, fault_node):
    with jax.named_scope("schur_z"):
        across = along_z(schur_inverse, 4)
    opened, send, *pick = first(fault_time, fault_node, volt, curr, breaker, ind_gain, tie, port_map, local_inverse)
    across, send = lax.optimization_barrier((across, send))
    with jax.named_scope("schur_z"):
        pair = jnp.stack([schur_inverse, across])
        (own,) = join(schur_inverse, across, *(along_z(pair, x) for x in (1, 2, 3)))
    with jax.named_scope("schur_y"):
        back, ahead = along_y(own, 1), along_y(own, -1)
        schur_rows = own, back, ahead, along_y(back[:2], 1), along_y(ahead[2:], -1)
    rhs, maps = summed(paired_exchange(send))
    (send,) = product(rhs, *schur_rows)
    volt, curr, opened, send = middle(fault_time, fault_node, paired_exchange(send), opened, volt, curr, breaker, ind_gain, tie, *pick, local_inverse)
    iface_block, send = interface(paired_exchange(send), maps, *schur_rows)
    volt, curr = last(exchange(send), opened, volt, curr, breaker, ind_gain, *pick, local_inverse)
    return volt, curr, iface_block


def solution(mesh):
    placed = (
        P("row", "col", None),
        P("row", "col", None),
        P("row", None, None),
        P("row", "col"),
        P("row", None),
        P("row", None),
        P("row", None),
        P("row", "col", None),
        P("col"),
        P("col"),
    )
    return jax.shard_map(
        local,
        mesh=mesh,
        in_specs=placed,
        out_specs=(P("row", "col", None), P("row", "col", None), P("col", "row")),
        check_vma=False,
    )
```

```python
import jax
import jax.numpy as jnp
from jax import lax
from jax.experimental import pallas as pl
from jax.experimental.pallas import tpu as pltpu
from jax.sharding import PartitionSpec as P

ROWS = 16
COLS = 32
SUBS = 8
SCEN = 16
NODES = 400
PORTS = 64
OWN = SUBS * PORTS
BLOCK = 256
LANES = 128
TILES = OWN // LANES
VALUE_ROWS = TILES * SCEN
MAP_ROWS = 2 * TILES
TURNED = [(n + ROWS // 2) % ROWS for n in range(ROWS)]
CORES = [[r for r in TURNED if r % 2 == core] for core in range(2)]
PAIRS = [[2 * n, 2 * n + 1] for n in range(ROWS // 2)]
VMEM_BYTES = 16 << 20
ALL_VMEM = 60 << 20
BF16, F32 = jnp.bfloat16, jnp.float32

NN = (((1,), (0,)), ((), ()))
NT = (((1,), (1,)), ((), ()))


def dot(a, b, dims=NN):
    return lax.dot_general(a, b, dims, preferred_element_type=F32)


def halves(x):
    coarse = x.astype(BF16)
    return coarse, (x - coarse.astype(F32)).astype(BF16)


def fetch(sources, targets, sems):
    copies = [pltpu.make_async_copy(a, b, sems.at[n]) for n, (a, b) in enumerate(zip(sources, targets))]
    for copy in copies:
        copy.start()
    return copies


def wait_for(copies):
    for copy in copies:
        copy.wait()


def each(ref, count):
    return [ref.at[k] for k in range(count)]


def flat_row(ref):
    return jnp.concatenate([ref[k : k + 1, :] for k in range(SUBS)], axis=1)


def tiles_of(row):
    return [row[:, t * LANES : (t + 1) * LANES] for t in range(TILES)]


def column(ref):
    place = lax.broadcasted_iota(jnp.int32, (SCEN, 1), 0)
    out = jnp.zeros((SCEN, 1), jnp.int32)
    for s in range(SCEN):
        out = jnp.where(place == s, ref[s], out)
    return out


def open_circuit(step, volts, currs, breaker_ref, gain_ref, inv_copies, inv_ref, time_ref, node_ref, tie_ref, open_ref, send_ref):
    fault_node = jnp.where(step >= column(time_ref), column(node_ref), -1)
    first = lax.axis_index("row") * SUBS
    lane = lax.broadcasted_iota(jnp.int32, (SCEN, NODES), 1)
    parts = []
    for k in range(SUBS):
        volt = volts[k]
        hist = breaker_ref[k].astype(F32) * (currs[k] + gain_ref[k : k + 1, :] * volt)
        hit = lane + (first + k) * NODES == fault_node
        inject = (-hist - jnp.where(hit, 2.0 * volt, 0.0)).astype(BF16)
        if inv_copies:
            inv_copies[k].wait()
        open_k = dot(inject, inv_ref[k])
        open_ref[k] = open_k
        parts.append(tie_ref[k : k + 1, :] * open_k[:, :PORTS])
    values = jnp.concatenate(parts, axis=1).astype(send_ref.dtype)
    for t, tile in enumerate(tiles_of(values)):
        for r in range(send_ref.shape[0]):
            send_ref[r, t * SCEN : (t + 1) * SCEN, :] = tile


def first_kernel(time_ref, node_ref, volt_hbm, curr_hbm, breaker_hbm, gain_hbm, tie_hbm, map_hbm, inv_hbm, open_ref, send_ref, right_ref, rows_ref, map_ref, gain_ref, tie_ref, volt_ref, curr_ref, breaker_ref, inv_ref, sems):
    copies = fetch(
        [map_hbm, gain_hbm, tie_hbm, volt_hbm, curr_hbm, breaker_hbm] + each(inv_hbm, SUBS),
        [map_ref, gain_ref, tie_ref, volt_ref, curr_ref, breaker_ref] + each(inv_ref, SUBS),
        sems,
    )
    copies[0].wait()
    mapped = flat_row(map_ref)
    rows = tiles_of((mapped // BLOCK).astype(F32)) + tiles_of((mapped % BLOCK).astype(F32))
    tail = jnp.concatenate(rows, axis=0)
    for r in range(send_ref.shape[0]):
        send_ref[r, VALUE_ROWS:, :] = tail
    wait_for(copies[1:6])
    low = lax.broadcasted_iota(jnp.int32, (BLOCK, OWN), 0)
    right_ref[...] = jnp.where(low == mapped % BLOCK, 1.0, 0.0).astype(BF16)
    rows_ref[...] = jnp.concatenate([(mapped // BLOCK).astype(F32), flat_row(tie_ref), jnp.zeros((6, OWN), F32)], axis=0)
    open_circuit(0, volt_ref, curr_ref, breaker_ref, gain_ref, copies[6:], inv_ref, time_ref, node_ref, tie_ref, open_ref, send_ref)


def right_hand_side(recv_ref, map_ref):
    low = lax.broadcasted_iota(jnp.int32, (BLOCK, OWN), 0).astype(F32).astype(BF16)
    one, zero = jnp.ones((), BF16), jnp.zeros((), BF16)
    rhs = jnp.zeros((ROWS * SCEN, BLOCK), F32)
    for r in range(ROWS):
        tail = map_ref[r]
        hi = jnp.concatenate([tail[t : t + 1] for t in range(TILES)], axis=1)
        lo = jnp.concatenate([tail[TILES + t : TILES + t + 1] for t in range(TILES)], axis=1)
        hi = jnp.broadcast_to(hi, (SCEN, OWN)).astype(BF16)
        right = jnp.where(low == lo.astype(BF16), one, zero)
        values = jnp.concatenate([recv_ref[r, t * SCEN : (t + 1) * SCEN, :] for t in range(TILES)], axis=1)
        for part in halves(values) if values.dtype == F32 else (values,):
            left = jnp.concatenate([jnp.where(hi == h, part, zero) for h in range(ROWS)], axis=0)
            rhs += dot(left, right, NT)
    return rhs.astype(BF16).reshape(ROWS, SCEN, BLOCK)


def join_kernel(own_ref, across_ref, *refs):
    quads, (out_ref,) = refs[:3], refs[3:]
    out_ref[0, 0] = own_ref[...]
    out_ref[0, 1] = across_ref[...]
    for x in (1, 2, 3):
        out_ref[x] = quads[x - 1][...]


def schur_copies(parts, schur_ref, sems):
    own, back, ahead, far_low, far_high = parts
    low, high = schur_ref.at[2, pl.ds(0, 2)], schur_ref.at[2, pl.ds(2, 2)]
    return fetch([own, back, ahead, far_low, far_high], [schur_ref.at[0], schur_ref.at[1], schur_ref.at[3], low, high], sems)


def schur_product(rhs_ref, schur_ref, copies):
    col = lax.axis_index("col")
    own_y, own_z = col // 8, col % 8
    wait_for(copies)
    left, right = [], []
    for n in range(4):
        for x in range(4):
            for o in range(2):
                left.append(rhs_ref[8 * ((own_y + 4 - n) % 4) + jnp.bitwise_xor(own_z, x + 4 * o)])
                right.append(schur_ref[n, x, o])
    return dot(jnp.concatenate(left, axis=1), jnp.concatenate(right, axis=1), NT)


def keep(rhs, rhs_ref):
    for h in range(ROWS):
        for side in range(2):
            rhs_ref[2 * h + side] = rhs[h, :, side * LANES : (side + 1) * LANES]


def rhs_kernel(recv_hbm, rhs_ref, map_out, recv_ref, sems):
    wait_for(fetch([recv_hbm], [recv_ref], sems))
    map_out[...] = recv_ref[:, VALUE_ROWS:, :]
    keep(right_hand_side(recv_ref, map_out), rhs_ref)


def product_kernel(rhs_hbm, *refs):
    parts, (send_ref, schur_ref, rhs_ref, sems, rhs_sem) = refs[:5], refs[5:]
    copies = schur_copies(parts, schur_ref, sems)
    wait_for(fetch([rhs_hbm], [rhs_ref], rhs_sem))
    total = schur_product(rhs_ref, schur_ref, copies)
    for r in range(send_ref.shape[0]):
        send_ref[r] = total


def interface_kernel(recv_hbm, map_hbm, *refs):
    parts, (iface_ref, send_ref, schur_ref, rhs_ref, recv_ref, map_ref, sems, recv_sems) = refs[:5], refs[5:]
    arrived = fetch([map_hbm, recv_hbm], [map_ref, recv_ref], recv_sems)
    copies = schur_copies(parts, schur_ref, sems)
    wait_for(arrived)
    keep(right_hand_side(recv_ref, map_ref), rhs_ref)
    total = schur_product(rhs_ref, schur_ref, copies)
    iface_ref[...] = total
    half = total.astype(BF16)
    for r in range(ROWS):
        send_ref[r] = half


def driven(recv_ref, right_ref, rows_ref, sender):
    hi = rows_ref[0:1, :].astype(jnp.int32)
    volts = recv_ref[...].reshape(ROWS * SCEN, BLOCK)
    found = sum(dot(part, right_ref[...]) for part in (halves(volts) if volts.dtype == F32 else (volts,)))
    picked = jnp.zeros((SCEN, OWN), F32)
    for n in range(ROWS):
        picked += jnp.where(hi == sender(n), found[n * SCEN : (n + 1) * SCEN, :], 0.0)
    return (rows_ref[1:2, :] * picked).astype(BF16)


def update(k, drive, open_ref, inv, volt, curr, breaker_ref, gain_ref):
    volt_next = open_ref[k] + dot(drive[:, k * PORTS : (k + 1) * PORTS], inv)
    closed = breaker_ref[k].astype(F32)
    return volt_next, closed * (curr + gain_ref[k : k + 1, :] * (volt_next + volt))


def paired_sender(place):
    return CORES[place // (ROWS // 2)][place % (ROWS // 2)]


def middle_kernel(time_ref, node_ref, recv_hbm, prev_hbm, volt_hbm, curr_hbm, breaker_hbm, gain_hbm, tie_hbm, right_hbm, rows_hbm, inv_hbm, volt_out, curr_out, open_ref, send_ref, recv_ref, prev_ref, right_ref, rows_ref, gain_ref, tie_ref, volt_ref, curr_ref, breaker_ref, inv_ref, sems):
    copies = fetch(
        [right_hbm, rows_hbm, recv_hbm, prev_hbm, volt_hbm, curr_hbm, breaker_hbm, gain_hbm, tie_hbm] + each(inv_hbm, SUBS),
        [right_ref, rows_ref, recv_ref, prev_ref, volt_ref, curr_ref, breaker_ref, gain_ref, tie_ref] + each(inv_ref, SUBS),
        sems,
    )
    wait_for(copies[:3])
    drive = driven(recv_ref, right_ref, rows_ref, paired_sender)
    wait_for(copies[3:9])
    for k in range(SUBS):
        copies[9 + k].wait()
        volt_out[k], curr_out[k] = update(k, drive, prev_ref, inv_ref[k, :PORTS, :], volt_ref[k], curr_ref[k], breaker_ref, gain_ref)
    open_circuit(1, volt_out, curr_out, breaker_ref, gain_ref, None, inv_ref, time_ref, node_ref, tie_ref, open_ref, send_ref)


def last_kernel(recv_hbm, prev_hbm, volt_hbm, curr_hbm, breaker_hbm, gain_hbm, right_hbm, rows_hbm, inv_hbm, volt_out, curr_out, recv_ref, prev_ref, right_ref, rows_ref, gain_ref, volt_ref, curr_ref, breaker_ref, inv_ref, sems):
    copies = fetch(
        [right_hbm, rows_hbm, recv_hbm, prev_hbm, volt_hbm, curr_hbm, breaker_hbm, gain_hbm] + [inv_hbm.at[k, pl.ds(0, PORTS)] for k in range(SUBS)],
        [right_ref, rows_ref, recv_ref, prev_ref, volt_ref, curr_ref, breaker_ref, gain_ref] + each(inv_ref, SUBS),
        sems,
    )
    wait_for(copies[:3])
    drive = driven(recv_ref, right_ref, rows_ref, TURNED.__getitem__)
    wait_for(copies[3:])
    for k in range(SUBS):
        volt_out[k], curr_out[k] = update(k, drive, prev_ref, inv_ref[k], volt_ref[k], curr_ref[k], breaker_ref, gain_ref)


SMEM = pl.BlockSpec(memory_space=pltpu.SMEM)
VMEM = pl.BlockSpec(memory_space=pltpu.VMEM)
HBM = pl.BlockSpec(memory_space=pltpu.HBM)

STATE = ((SUBS, SCEN, NODES), F32)
SCHUR = ((4, 4, 2, BLOCK, LANES), BF16)
RHS = ((COLS, SCEN, LANES), BF16)
MAPS = ((ROWS, MAP_ROWS, LANES), F32)
FACE = (ROWS, SCEN, BLOCK)
GIGA = 1_000_000_000


def held(*shapes):
    return [pltpu.VMEM(*shape) for shape in shapes]


def copies_of(count):
    return [pltpu.SemaphoreType.DMA((count,))]


GAIN, TIE = held(((SUBS, NODES), F32), ((SUBS, PORTS), F32))
BREAKER = held(((SUBS, SCEN, NODES), jnp.int32))
INVERSE = held(((SUBS, NODES, NODES), BF16))
PICK = [((BLOCK, OWN), BF16), ((8, OWN), F32)]


def call(body, ins, outs, scratch, flops, moved, vmem=VMEM_BYTES):
    return pl.pallas_call(
        body,
        out_shape=[jax.ShapeDtypeStruct(shape, kind) for shape, kind in outs],
        in_specs=ins,
        out_specs=[VMEM] * len(outs),
        scratch_shapes=scratch,
        compiler_params=pltpu.CompilerParams(vmem_limit_bytes=vmem),
        cost_estimate=pl.CostEstimate(flops=flops, bytes_accessed=moved, transcendentals=0),
    )


first = call(
    first_kernel,
    [SMEM] * 2 + [HBM] * 7,
    [STATE, ((ROWS // 2, VALUE_ROWS + MAP_ROWS, LANES), F32)] + PICK,
    held(((SUBS, PORTS), jnp.int32)) + [GAIN, TIE] + held(STATE, STATE) + BREAKER + INVERSE + copies_of(6 + SUBS),
    GIGA,
    4 << 20,
    ALL_VMEM,
)
join = call(join_kernel, [VMEM] * 5, [((4, 2, BLOCK, LANES), BF16)], [], 100_000 * GIGA, 1 << 20, 8 << 20)
summed = call(rhs_kernel, [HBM], [RHS, MAPS], held(((ROWS, VALUE_ROWS + MAP_ROWS, LANES), F32)) + copies_of(1), GIGA, 1 << 20)
product = call(product_kernel, [HBM] * 6, [((ROWS // 2, SCEN, BLOCK), F32)], held(SCHUR, RHS) + copies_of(5) + copies_of(1), GIGA, 3 << 20)
interface = call(
    interface_kernel,
    [HBM] * 7,
    [(FACE[1:], F32), (FACE, BF16)],
    held(SCHUR, RHS, ((ROWS, VALUE_ROWS, LANES), BF16), MAPS) + copies_of(5) + copies_of(2),
    GIGA,
    3 << 20,
)
middle = call(
    middle_kernel,
    [SMEM] * 2 + [HBM] * 10,
    [STATE, STATE, STATE, ((ROWS // 2, VALUE_ROWS, LANES), BF16)],
    held((FACE, F32), STATE, *PICK) + [GAIN, TIE] + held(STATE, STATE) + BREAKER + INVERSE + copies_of(9 + SUBS),
    GIGA,
    4 << 20,
)
last = call(
    last_kernel,
    [HBM] * 9,
    [STATE, STATE],
    held((FACE, BF16), STATE, *PICK) + [GAIN] + held(STATE, STATE) + BREAKER + held(((SUBS, PORTS, NODES), BF16)) + copies_of(8 + SUBS),
    GIGA,
    2 << 20,
)


def along_z(block, flip):
    return lax.ppermute(block, "col", [(c, c ^ flip) for c in range(COLS)])


def along_y(block, steps):
    return lax.ppermute(block, "col", [(c, (c + 8 * steps) % COLS) for c in range(COLS)])


def exchange(send, groups):
    return lax.all_to_all(send, "row", 0, 0, axis_index_groups=groups)


def paired_exchange(send):
    both = lax.all_gather(exchange(send, CORES), "row", axis_index_groups=PAIRS)
    return both.reshape(ROWS, *send.shape[1:])


def local(volt, curr, local_inverse, schur_inverse, ind_gain, tie, port_map, breaker, fault_time, fault_node):
    with jax.named_scope("schur_z"):
        across = along_z(schur_inverse, 4)
    opened, send, *pick = first(fault_time, fault_node, volt, curr, breaker, ind_gain, tie, port_map, local_inverse)
    across, send = lax.optimization_barrier((across, send))
    with jax.named_scope("schur_z"):
        pair = jnp.stack([schur_inverse, across])
        (own,) = join(schur_inverse, across, *(along_z(pair, x) for x in (1, 2, 3)))
    with jax.named_scope("schur_y"):
        back, ahead = along_y(own, 1), along_y(own, -1)
        schur_rows = own, back, ahead, along_y(back[:2], 1), along_y(ahead[2:], -1)
    rhs, maps = summed(paired_exchange(send))
    (send,) = product(rhs, *schur_rows)
    volt, curr, opened, send = middle(fault_time, fault_node, paired_exchange(send), opened, volt, curr, breaker, ind_gain, tie, *pick, local_inverse)
    iface_block, send = interface(paired_exchange(send), maps, *schur_rows)
    volt, curr = last(exchange(send, [TURNED]), opened, volt, curr, breaker, ind_gain, *pick, local_inverse)
    return volt, curr, iface_block


def solution(mesh):
    placed = (
        P("row", "col", None),
        P("row", "col", None),
        P("row", None, None),
        P("row", "col"),
        P("row", None),
        P("row", None),
        P("row", None),
        P("row", "col", None),
        P("col"),
        P("col"),
    )
    return jax.shard_map(
        local,
        mesh=mesh,
        in_specs=placed,
        out_specs=(P("row", "col", None), P("row", "col", None), P("col", "row")),
        check_vma=False,
    )
```

```python
import jax
import jax.numpy as jnp
from jax import lax
from jax.experimental import pallas as pl
from jax.experimental.pallas import tpu as pltpu
from jax.sharding import PartitionSpec as P

ROWS = 16
COLS = 32
SUBS = 8
SCEN = 16
NODES = 400
PORTS = 64
OWN = SUBS * PORTS
BLOCK = 256
LANES = 128
TILES = OWN // LANES
VALUE_ROWS = TILES * SCEN
MAP_ROWS = 2 * TILES
TURNED = [(n + ROWS // 2) % ROWS for n in range(ROWS)]
CORES = [[r for r in TURNED if r % 2 == core] for core in range(2)]
PAIRS = [[2 * n, 2 * n + 1] for n in range(ROWS // 2)]
VMEM_BYTES = 16 << 20
ALL_VMEM = 60 << 20
BF16, F32 = jnp.bfloat16, jnp.float32

NN = (((1,), (0,)), ((), ()))
NT = (((1,), (1,)), ((), ()))


def dot(a, b, dims=NN):
    return lax.dot_general(a, b, dims, preferred_element_type=F32)


def halves(x):
    coarse = x.astype(BF16)
    return coarse, (x - coarse.astype(F32)).astype(BF16)


def fetch(sources, targets, sems):
    copies = [pltpu.make_async_copy(a, b, sems.at[n]) for n, (a, b) in enumerate(zip(sources, targets))]
    for copy in copies:
        copy.start()
    return copies


def wait_for(copies):
    for copy in copies:
        copy.wait()


def each(ref, count):
    return [ref.at[k] for k in range(count)]


def flat_row(ref):
    return jnp.concatenate([ref[k : k + 1, :] for k in range(SUBS)], axis=1)


def tiles_of(row):
    return [row[:, t * LANES : (t + 1) * LANES] for t in range(TILES)]


def column(ref):
    place = lax.broadcasted_iota(jnp.int32, (SCEN, 1), 0)
    out = jnp.zeros((SCEN, 1), jnp.int32)
    for s in range(SCEN):
        out = jnp.where(place == s, ref[s], out)
    return out


def open_circuit(step, volts, currs, breaker_ref, gain_ref, inv_copies, inv_ref, time_ref, node_ref, tie_ref, open_ref, send_ref):
    fault_node = jnp.where(step >= column(time_ref), column(node_ref), -1)
    first = lax.axis_index("row") * SUBS
    lane = lax.broadcasted_iota(jnp.int32, (SCEN, NODES), 1)
    parts = []
    for k in range(SUBS):
        volt = volts[k]
        hist = breaker_ref[k].astype(F32) * (currs[k] + gain_ref[k : k + 1, :] * volt)
        hit = lane + (first + k) * NODES == fault_node
        inject = (-hist - jnp.where(hit, 2.0 * volt, 0.0)).astype(BF16)
        if inv_copies:
            inv_copies[k].wait()
        open_k = dot(inject, inv_ref[k])
        open_ref[k] = open_k
        parts.append(tie_ref[k : k + 1, :] * open_k[:, :PORTS])
    values = jnp.concatenate(parts, axis=1).astype(send_ref.dtype)
    for t, tile in enumerate(tiles_of(values)):
        for r in range(send_ref.shape[0]):
            send_ref[r, t * SCEN : (t + 1) * SCEN, :] = tile


def first_kernel(time_ref, node_ref, volt_hbm, curr_hbm, breaker_hbm, gain_hbm, tie_hbm, map_hbm, inv_hbm, open_ref, send_ref, right_ref, rows_ref, map_ref, gain_ref, tie_ref, volt_ref, curr_ref, breaker_ref, inv_ref, sems):
    copies = fetch(
        [map_hbm, gain_hbm, tie_hbm, volt_hbm, curr_hbm, breaker_hbm] + each(inv_hbm, SUBS),
        [map_ref, gain_ref, tie_ref, volt_ref, curr_ref, breaker_ref] + each(inv_ref, SUBS),
        sems,
    )
    copies[0].wait()
    mapped = flat_row(map_ref)
    rows = tiles_of((mapped // BLOCK).astype(F32)) + tiles_of((mapped % BLOCK).astype(F32))
    tail = jnp.concatenate(rows, axis=0)
    for r in range(send_ref.shape[0]):
        send_ref[r, VALUE_ROWS:, :] = tail
    wait_for(copies[1:6])
    low = lax.broadcasted_iota(jnp.int32, (BLOCK, OWN), 0)
    right_ref[...] = jnp.where(low == mapped % BLOCK, 1.0, 0.0).astype(BF16)
    rows_ref[...] = jnp.concatenate([(mapped // BLOCK).astype(F32), flat_row(tie_ref), jnp.zeros((6, OWN), F32)], axis=0)
    open_circuit(0, volt_ref, curr_ref, breaker_ref, gain_ref, copies[6:], inv_ref, time_ref, node_ref, tie_ref, open_ref, send_ref)


def right_hand_side(recv_ref, map_ref):
    low = lax.broadcasted_iota(jnp.int32, (BLOCK, OWN), 0).astype(F32).astype(BF16)
    one, zero = jnp.ones((), BF16), jnp.zeros((), BF16)
    rhs = jnp.zeros((ROWS * SCEN, BLOCK), F32)
    for r in range(ROWS):
        tail = map_ref[r]
        hi = jnp.concatenate([tail[t : t + 1] for t in range(TILES)], axis=1)
        lo = jnp.concatenate([tail[TILES + t : TILES + t + 1] for t in range(TILES)], axis=1)
        hi = jnp.broadcast_to(hi, (SCEN, OWN)).astype(BF16)
        right = jnp.where(low == lo.astype(BF16), one, zero)
        values = jnp.concatenate([recv_ref[r, t * SCEN : (t + 1) * SCEN, :] for t in range(TILES)], axis=1)
        for part in halves(values) if values.dtype == F32 else (values,):
            left = jnp.concatenate([jnp.where(hi == h, part, zero) for h in range(ROWS)], axis=0)
            rhs += dot(left, right, NT)
    return rhs.astype(BF16).reshape(ROWS, SCEN, BLOCK)


def join_kernel(own_ref, across_ref, *refs):
    quads, (out_ref,) = refs[:3], refs[3:]
    out_ref[0, 0] = own_ref[...]
    out_ref[0, 1] = across_ref[...]
    for x in (1, 2, 3):
        out_ref[x] = quads[x - 1][...]


def schur_product(rhs_ref, parts):
    own, back, ahead, far_low, far_high = parts
    col = lax.axis_index("col")
    own_y, own_z = col // 8, col % 8
    left, right = [], []
    for n in range(4):
        for x in range(4):
            for o in range(2):
                left.append(rhs_ref[8 * ((own_y + 4 - n) % 4) + jnp.bitwise_xor(own_z, x + 4 * o)])
                far = far_low if x < 2 else far_high
                right.append((own, back, far, ahead)[n][x % 2 if n == 2 else x, o])
    return dot(jnp.concatenate(left, axis=1), jnp.concatenate(right, axis=1), NT)


def keep(rhs, rhs_ref):
    for h in range(ROWS):
        for side in range(2):
            rhs_ref[2 * h + side] = rhs[h, :, side * LANES : (side + 1) * LANES]


def rhs_kernel(recv_ref, rhs_ref, map_out):
    map_out[...] = recv_ref[:, VALUE_ROWS:, :]
    keep(right_hand_side(recv_ref, map_out), rhs_ref)


def product_kernel(rhs_ref, *refs):
    parts, (send_ref,) = refs[:5], refs[5:]
    total = schur_product(rhs_ref, parts)
    for r in range(send_ref.shape[0]):
        send_ref[r] = total


def interface_kernel(recv_ref, map_ref, *refs):
    parts, (iface_ref, send_ref, rhs_ref) = refs[:5], refs[5:]
    keep(right_hand_side(recv_ref, map_ref), rhs_ref)
    total = schur_product(rhs_ref, parts)
    iface_ref[...] = total
    half = total.astype(BF16)
    for r in range(ROWS):
        send_ref[r] = half


def driven(recv_ref, right_ref, rows_ref, sender):
    hi = rows_ref[0:1, :].astype(jnp.int32)
    volts = recv_ref[...].reshape(ROWS * SCEN, BLOCK)
    found = sum(dot(part, right_ref[...]) for part in (halves(volts) if volts.dtype == F32 else (volts,)))
    picked = jnp.zeros((SCEN, OWN), F32)
    for n in range(ROWS):
        picked += jnp.where(hi == sender(n), found[n * SCEN : (n + 1) * SCEN, :], 0.0)
    return (rows_ref[1:2, :] * picked).astype(BF16)


def update(k, drive, open_ref, inv, volt, curr, breaker_ref, gain_ref):
    volt_next = open_ref[k] + dot(drive[:, k * PORTS : (k + 1) * PORTS], inv)
    closed = breaker_ref[k].astype(F32)
    return volt_next, closed * (curr + gain_ref[k : k + 1, :] * (volt_next + volt))


def paired_sender(place):
    return CORES[place // (ROWS // 2)][place % (ROWS // 2)]


def middle_kernel(time_ref, node_ref, recv_ref, prev_ref, volt_ref, curr_ref, breaker_ref, gain_ref, tie_ref, right_ref, rows_ref, inv_ref, volt_out, curr_out, open_ref, send_ref):
    drive = driven(recv_ref, right_ref, rows_ref, paired_sender)
    for k in range(SUBS):
        volt_out[k], curr_out[k] = update(k, drive, prev_ref, inv_ref[k, :PORTS, :], volt_ref[k], curr_ref[k], breaker_ref, gain_ref)
    open_circuit(1, volt_out, curr_out, breaker_ref, gain_ref, None, inv_ref, time_ref, node_ref, tie_ref, open_ref, send_ref)


def last_kernel(recv_ref, prev_ref, volt_ref, curr_ref, breaker_ref, gain_ref, right_ref, rows_ref, face_ref, inv_hbm, volt_out, curr_out, face_out, inv_ref, sems):
    copies = fetch([inv_hbm.at[k, pl.ds(0, PORTS)] for k in range(SUBS)], each(inv_ref, SUBS), sems)
    face_out[...] = face_ref[...]
    drive = driven(recv_ref, right_ref, rows_ref, TURNED.__getitem__)
    wait_for(copies)
    for k in range(SUBS):
        volt_out[k], curr_out[k] = update(k, drive, prev_ref, inv_ref[k], volt_ref[k], curr_ref[k], breaker_ref, gain_ref)


SMEM = pl.BlockSpec(memory_space=pltpu.SMEM)
VMEM = pl.BlockSpec(memory_space=pltpu.VMEM)
HBM = pl.BlockSpec(memory_space=pltpu.HBM)

STATE = ((SUBS, SCEN, NODES), F32)
RHS = ((COLS, SCEN, LANES), BF16)
MAPS = ((ROWS, MAP_ROWS, LANES), F32)
FACE = (ROWS, SCEN, BLOCK)
GIGA = 1_000_000_000


def held(*shapes):
    return [pltpu.VMEM(*shape) for shape in shapes]


def copies_of(count):
    return [pltpu.SemaphoreType.DMA((count,))]


GAIN, TIE = held(((SUBS, NODES), F32), ((SUBS, PORTS), F32))
BREAKER = held(((SUBS, SCEN, NODES), jnp.int32))
INVERSE = held(((SUBS, NODES, NODES), BF16))
PICK = [((BLOCK, OWN), BF16), ((8, OWN), F32)]


def call(body, ins, outs, scratch, flops, moved, vmem=VMEM_BYTES):
    return pl.pallas_call(
        body,
        out_shape=[jax.ShapeDtypeStruct(shape, kind) for shape, kind in outs],
        in_specs=ins,
        out_specs=[VMEM] * len(outs),
        scratch_shapes=scratch,
        compiler_params=pltpu.CompilerParams(vmem_limit_bytes=vmem),
        cost_estimate=pl.CostEstimate(flops=flops, bytes_accessed=moved, transcendentals=0),
    )


first = call(
    first_kernel,
    [SMEM] * 2 + [HBM] * 7,
    [STATE, ((ROWS // 2, VALUE_ROWS + MAP_ROWS, LANES), F32)] + PICK,
    held(((SUBS, PORTS), jnp.int32)) + [GAIN, TIE] + held(STATE, STATE) + BREAKER + INVERSE + copies_of(6 + SUBS),
    GIGA,
    4 << 20,
    ALL_VMEM,
)
join = call(join_kernel, [VMEM] * 5, [((4, 2, BLOCK, LANES), BF16)], [], 100_000 * GIGA, 1 << 20, 8 << 20)
summed = call(rhs_kernel, [VMEM], [RHS, MAPS], [], GIGA, 1 << 20)
product = call(product_kernel, [VMEM] * 6, [((ROWS // 2, SCEN, BLOCK), F32)], [], GIGA, 3 << 20)
interface = call(interface_kernel, [VMEM] * 7, [(FACE[1:], F32), (FACE, BF16)], held(RHS), GIGA, 3 << 20)
middle = call(middle_kernel, [SMEM] * 2 + [VMEM] * 10, [STATE, STATE, STATE, ((ROWS // 2, VALUE_ROWS, LANES), BF16)], [], GIGA, 4 << 20)
last = call(
    last_kernel,
    [VMEM] * 9 + [HBM],
    [STATE, STATE, (FACE[1:], F32)],
    held(((SUBS, PORTS, NODES), BF16)) + copies_of(SUBS),
    GIGA,
    2 << 20,
)


def along_z(block, flip):
    return lax.ppermute(block, "col", [(c, c ^ flip) for c in range(COLS)])


def along_y(block, steps):
    return lax.ppermute(block, "col", [(c, (c + 8 * steps) % COLS) for c in range(COLS)])


def exchange(send, groups):
    return lax.all_to_all(send, "row", 0, 0, axis_index_groups=groups)


def paired_exchange(send):
    both = lax.all_gather(exchange(send, CORES), "row", axis_index_groups=PAIRS)
    return both.reshape(ROWS, *send.shape[1:])


def local(volt, curr, local_inverse, schur_inverse, ind_gain, tie, port_map, breaker, fault_time, fault_node):
    with jax.named_scope("schur_z"):
        across = along_z(schur_inverse, 4)
    opened, send, *pick = first(fault_time, fault_node, volt, curr, breaker, ind_gain, tie, port_map, local_inverse)
    across, send = lax.optimization_barrier((across, send))
    with jax.named_scope("schur_z"):
        pair = jnp.stack([schur_inverse, across])
        (own,) = join(schur_inverse, across, *(along_z(pair, x) for x in (1, 2, 3)))
    with jax.named_scope("schur_y"):
        back, ahead = along_y(own, 1), along_y(own, -1)
        schur_rows = own, back, ahead, along_y(back[:2], 1), along_y(ahead[2:], -1)
    rhs, maps = summed(paired_exchange(send))
    (send,) = product(rhs, *schur_rows)
    volt, curr, opened, send = middle(fault_time, fault_node, paired_exchange(send), opened, volt, curr, breaker, ind_gain, tie, *pick, local_inverse)
    face, send = interface(paired_exchange(send), maps, *schur_rows)
    return tuple(last(exchange(send, [TURNED]), opened, volt, curr, breaker, ind_gain, *pick, face, local_inverse))


def solution(mesh):
    placed = (
        P("row", "col", None),
        P("row", "col", None),
        P("row", None, None),
        P("row", "col"),
        P("row", None),
        P("row", None),
        P("row", None),
        P("row", "col", None),
        P("col"),
        P("col"),
    )
    return jax.shard_map(
        local,
        mesh=mesh,
        in_specs=placed,
        out_specs=(P("row", "col", None), P("row", "col", None), P("col", "row")),
        check_vma=False,
    )
```

```python
import jax
import jax.numpy as jnp
from jax import lax
from jax.experimental import pallas as pl
from jax.experimental.pallas import tpu as pltpu
from jax.sharding import PartitionSpec as P

ROWS = 16
COLS = 32
SUBS = 8
SCEN = 16
NODES = 400
PORTS = 64
OWN = SUBS * PORTS
BLOCK = 256
LANES = 128
TILES = OWN // LANES
VALUE_ROWS = TILES * SCEN
MAP_ROWS = 2 * TILES
TURNED = [(n + ROWS // 2) % ROWS for n in range(ROWS)]
CORES = [[r for r in TURNED if r % 2 == core] for core in range(2)]
PAIRS = [[2 * n, 2 * n + 1] for n in range(ROWS // 2)]
VMEM_BYTES = 16 << 20
ALL_VMEM = 60 << 20
BF16, F32 = jnp.bfloat16, jnp.float32

NN = (((1,), (0,)), ((), ()))
NT = (((1,), (1,)), ((), ()))


def dot(a, b, dims=NN):
    return lax.dot_general(a, b, dims, preferred_element_type=F32)


def halves(x):
    coarse = x.astype(BF16)
    return coarse, (x - coarse.astype(F32)).astype(BF16)


def fetch(sources, targets, sems):
    copies = [pltpu.make_async_copy(a, b, sems.at[n]) for n, (a, b) in enumerate(zip(sources, targets))]
    for copy in copies:
        copy.start()
    return copies


def wait_for(copies):
    for copy in copies:
        copy.wait()


def each(ref, count):
    return [ref.at[k] for k in range(count)]


def flat_row(ref):
    return jnp.concatenate([ref[k : k + 1, :] for k in range(SUBS)], axis=1)


def tiles_of(row):
    return [row[:, t * LANES : (t + 1) * LANES] for t in range(TILES)]


def column(ref):
    place = lax.broadcasted_iota(jnp.int32, (SCEN, 1), 0)
    out = jnp.zeros((SCEN, 1), jnp.int32)
    for s in range(SCEN):
        out = jnp.where(place == s, ref[s], out)
    return out


def open_circuit(step, volts, currs, breaker_ref, gain_ref, inv_copies, inv_ref, time_ref, node_ref, tie_ref, open_ref, send_ref):
    fault_node = jnp.where(step >= column(time_ref), column(node_ref), -1)
    first = lax.axis_index("row") * SUBS
    lane = lax.broadcasted_iota(jnp.int32, (SCEN, NODES), 1)
    parts = []
    for k in range(SUBS):
        volt = volts[k]
        hist = breaker_ref[k].astype(F32) * (currs[k] + gain_ref[k : k + 1, :] * volt)
        hit = lane + (first + k) * NODES == fault_node
        inject = (-hist - jnp.where(hit, 2.0 * volt, 0.0)).astype(BF16)
        if inv_copies:
            inv_copies[k].wait()
        open_k = dot(inject, inv_ref[k])
        open_ref[k] = open_k
        parts.append(tie_ref[k : k + 1, :] * open_k[:, :PORTS])
    values = jnp.concatenate(parts, axis=1).astype(send_ref.dtype)
    for t, tile in enumerate(tiles_of(values)):
        for r in range(send_ref.shape[0]):
            send_ref[r, t * SCEN : (t + 1) * SCEN, :] = tile


def first_kernel(time_ref, node_ref, volt_hbm, curr_hbm, breaker_hbm, gain_hbm, tie_hbm, map_hbm, inv_hbm, open_ref, send_ref, right_ref, rows_ref, map_ref, gain_ref, tie_ref, volt_ref, curr_ref, breaker_ref, inv_ref, sems):
    copies = fetch(
        [map_hbm, gain_hbm, tie_hbm, volt_hbm, curr_hbm, breaker_hbm] + each(inv_hbm, SUBS),
        [map_ref, gain_ref, tie_ref, volt_ref, curr_ref, breaker_ref] + each(inv_ref, SUBS),
        sems,
    )
    copies[0].wait()
    mapped = flat_row(map_ref)
    rows = tiles_of((mapped // BLOCK).astype(F32)) + tiles_of((mapped % BLOCK).astype(F32))
    tail = jnp.concatenate(rows, axis=0)
    for r in range(send_ref.shape[0]):
        send_ref[r, VALUE_ROWS:, :] = tail
    wait_for(copies[1:6])
    low = lax.broadcasted_iota(jnp.int32, (BLOCK, OWN), 0)
    right_ref[...] = jnp.where(low == mapped % BLOCK, 1.0, 0.0).astype(BF16)
    rows_ref[...] = jnp.concatenate([(mapped // BLOCK).astype(F32), flat_row(tie_ref), jnp.zeros((6, OWN), F32)], axis=0)
    open_circuit(0, volt_ref, curr_ref, breaker_ref, gain_ref, copies[6:], inv_ref, time_ref, node_ref, tie_ref, open_ref, send_ref)


def right_hand_side(recv_ref, map_ref):
    low = lax.broadcasted_iota(jnp.int32, (BLOCK, OWN), 0).astype(F32).astype(BF16)
    one, zero = jnp.ones((), BF16), jnp.zeros((), BF16)
    rhs = jnp.zeros((ROWS * SCEN, BLOCK), F32)
    for r in range(ROWS):
        tail = map_ref[r]
        hi = jnp.concatenate([tail[t : t + 1] for t in range(TILES)], axis=1)
        lo = jnp.concatenate([tail[TILES + t : TILES + t + 1] for t in range(TILES)], axis=1)
        hi = jnp.broadcast_to(hi, (SCEN, OWN)).astype(BF16)
        right = jnp.where(low == lo.astype(BF16), one, zero)
        values = jnp.concatenate([recv_ref[r, t * SCEN : (t + 1) * SCEN, :] for t in range(TILES)], axis=1)
        for part in halves(values) if values.dtype == F32 else (values,):
            left = jnp.concatenate([jnp.where(hi == h, part, zero) for h in range(ROWS)], axis=0)
            rhs += dot(left, right, NT)
    return rhs.astype(BF16).reshape(ROWS, SCEN, BLOCK)


def join_kernel(own_ref, across_ref, *refs):
    quads, (out_ref,) = refs[:3], refs[3:]
    out_ref[0, 0] = own_ref[...]
    out_ref[0, 1] = across_ref[...]
    for x in (1, 2, 3):
        out_ref[x] = quads[x - 1][...]


def schur_product(rhs_ref, parts):
    own, back, ahead, far_low, far_high = parts
    col = lax.axis_index("col")
    own_y, own_z = col // 8, col % 8
    left, right = [], []
    for n in range(4):
        for x in range(4):
            for o in range(2):
                left.append(rhs_ref[8 * ((own_y + 4 - n) % 4) + jnp.bitwise_xor(own_z, x + 4 * o)])
                far = far_low if x < 2 else far_high
                right.append((own, back, far, ahead)[n][x % 2 if n == 2 else x, o])
    return dot(jnp.concatenate(left, axis=1), jnp.concatenate(right, axis=1), NT)


def keep(rhs, rhs_ref):
    for h in range(ROWS):
        for side in range(2):
            rhs_ref[2 * h + side] = rhs[h, :, side * LANES : (side + 1) * LANES]


def rhs_kernel(recv_ref, rhs_ref, map_out):
    map_out[...] = recv_ref[:, VALUE_ROWS:, :]
    keep(right_hand_side(recv_ref, map_out), rhs_ref)


def product_kernel(rhs_ref, *refs):
    parts, (send_ref,) = refs[:5], refs[5:]
    total = schur_product(rhs_ref, parts)
    for r in range(send_ref.shape[0]):
        send_ref[r] = total


def interface_kernel(recv_ref, map_ref, *refs):
    parts, (iface_ref, send_ref, rhs_ref) = refs[:5], refs[5:]
    keep(right_hand_side(recv_ref, map_ref), rhs_ref)
    total = schur_product(rhs_ref, parts)
    iface_ref[...] = total
    half = total.astype(BF16)
    for r in range(send_ref.shape[0]):
        send_ref[r] = half


def driven(recv_ref, right_ref, rows_ref):
    hi = rows_ref[0:1, :].astype(jnp.int32)
    volts = recv_ref[...].reshape(ROWS * SCEN, BLOCK)
    found = sum(dot(part, right_ref[...]) for part in (halves(volts) if volts.dtype == F32 else (volts,)))
    picked = jnp.zeros((SCEN, OWN), F32)
    for n in range(ROWS):
        picked += jnp.where(hi == paired_sender(n), found[n * SCEN : (n + 1) * SCEN, :], 0.0)
    return (rows_ref[1:2, :] * picked).astype(BF16)


def update(k, drive, open_ref, inv, volt, curr, breaker_ref, gain_ref):
    volt_next = open_ref[k] + dot(drive[:, k * PORTS : (k + 1) * PORTS], inv)
    closed = breaker_ref[k].astype(F32)
    return volt_next, closed * (curr + gain_ref[k : k + 1, :] * (volt_next + volt))


def paired_sender(place):
    return CORES[place // (ROWS // 2)][place % (ROWS // 2)]


def middle_kernel(time_ref, node_ref, recv_ref, prev_ref, volt_ref, curr_ref, breaker_ref, gain_ref, tie_ref, right_ref, rows_ref, inv_ref, volt_out, curr_out, open_ref, send_ref):
    drive = driven(recv_ref, right_ref, rows_ref)
    for k in range(SUBS):
        volt_out[k], curr_out[k] = update(k, drive, prev_ref, inv_ref[k, :PORTS, :], volt_ref[k], curr_ref[k], breaker_ref, gain_ref)
    open_circuit(1, volt_out, curr_out, breaker_ref, gain_ref, None, inv_ref, time_ref, node_ref, tie_ref, open_ref, send_ref)


def last_kernel(recv_ref, prev_ref, volt_ref, curr_ref, breaker_ref, gain_ref, right_ref, rows_ref, face_ref, inv_hbm, volt_out, curr_out, face_out, inv_ref, sems):
    copies = fetch([inv_hbm.at[k, pl.ds(0, PORTS)] for k in range(SUBS)], each(inv_ref, SUBS), sems)
    face_out[...] = face_ref[...]
    drive = driven(recv_ref, right_ref, rows_ref)
    wait_for(copies)
    for k in range(SUBS):
        volt_out[k], curr_out[k] = update(k, drive, prev_ref, inv_ref[k], volt_ref[k], curr_ref[k], breaker_ref, gain_ref)


SMEM = pl.BlockSpec(memory_space=pltpu.SMEM)
VMEM = pl.BlockSpec(memory_space=pltpu.VMEM)
HBM = pl.BlockSpec(memory_space=pltpu.HBM)

STATE = ((SUBS, SCEN, NODES), F32)
RHS = ((COLS, SCEN, LANES), BF16)
MAPS = ((ROWS, MAP_ROWS, LANES), F32)
FACE = (ROWS, SCEN, BLOCK)
GIGA = 1_000_000_000


def held(*shapes):
    return [pltpu.VMEM(*shape) for shape in shapes]


def copies_of(count):
    return [pltpu.SemaphoreType.DMA((count,))]


GAIN, TIE = held(((SUBS, NODES), F32), ((SUBS, PORTS), F32))
BREAKER = held(((SUBS, SCEN, NODES), jnp.int32))
INVERSE = held(((SUBS, NODES, NODES), BF16))
PICK = [((BLOCK, OWN), BF16), ((8, OWN), F32)]


def call(body, ins, outs, scratch, flops, moved, vmem=VMEM_BYTES):
    return pl.pallas_call(
        body,
        out_shape=[jax.ShapeDtypeStruct(shape, kind) for shape, kind in outs],
        in_specs=ins,
        out_specs=[VMEM] * len(outs),
        scratch_shapes=scratch,
        compiler_params=pltpu.CompilerParams(vmem_limit_bytes=vmem),
        cost_estimate=pl.CostEstimate(flops=flops, bytes_accessed=moved, transcendentals=0),
    )


first = call(
    first_kernel,
    [SMEM] * 2 + [HBM] * 7,
    [STATE, ((ROWS // 2, VALUE_ROWS + MAP_ROWS, LANES), F32)] + PICK,
    held(((SUBS, PORTS), jnp.int32)) + [GAIN, TIE] + held(STATE, STATE) + BREAKER + INVERSE + copies_of(6 + SUBS),
    GIGA,
    4 << 20,
    ALL_VMEM,
)
join = call(join_kernel, [VMEM] * 5, [((4, 2, BLOCK, LANES), BF16)], [], 100_000 * GIGA, 1 << 20, 8 << 20)
summed = call(rhs_kernel, [VMEM], [RHS, MAPS], [], GIGA, 1 << 20)
product = call(product_kernel, [VMEM] * 6, [((ROWS // 2, SCEN, BLOCK), F32)], [], GIGA, 3 << 20)
interface = call(interface_kernel, [VMEM] * 7, [(FACE[1:], F32), ((ROWS // 2, SCEN, BLOCK), BF16)], held(RHS), GIGA, 3 << 20)
middle = call(middle_kernel, [SMEM] * 2 + [VMEM] * 10, [STATE, STATE, STATE, ((ROWS // 2, VALUE_ROWS, LANES), BF16)], [], GIGA, 4 << 20)
last = call(
    last_kernel,
    [VMEM] * 9 + [HBM],
    [STATE, STATE, (FACE[1:], F32)],
    held(((SUBS, PORTS, NODES), BF16)) + copies_of(SUBS),
    GIGA,
    2 << 20,
)


def along_z(block, flip):
    return lax.ppermute(block, "col", [(c, c ^ flip) for c in range(COLS)])


def along_y(block, steps):
    return lax.ppermute(block, "col", [(c, (c + 8 * steps) % COLS) for c in range(COLS)])


def exchange(send, groups):
    return lax.all_to_all(send, "row", 0, 0, axis_index_groups=groups)


def paired_exchange(send):
    both = lax.all_gather(exchange(send, CORES), "row", axis_index_groups=PAIRS)
    return both.reshape(ROWS, *send.shape[1:])


def local(volt, curr, local_inverse, schur_inverse, ind_gain, tie, port_map, breaker, fault_time, fault_node):
    with jax.named_scope("schur_z"):
        across = along_z(schur_inverse, 4)
    opened, send, *pick = first(fault_time, fault_node, volt, curr, breaker, ind_gain, tie, port_map, local_inverse)
    across, send = lax.optimization_barrier((across, send))
    with jax.named_scope("schur_z"):
        pair = jnp.stack([schur_inverse, across])
        (own,) = join(schur_inverse, across, *(along_z(pair, x) for x in (1, 2, 3)))
    with jax.named_scope("schur_y"):
        back, ahead = along_y(own, 1), along_y(own, -1)
        schur_rows = own, back, ahead, along_y(back[:2], 1), along_y(ahead[2:], -1)
    rhs, maps = summed(paired_exchange(send))
    (send,) = product(rhs, *schur_rows)
    volt, curr, opened, send = middle(fault_time, fault_node, paired_exchange(send), opened, volt, curr, breaker, ind_gain, tie, *pick, local_inverse)
    face, send = interface(paired_exchange(send), maps, *schur_rows)
    return tuple(last(paired_exchange(send), opened, volt, curr, breaker, ind_gain, *pick, face, local_inverse))


def solution(mesh):
    placed = (
        P("row", "col", None),
        P("row", "col", None),
        P("row", None, None),
        P("row", "col"),
        P("row", None),
        P("row", None),
        P("row", None),
        P("row", "col", None),
        P("col"),
        P("col"),
    )
    return jax.shard_map(
        local,
        mesh=mesh,
        in_specs=placed,
        out_specs=(P("row", "col", None), P("row", "col", None), P("col", "row")),
        check_vma=False,
    )
```

```python
import jax
import jax.numpy as jnp
from jax import lax
from jax.experimental import pallas as pl
from jax.experimental.pallas import tpu as pltpu
from jax.sharding import PartitionSpec as P

ROWS = 16
COLS = 32
SUBS = 8
SCEN = 16
NODES = 400
PORTS = 64
OWN = SUBS * PORTS
BLOCK = 256
LANES = 128
TILES = OWN // LANES
VALUE_ROWS = TILES * SCEN
MAP_ROWS = 2 * TILES
TURNED = [(n + ROWS // 2) % ROWS for n in range(ROWS)]
CORES = [[r for r in TURNED if r % 2 == core] for core in range(2)]
PAIRS = [[2 * n, 2 * n + 1] for n in range(ROWS // 2)]
VMEM_BYTES = 16 << 20
ALL_VMEM = 60 << 20
BF16, F32 = jnp.bfloat16, jnp.float32

NN = (((1,), (0,)), ((), ()))
NT = (((1,), (1,)), ((), ()))


def dot(a, b, dims=NN):
    return lax.dot_general(a, b, dims, preferred_element_type=F32)


def halves(x):
    coarse = x.astype(BF16)
    return coarse, (x - coarse.astype(F32)).astype(BF16)


def fetch(sources, targets, sems):
    copies = [pltpu.make_async_copy(a, b, sems.at[n]) for n, (a, b) in enumerate(zip(sources, targets))]
    for copy in copies:
        copy.start()
    return copies


def wait_for(copies):
    for copy in copies:
        copy.wait()


def each(ref, count):
    return [ref.at[k] for k in range(count)]


def flat_row(ref):
    return jnp.concatenate([ref[k : k + 1, :] for k in range(SUBS)], axis=1)


def tiles_of(row):
    return [row[:, t * LANES : (t + 1) * LANES] for t in range(TILES)]


def column(ref):
    place = lax.broadcasted_iota(jnp.int32, (SCEN, 1), 0)
    out = jnp.zeros((SCEN, 1), jnp.int32)
    for s in range(SCEN):
        out = jnp.where(place == s, ref[s], out)
    return out


def open_circuit(step, volts, currs, breaker_ref, gain_ref, inv_copies, inv_ref, time_ref, node_ref, tie_ref, open_ref, send_ref):
    fault_node = jnp.where(step >= column(time_ref), column(node_ref), -1)
    first = lax.axis_index("row") * SUBS
    lane = lax.broadcasted_iota(jnp.int32, (SCEN, NODES), 1)
    parts = []
    for k in range(SUBS):
        volt = volts[k]
        hist = breaker_ref[k].astype(F32) * (currs[k] + gain_ref[k : k + 1, :] * volt)
        hit = lane + (first + k) * NODES == fault_node
        inject = (-hist - jnp.where(hit, 2.0 * volt, 0.0)).astype(BF16)
        if inv_copies:
            inv_copies[k].wait()
        open_k = dot(inject, inv_ref[k])
        open_ref[k] = open_k
        parts.append(tie_ref[k : k + 1, :] * open_k[:, :PORTS])
    values = jnp.concatenate(parts, axis=1).astype(send_ref.dtype)
    for t, tile in enumerate(tiles_of(values)):
        for r in range(send_ref.shape[0]):
            send_ref[r, t * SCEN : (t + 1) * SCEN, :] = tile


def first_kernel(time_ref, node_ref, volt_hbm, curr_hbm, breaker_hbm, gain_hbm, tie_hbm, map_hbm, inv_hbm, open_ref, send_ref, right_ref, rows_ref, map_ref, gain_ref, tie_ref, volt_ref, curr_ref, breaker_ref, inv_ref, sems):
    copies = fetch(
        [map_hbm, gain_hbm, tie_hbm, volt_hbm, curr_hbm, breaker_hbm] + each(inv_hbm, SUBS),
        [map_ref, gain_ref, tie_ref, volt_ref, curr_ref, breaker_ref] + each(inv_ref, SUBS),
        sems,
    )
    copies[0].wait()
    mapped = flat_row(map_ref)
    rows = tiles_of((mapped // BLOCK).astype(F32)) + tiles_of((mapped % BLOCK).astype(F32))
    tail = jnp.concatenate(rows, axis=0)
    for r in range(send_ref.shape[0]):
        send_ref[r, VALUE_ROWS:, :] = tail
    wait_for(copies[1:6])
    low = lax.broadcasted_iota(jnp.int32, (BLOCK, OWN), 0)
    right_ref[...] = jnp.where(low == mapped % BLOCK, 1.0, 0.0).astype(BF16)
    rows_ref[...] = jnp.concatenate([(mapped // BLOCK).astype(F32), flat_row(tie_ref), jnp.zeros((6, OWN), F32)], axis=0)
    open_circuit(0, volt_ref, curr_ref, breaker_ref, gain_ref, copies[6:], inv_ref, time_ref, node_ref, tie_ref, open_ref, send_ref)


def right_hand_side(recv_ref, map_ref):
    low = lax.broadcasted_iota(jnp.int32, (BLOCK, OWN), 0).astype(F32).astype(BF16)
    one, zero = jnp.ones((), BF16), jnp.zeros((), BF16)
    rhs = jnp.zeros((ROWS * SCEN, BLOCK), F32)
    for r in range(ROWS):
        tail = map_ref[r]
        hi = jnp.concatenate([tail[t : t + 1] for t in range(TILES)], axis=1)
        lo = jnp.concatenate([tail[TILES + t : TILES + t + 1] for t in range(TILES)], axis=1)
        hi = jnp.broadcast_to(hi, (SCEN, OWN)).astype(BF16)
        right = jnp.where(low == lo.astype(BF16), one, zero)
        values = jnp.concatenate([recv_ref[r, t * SCEN : (t + 1) * SCEN, :] for t in range(TILES)], axis=1)
        for part in halves(values) if values.dtype == F32 else (values,):
            left = jnp.concatenate([jnp.where(hi == h, part, zero) for h in range(ROWS)], axis=0)
            rhs += dot(left, right, NT)
    return rhs.astype(BF16).reshape(ROWS, SCEN, BLOCK)


def join_kernel(own_ref, across_ref, near_ref, mid_ref, far_ref, low_ref, high_ref):
    low_ref[0, 0] = own_ref[...]
    low_ref[0, 1] = across_ref[...]
    low_ref[1] = near_ref[...]
    high_ref[0] = mid_ref[...]
    high_ref[1] = far_ref[...]


def schur_product(rhs_ref, parts):
    parts = [parts[2 * y : 2 * y + 2] for y in range(4)]
    col = lax.axis_index("col")
    own_y, own_z = col // 8, col % 8
    left, right = [], []
    for n in range(4):
        for x in range(4):
            for o in range(2):
                left.append(rhs_ref[8 * ((own_y + 4 - n) % 4) + jnp.bitwise_xor(own_z, x + 4 * o)])
                right.append(parts[n][x // 2][x % 2, o])
    return dot(jnp.concatenate(left, axis=1), jnp.concatenate(right, axis=1), NT)


def keep(rhs, rhs_ref):
    for h in range(ROWS):
        for side in range(2):
            rhs_ref[2 * h + side] = rhs[h, :, side * LANES : (side + 1) * LANES]


def rhs_kernel(recv_ref, rhs_ref, map_out):
    map_out[...] = recv_ref[:, VALUE_ROWS:, :]
    keep(right_hand_side(recv_ref, map_out), rhs_ref)


def product_kernel(rhs_ref, *refs):
    parts, (send_ref,) = refs[:8], refs[8:]
    total = schur_product(rhs_ref, parts)
    for r in range(send_ref.shape[0]):
        send_ref[r] = total


def interface_kernel(recv_ref, map_ref, *refs):
    parts, (iface_ref, send_ref, rhs_ref) = refs[:8], refs[8:]
    keep(right_hand_side(recv_ref, map_ref), rhs_ref)
    total = schur_product(rhs_ref, parts)
    iface_ref[...] = total
    half = total.astype(BF16)
    for r in range(send_ref.shape[0]):
        send_ref[r] = half


def driven(recv_ref, right_ref, rows_ref):
    hi = rows_ref[0:1, :].astype(jnp.int32)
    volts = recv_ref[...].reshape(ROWS * SCEN, BLOCK)
    found = sum(dot(part, right_ref[...]) for part in (halves(volts) if volts.dtype == F32 else (volts,)))
    picked = jnp.zeros((SCEN, OWN), F32)
    for n in range(ROWS):
        picked += jnp.where(hi == paired_sender(n), found[n * SCEN : (n + 1) * SCEN, :], 0.0)
    return (rows_ref[1:2, :] * picked).astype(BF16)


def update(k, drive, open_ref, inv, volt, curr, breaker_ref, gain_ref):
    volt_next = open_ref[k] + dot(drive[:, k * PORTS : (k + 1) * PORTS], inv)
    closed = breaker_ref[k].astype(F32)
    return volt_next, closed * (curr + gain_ref[k : k + 1, :] * (volt_next + volt))


def paired_sender(place):
    return CORES[place // (ROWS // 2)][place % (ROWS // 2)]


def middle_kernel(time_ref, node_ref, recv_ref, prev_ref, volt_ref, curr_ref, breaker_ref, gain_ref, tie_ref, right_ref, rows_ref, inv_ref, volt_out, curr_out, open_ref, send_ref):
    drive = driven(recv_ref, right_ref, rows_ref)
    for k in range(SUBS):
        volt_out[k], curr_out[k] = update(k, drive, prev_ref, inv_ref[k, :PORTS, :], volt_ref[k], curr_ref[k], breaker_ref, gain_ref)
    open_circuit(1, volt_out, curr_out, breaker_ref, gain_ref, None, inv_ref, time_ref, node_ref, tie_ref, open_ref, send_ref)


def last_kernel(recv_ref, prev_ref, volt_ref, curr_ref, breaker_ref, gain_ref, right_ref, rows_ref, face_ref, inv_hbm, volt_out, curr_out, face_out, inv_ref, sems):
    copies = fetch([inv_hbm.at[k, pl.ds(0, PORTS)] for k in range(SUBS)], each(inv_ref, SUBS), sems)
    face_out[...] = face_ref[...]
    drive = driven(recv_ref, right_ref, rows_ref)
    wait_for(copies)
    for k in range(SUBS):
        volt_out[k], curr_out[k] = update(k, drive, prev_ref, inv_ref[k], volt_ref[k], curr_ref[k], breaker_ref, gain_ref)


SMEM = pl.BlockSpec(memory_space=pltpu.SMEM)
VMEM = pl.BlockSpec(memory_space=pltpu.VMEM)
HBM = pl.BlockSpec(memory_space=pltpu.HBM)

STATE = ((SUBS, SCEN, NODES), F32)
RHS = ((COLS, SCEN, LANES), BF16)
MAPS = ((ROWS, MAP_ROWS, LANES), F32)
FACE = (ROWS, SCEN, BLOCK)
GIGA = 1_000_000_000


def held(*shapes):
    return [pltpu.VMEM(*shape) for shape in shapes]


def copies_of(count):
    return [pltpu.SemaphoreType.DMA((count,))]


GAIN, TIE = held(((SUBS, NODES), F32), ((SUBS, PORTS), F32))
BREAKER = held(((SUBS, SCEN, NODES), jnp.int32))
INVERSE = held(((SUBS, NODES, NODES), BF16))
PICK = [((BLOCK, OWN), BF16), ((8, OWN), F32)]


def call(body, ins, outs, scratch, flops, moved, vmem=VMEM_BYTES):
    return pl.pallas_call(
        body,
        out_shape=[jax.ShapeDtypeStruct(shape, kind) for shape, kind in outs],
        in_specs=ins,
        out_specs=[VMEM] * len(outs),
        scratch_shapes=scratch,
        compiler_params=pltpu.CompilerParams(vmem_limit_bytes=vmem),
        cost_estimate=pl.CostEstimate(flops=flops, bytes_accessed=moved, transcendentals=0),
    )


first = call(
    first_kernel,
    [SMEM] * 2 + [HBM] * 7,
    [STATE, ((ROWS // 2, VALUE_ROWS + MAP_ROWS, LANES), F32)] + PICK,
    held(((SUBS, PORTS), jnp.int32)) + [GAIN, TIE] + held(STATE, STATE) + BREAKER + INVERSE + copies_of(6 + SUBS),
    GIGA,
    4 << 20,
    ALL_VMEM,
)
join = call(join_kernel, [VMEM] * 5, [((2, 2, BLOCK, LANES), BF16)] * 2, [], 100_000 * GIGA, 1 << 20, 8 << 20)
summed = call(rhs_kernel, [VMEM], [RHS, MAPS], [], GIGA, 1 << 20)
product = call(product_kernel, [VMEM] * 9, [((ROWS // 2, SCEN, BLOCK), F32)], [], GIGA, 3 << 20)
interface = call(interface_kernel, [VMEM] * 10, [(FACE[1:], F32), ((ROWS // 2, SCEN, BLOCK), BF16)], held(RHS), GIGA, 3 << 20)
middle = call(middle_kernel, [SMEM] * 2 + [VMEM] * 10, [STATE, STATE, STATE, ((ROWS // 2, VALUE_ROWS, LANES), BF16)], [], GIGA, 4 << 20)
last = call(
    last_kernel,
    [VMEM] * 9 + [HBM],
    [STATE, STATE, (FACE[1:], F32)],
    held(((SUBS, PORTS, NODES), BF16)) + copies_of(SUBS),
    GIGA,
    2 << 20,
)


def along_z(block, flip):
    return lax.ppermute(block, "col", [(c, c ^ flip) for c in range(COLS)])


def along_y(block, steps):
    return lax.ppermute(block, "col", [(c, (c + 8 * steps) % COLS) for c in range(COLS)])


def exchange(send, groups):
    return lax.all_to_all(send, "row", 0, 0, axis_index_groups=groups)


def paired_exchange(send):
    both = lax.all_gather(exchange(send, CORES), "row", axis_index_groups=PAIRS)
    return both.reshape(ROWS, *send.shape[1:])


def local(volt, curr, local_inverse, schur_inverse, ind_gain, tie, port_map, breaker, fault_time, fault_node):
    with jax.named_scope("schur_z"):
        across = along_z(schur_inverse, 4)
    opened, send, *pick = first(fault_time, fault_node, volt, curr, breaker, ind_gain, tie, port_map, local_inverse)
    across, send = lax.optimization_barrier((across, send))
    with jax.named_scope("schur_z"):
        pair = jnp.stack([schur_inverse, across])
        low, high = join(schur_inverse, across, *(along_z(pair, x) for x in (1, 2, 3)))
    with jax.named_scope("schur_y"):
        back, ahead = along_y(low, 1), along_y(high, -1)
        schur_rows = low, high, back, along_y(high, 1), along_y(back, 1), along_y(ahead, -1), along_y(low, -1), ahead
    rhs, maps = summed(paired_exchange(send))
    (send,) = product(rhs, *schur_rows)
    volt, curr, opened, send = middle(fault_time, fault_node, paired_exchange(send), opened, volt, curr, breaker, ind_gain, tie, *pick, local_inverse)
    face, send = interface(paired_exchange(send), maps, *schur_rows)
    return tuple(last(paired_exchange(send), opened, volt, curr, breaker, ind_gain, *pick, face, local_inverse))


def solution(mesh):
    placed = (
        P("row", "col", None),
        P("row", "col", None),
        P("row", None, None),
        P("row", "col"),
        P("row", None),
        P("row", None),
        P("row", None),
        P("row", "col", None),
        P("col"),
        P("col"),
    )
    return jax.shard_map(
        local,
        mesh=mesh,
        in_specs=placed,
        out_specs=(P("row", "col", None), P("row", "col", None), P("col", "row")),
        check_vma=False,
    )
```

```python
import jax
import jax.numpy as jnp
from jax import lax
from jax.experimental import pallas as pl
from jax.experimental.pallas import tpu as pltpu
from jax.sharding import PartitionSpec as P

ROWS = 16
COLS = 32
SUBS = 8
SCEN = 16
NODES = 400
PORTS = 64
OWN = SUBS * PORTS
BLOCK = 256
LANES = 128
TILES = OWN // LANES
VALUE_ROWS = TILES * SCEN
MAP_ROWS = 2 * TILES
TURNED = [ROWS - 1 - n for n in range(ROWS)]
CORES = [[r for r in TURNED if r % 2 == core] for core in range(2)]
PAIRS = [[2 * n, 2 * n + 1] for n in range(ROWS // 2)]
VMEM_BYTES = 16 << 20
ALL_VMEM = 60 << 20
BF16, F32 = jnp.bfloat16, jnp.float32

NN = (((1,), (0,)), ((), ()))
NT = (((1,), (1,)), ((), ()))


def dot(a, b, dims=NN):
    return lax.dot_general(a, b, dims, preferred_element_type=F32)


def halves(x):
    coarse = x.astype(BF16)
    return coarse, (x - coarse.astype(F32)).astype(BF16)


def fetch(sources, targets, sems):
    copies = [pltpu.make_async_copy(a, b, sems.at[n]) for n, (a, b) in enumerate(zip(sources, targets))]
    for copy in copies:
        copy.start()
    return copies


def wait_for(copies):
    for copy in copies:
        copy.wait()


def each(ref, count):
    return [ref.at[k] for k in range(count)]


def flat_row(ref):
    return jnp.concatenate([ref[k : k + 1, :] for k in range(SUBS)], axis=1)


def tiles_of(row):
    return [row[:, t * LANES : (t + 1) * LANES] for t in range(TILES)]


def column(ref):
    place = lax.broadcasted_iota(jnp.int32, (SCEN, 1), 0)
    out = jnp.zeros((SCEN, 1), jnp.int32)
    for s in range(SCEN):
        out = jnp.where(place == s, ref[s], out)
    return out


def open_circuit(step, volts, currs, breaker_ref, gain_ref, inv_copies, inv_ref, time_ref, node_ref, tie_ref, open_ref, send_ref):
    fault_node = jnp.where(step >= column(time_ref), column(node_ref), -1)
    first = lax.axis_index("row") * SUBS
    lane = lax.broadcasted_iota(jnp.int32, (SCEN, NODES), 1)
    parts = []
    for k in range(SUBS):
        volt = volts[k]
        hist = breaker_ref[k].astype(F32) * (currs[k] + gain_ref[k : k + 1, :] * volt)
        hit = lane + (first + k) * NODES == fault_node
        inject = (-hist - jnp.where(hit, 2.0 * volt, 0.0)).astype(BF16)
        if inv_copies:
            inv_copies[k].wait()
        open_k = dot(inject, inv_ref[k])
        open_ref[k] = open_k
        parts.append(tie_ref[k : k + 1, :] * open_k[:, :PORTS])
    values = jnp.concatenate(parts, axis=1).astype(send_ref.dtype)
    for t, tile in enumerate(tiles_of(values)):
        for r in range(send_ref.shape[0]):
            send_ref[r, t * SCEN : (t + 1) * SCEN, :] = tile


def first_kernel(time_ref, node_ref, volt_hbm, curr_hbm, breaker_hbm, gain_hbm, tie_hbm, map_hbm, inv_hbm, open_ref, send_ref, right_ref, rows_ref, map_ref, gain_ref, tie_ref, volt_ref, curr_ref, breaker_ref, inv_ref, sems):
    copies = fetch(
        [map_hbm, gain_hbm, tie_hbm, volt_hbm, curr_hbm, breaker_hbm] + each(inv_hbm, SUBS),
        [map_ref, gain_ref, tie_ref, volt_ref, curr_ref, breaker_ref] + each(inv_ref, SUBS),
        sems,
    )
    copies[0].wait()
    mapped = flat_row(map_ref)
    rows = tiles_of((mapped // BLOCK).astype(F32)) + tiles_of((mapped % BLOCK).astype(F32))
    tail = jnp.concatenate(rows, axis=0)
    for r in range(send_ref.shape[0]):
        send_ref[r, VALUE_ROWS:, :] = tail
    wait_for(copies[1:6])
    low = lax.broadcasted_iota(jnp.int32, (BLOCK, OWN), 0)
    right_ref[...] = jnp.where(low == mapped % BLOCK, 1.0, 0.0).astype(BF16)
    rows_ref[...] = jnp.concatenate([(mapped // BLOCK).astype(F32), flat_row(tie_ref), jnp.zeros((6, OWN), F32)], axis=0)
    open_circuit(0, volt_ref, curr_ref, breaker_ref, gain_ref, copies[6:], inv_ref, time_ref, node_ref, tie_ref, open_ref, send_ref)


def right_hand_side(recv_ref, map_ref):
    low = lax.broadcasted_iota(jnp.int32, (BLOCK, OWN), 0).astype(F32).astype(BF16)
    one, zero = jnp.ones((), BF16), jnp.zeros((), BF16)
    rhs = jnp.zeros((ROWS * SCEN, BLOCK), F32)
    for r in range(ROWS):
        tail = map_ref[r]
        hi = jnp.concatenate([tail[t : t + 1] for t in range(TILES)], axis=1)
        lo = jnp.concatenate([tail[TILES + t : TILES + t + 1] for t in range(TILES)], axis=1)
        hi = jnp.broadcast_to(hi, (SCEN, OWN)).astype(BF16)
        right = jnp.where(low == lo.astype(BF16), one, zero)
        values = jnp.concatenate([recv_ref[r, t * SCEN : (t + 1) * SCEN, :] for t in range(TILES)], axis=1)
        for part in halves(values) if values.dtype == F32 else (values,):
            left = jnp.concatenate([jnp.where(hi == h, part, zero) for h in range(ROWS)], axis=0)
            rhs += dot(left, right, NT)
    return rhs.astype(BF16).reshape(ROWS, SCEN, BLOCK)


def join_kernel(own_ref, across_ref, near_ref, mid_ref, far_ref, low_ref, high_ref):
    low_ref[0, 0] = own_ref[...]
    low_ref[0, 1] = across_ref[...]
    low_ref[1] = near_ref[...]
    high_ref[0] = mid_ref[...]
    high_ref[1] = far_ref[...]


def schur_product(rhs_ref, parts):
    parts = [parts[2 * y : 2 * y + 2] for y in range(4)]
    col = lax.axis_index("col")
    own_y, own_z = col // 8, col % 8
    left, right = [], []
    for n in range(4):
        for x in range(4):
            for o in range(2):
                left.append(rhs_ref[8 * ((own_y + 4 - n) % 4) + jnp.bitwise_xor(own_z, x + 4 * o)])
                right.append(parts[n][x // 2][x % 2, o])
    return dot(jnp.concatenate(left, axis=1), jnp.concatenate(right, axis=1), NT)


def keep(rhs, rhs_ref):
    for h in range(ROWS):
        for side in range(2):
            rhs_ref[2 * h + side] = rhs[h, :, side * LANES : (side + 1) * LANES]


def rhs_kernel(recv_ref, rhs_ref, map_out):
    map_out[...] = recv_ref[:, VALUE_ROWS:, :]
    keep(right_hand_side(recv_ref, map_out), rhs_ref)


def product_kernel(rhs_ref, *refs):
    parts, (send_ref,) = refs[:8], refs[8:]
    total = schur_product(rhs_ref, parts)
    for r in range(send_ref.shape[0]):
        send_ref[r] = total


def interface_kernel(recv_ref, map_ref, *refs):
    parts, (iface_ref, send_ref, rhs_ref) = refs[:8], refs[8:]
    keep(right_hand_side(recv_ref, map_ref), rhs_ref)
    total = schur_product(rhs_ref, parts)
    iface_ref[...] = total
    half = total.astype(BF16)
    for r in range(send_ref.shape[0]):
        send_ref[r] = half


def driven(recv_ref, right_ref, rows_ref):
    hi = rows_ref[0:1, :].astype(jnp.int32)
    volts = recv_ref[...].reshape(ROWS * SCEN, BLOCK)
    found = sum(dot(part, right_ref[...]) for part in (halves(volts) if volts.dtype == F32 else (volts,)))
    picked = jnp.zeros((SCEN, OWN), F32)
    for n in range(ROWS):
        picked += jnp.where(hi == paired_sender(n), found[n * SCEN : (n + 1) * SCEN, :], 0.0)
    return (rows_ref[1:2, :] * picked).astype(BF16)


def update(k, drive, open_ref, inv, volt, curr, breaker_ref, gain_ref):
    volt_next = open_ref[k] + dot(drive[:, k * PORTS : (k + 1) * PORTS], inv)
    closed = breaker_ref[k].astype(F32)
    return volt_next, closed * (curr + gain_ref[k : k + 1, :] * (volt_next + volt))


def paired_sender(place):
    return CORES[place // (ROWS // 2)][place % (ROWS // 2)]


def middle_kernel(time_ref, node_ref, recv_ref, prev_ref, volt_ref, curr_ref, breaker_ref, gain_ref, tie_ref, right_ref, rows_ref, inv_ref, volt_out, curr_out, open_ref, send_ref):
    drive = driven(recv_ref, right_ref, rows_ref)
    for k in range(SUBS):
        volt_out[k], curr_out[k] = update(k, drive, prev_ref, inv_ref[k, :PORTS, :], volt_ref[k], curr_ref[k], breaker_ref, gain_ref)
    open_circuit(1, volt_out, curr_out, breaker_ref, gain_ref, None, inv_ref, time_ref, node_ref, tie_ref, open_ref, send_ref)


def last_kernel(recv_ref, prev_ref, volt_ref, curr_ref, breaker_ref, gain_ref, right_ref, rows_ref, face_ref, inv_ref, volt_out, curr_out, face_out):
    face_out[...] = face_ref[...]
    drive = driven(recv_ref, right_ref, rows_ref)
    for k in range(SUBS):
        volt_out[k], curr_out[k] = update(k, drive, prev_ref, inv_ref[k, :PORTS, :], volt_ref[k], curr_ref[k], breaker_ref, gain_ref)


SMEM = pl.BlockSpec(memory_space=pltpu.SMEM)
VMEM = pl.BlockSpec(memory_space=pltpu.VMEM)
HBM = pl.BlockSpec(memory_space=pltpu.HBM)

STATE = ((SUBS, SCEN, NODES), F32)
RHS = ((COLS, SCEN, LANES), BF16)
MAPS = ((ROWS, MAP_ROWS, LANES), F32)
FACE = (ROWS, SCEN, BLOCK)
GIGA = 1_000_000_000


def held(*shapes):
    return [pltpu.VMEM(*shape) for shape in shapes]


def copies_of(count):
    return [pltpu.SemaphoreType.DMA((count,))]


GAIN, TIE = held(((SUBS, NODES), F32), ((SUBS, PORTS), F32))
BREAKER = held(((SUBS, SCEN, NODES), jnp.int32))
INVERSE = held(((SUBS, NODES, NODES), BF16))
PICK = [((BLOCK, OWN), BF16), ((8, OWN), F32)]


def call(body, ins, outs, scratch, flops, moved, vmem=VMEM_BYTES):
    return pl.pallas_call(
        body,
        out_shape=[jax.ShapeDtypeStruct(shape, kind) for shape, kind in outs],
        in_specs=ins,
        out_specs=[VMEM] * len(outs),
        scratch_shapes=scratch,
        compiler_params=pltpu.CompilerParams(vmem_limit_bytes=vmem),
        cost_estimate=pl.CostEstimate(flops=flops, bytes_accessed=moved, transcendentals=0),
    )


first = call(
    first_kernel,
    [SMEM] * 2 + [HBM] * 7,
    [STATE, ((ROWS // 2, VALUE_ROWS + MAP_ROWS, LANES), F32)] + PICK,
    held(((SUBS, PORTS), jnp.int32)) + [GAIN, TIE] + held(STATE, STATE) + BREAKER + INVERSE + copies_of(6 + SUBS),
    GIGA,
    4 << 20,
    ALL_VMEM,
)
join = call(join_kernel, [VMEM] * 5, [((2, 2, BLOCK, LANES), BF16)] * 2, [], 100_000 * GIGA, 1 << 20, 8 << 20)
summed = call(rhs_kernel, [VMEM], [RHS, MAPS], [], GIGA, 1 << 20)
product = call(product_kernel, [VMEM] * 9, [((ROWS // 2, SCEN, BLOCK), F32)], [], GIGA, 3 << 20)
interface = call(interface_kernel, [VMEM] * 10, [(FACE[1:], F32), ((ROWS // 2, SCEN, BLOCK), BF16)], held(RHS), GIGA, 3 << 20)
middle = call(middle_kernel, [SMEM] * 2 + [VMEM] * 10, [STATE, STATE, STATE, ((ROWS // 2, VALUE_ROWS, LANES), BF16)], [], GIGA, 4 << 20)
last = call(
    last_kernel,
    [VMEM] * 10,
    [STATE, STATE, (FACE[1:], F32)],
    [],
    GIGA,
    2 << 20,
)


def along_z(block, flip):
    return lax.ppermute(block, "col", [(c, c ^ flip) for c in range(COLS)])


def along_y(block, steps):
    return lax.ppermute(block, "col", [(c, (c + 8 * steps) % COLS) for c in range(COLS)])


def exchange(send, groups):
    return lax.all_to_all(send, "row", 0, 0, axis_index_groups=groups)


def paired_exchange(send):
    both = lax.all_gather(exchange(send, CORES), "row", axis_index_groups=PAIRS)
    return both.reshape(ROWS, *send.shape[1:])


def local(volt, curr, local_inverse, schur_inverse, ind_gain, tie, port_map, breaker, fault_time, fault_node):
    with jax.named_scope("schur_z"):
        across = along_z(schur_inverse, 4)
    opened, send, *pick = first(fault_time, fault_node, volt, curr, breaker, ind_gain, tie, port_map, local_inverse)
    across, send = lax.optimization_barrier((across, send))
    with jax.named_scope("schur_z"):
        pair = jnp.stack([schur_inverse, across])
        low, high = join(schur_inverse, across, *(along_z(pair, x) for x in (1, 2, 3)))
    with jax.named_scope("schur_y"):
        back, ahead = along_y(low, 1), along_y(high, -1)
        schur_rows = low, high, back, along_y(high, 1), along_y(back, 1), along_y(ahead, -1), along_y(low, -1), ahead
    rhs, maps = summed(paired_exchange(send))
    (send,) = product(rhs, *schur_rows)
    volt, curr, opened, send = middle(fault_time, fault_node, paired_exchange(send), opened, volt, curr, breaker, ind_gain, tie, *pick, local_inverse)
    face, send = interface(paired_exchange(send), maps, *schur_rows)
    return tuple(last(paired_exchange(send), opened, volt, curr, breaker, ind_gain, *pick, face, local_inverse))


def solution(mesh):
    placed = (
        P("row", "col", None),
        P("row", "col", None),
        P("row", None, None),
        P("row", "col"),
        P("row", None),
        P("row", None),
        P("row", None),
        P("row", "col", None),
        P("col"),
        P("col"),
    )
    return jax.shard_map(
        local,
        mesh=mesh,
        in_specs=placed,
        out_specs=(P("row", "col", None), P("row", "col", None), P("col", "row")),
        check_vma=False,
    )
```

```python
import jax
import jax.numpy as jnp
from jax import lax
from jax.experimental import pallas as pl
from jax.experimental.pallas import tpu as pltpu
from jax.sharding import PartitionSpec as P

ROWS = 16
COLS = 32
SUBS = 8
SCEN = 16
NODES = 400
PORTS = 64
OWN = SUBS * PORTS
BLOCK = 256
LANES = 128
TILES = OWN // LANES
VALUE_ROWS = TILES * SCEN
MAP_ROWS = 2 * TILES
TURNED = [ROWS - 1 - n for n in range(ROWS)]
CORES = [[r for r in TURNED if r % 2 == core] for core in range(2)]
PAIRS = [[2 * n, 2 * n + 1] for n in range(ROWS // 2)]
VMEM_BYTES = 16 << 20
ALL_VMEM = 60 << 20
BF16, F32 = jnp.bfloat16, jnp.float32

NN = (((1,), (0,)), ((), ()))
NT = (((1,), (1,)), ((), ()))


def dot(a, b, dims=NN):
    return lax.dot_general(a, b, dims, preferred_element_type=F32)


def halves(x):
    coarse = x.astype(BF16)
    return coarse, (x - coarse.astype(F32)).astype(BF16)


def fetch(sources, targets, sems):
    copies = [pltpu.make_async_copy(a, b, sems.at[n]) for n, (a, b) in enumerate(zip(sources, targets))]
    for copy in copies:
        copy.start()
    return copies


def wait_for(copies):
    for copy in copies:
        copy.wait()


def each(ref, count):
    return [ref.at[k] for k in range(count)]


def flat_row(ref):
    return jnp.concatenate([ref[k : k + 1, :] for k in range(SUBS)], axis=1)


def tiles_of(row):
    return [row[:, t * LANES : (t + 1) * LANES] for t in range(TILES)]


def column(ref):
    place = lax.broadcasted_iota(jnp.int32, (SCEN, 1), 0)
    out = jnp.zeros((SCEN, 1), jnp.int32)
    for s in range(SCEN):
        out = jnp.where(place == s, ref[s], out)
    return out


def open_circuit(step, volts, currs, breaker_ref, gain_ref, inv_copies, inv_ref, time_ref, node_ref, tie_ref, open_ref, send_ref):
    fault_node = jnp.where(step >= column(time_ref), column(node_ref), -1)
    first = lax.axis_index("row") * SUBS
    lane = lax.broadcasted_iota(jnp.int32, (SCEN, NODES), 1)
    parts = []
    for k in range(SUBS):
        volt = volts[k]
        hist = breaker_ref[k].astype(F32) * (currs[k] + gain_ref[k : k + 1, :] * volt)
        hit = lane + (first + k) * NODES == fault_node
        inject = (-hist - jnp.where(hit, 2.0 * volt, 0.0)).astype(BF16)
        if inv_copies:
            inv_copies[k].wait()
        open_k = dot(inject, inv_ref[k])
        open_ref[k] = open_k
        parts.append(tie_ref[k : k + 1, :] * open_k[:, :PORTS])
    values = jnp.concatenate(parts, axis=1).astype(send_ref.dtype)
    for t, tile in enumerate(tiles_of(values)):
        for r in range(send_ref.shape[0]):
            send_ref[r, t * SCEN : (t + 1) * SCEN, :] = tile


def first_kernel(time_ref, node_ref, volt_hbm, curr_hbm, breaker_hbm, gain_hbm, tie_hbm, map_hbm, inv_hbm, open_ref, send_ref, right_ref, rows_ref, map_ref, gain_ref, tie_ref, volt_ref, curr_ref, breaker_ref, inv_ref, sems):
    copies = fetch(
        [map_hbm, gain_hbm, tie_hbm, volt_hbm, curr_hbm, breaker_hbm] + each(inv_hbm, SUBS),
        [map_ref, gain_ref, tie_ref, volt_ref, curr_ref, breaker_ref] + each(inv_ref, SUBS),
        sems,
    )
    copies[0].wait()
    mapped = flat_row(map_ref)
    rows = tiles_of((mapped // BLOCK).astype(F32)) + tiles_of((mapped % BLOCK).astype(F32))
    tail = jnp.concatenate(rows, axis=0)
    for r in range(send_ref.shape[0]):
        send_ref[r, VALUE_ROWS:, :] = tail
    wait_for(copies[1:6])
    low = lax.broadcasted_iota(jnp.int32, (BLOCK, OWN), 0)
    right_ref[...] = jnp.where(low == mapped % BLOCK, 1.0, 0.0).astype(BF16)
    rows_ref[...] = jnp.concatenate([(mapped // BLOCK).astype(F32), flat_row(tie_ref), jnp.zeros((6, OWN), F32)], axis=0)
    open_circuit(0, volt_ref, curr_ref, breaker_ref, gain_ref, copies[6:], inv_ref, time_ref, node_ref, tie_ref, open_ref, send_ref)


def right_hand_side(recv_ref, map_ref):
    low = lax.broadcasted_iota(jnp.int32, (BLOCK, OWN), 0).astype(F32).astype(BF16)
    one, zero = jnp.ones((), BF16), jnp.zeros((), BF16)
    rhs = jnp.zeros((ROWS * SCEN, BLOCK), F32)
    for r in range(ROWS):
        tail = map_ref[r]
        hi = jnp.concatenate([tail[t : t + 1] for t in range(TILES)], axis=1)
        lo = jnp.concatenate([tail[TILES + t : TILES + t + 1] for t in range(TILES)], axis=1)
        hi = jnp.broadcast_to(hi, (SCEN, OWN)).astype(BF16)
        right = jnp.where(low == lo.astype(BF16), one, zero)
        values = jnp.concatenate([recv_ref[r, t * SCEN : (t + 1) * SCEN, :] for t in range(TILES)], axis=1)
        for part in halves(values) if values.dtype == F32 else (values,):
            left = jnp.concatenate([jnp.where(hi == h, part, zero) for h in range(ROWS)], axis=0)
            rhs += dot(left, right, NT)
    return rhs.astype(BF16).reshape(ROWS, SCEN, BLOCK)


def join_kernel(own_ref, across_ref, near_ref, mid_ref, far_ref, low_ref, high_ref):
    low_ref[0, 0] = own_ref[...]
    low_ref[0, 1] = across_ref[...]
    low_ref[1] = near_ref[...]
    high_ref[0] = mid_ref[...]
    high_ref[1] = far_ref[...]


def schur_product(rhs_ref, parts):
    parts = [parts[2 * y : 2 * y + 2] for y in range(4)]
    col = lax.axis_index("col")
    own_y, own_z = col // 8, col % 8
    left, right = [], []
    for n in range(4):
        for x in range(4):
            for o in range(2):
                left.append(rhs_ref[8 * ((own_y + 4 - n) % 4) + jnp.bitwise_xor(own_z, x + 4 * o)])
                right.append(parts[n][x // 2][x % 2, o])
    return dot(jnp.concatenate(left, axis=1), jnp.concatenate(right, axis=1), NT)


def keep(rhs, rhs_ref):
    for h in range(ROWS):
        for side in range(2):
            rhs_ref[2 * h + side] = rhs[h, :, side * LANES : (side + 1) * LANES]


def rhs_kernel(recv_ref, rhs_ref, map_out):
    map_out[...] = recv_ref[:, VALUE_ROWS:, :]
    keep(right_hand_side(recv_ref, map_out), rhs_ref)


def product_kernel(rhs_ref, *refs):
    parts, (send_ref,) = refs[:8], refs[8:]
    total = schur_product(rhs_ref, parts)
    for r in range(send_ref.shape[0]):
        send_ref[r] = total


def interface_kernel(recv_ref, map_ref, *refs):
    parts, (iface_ref, send_ref, rhs_ref) = refs[:8], refs[8:]
    keep(right_hand_side(recv_ref, map_ref), rhs_ref)
    total = schur_product(rhs_ref, parts)
    iface_ref[...] = total
    half = total.astype(BF16)
    for r in range(send_ref.shape[0]):
        send_ref[r] = half


def driven(recv_ref, right_ref, rows_ref):
    hi = rows_ref[0:1, :].astype(jnp.int32)
    volts = recv_ref[...].reshape(ROWS * SCEN, BLOCK)
    found = sum(dot(part, right_ref[...]) for part in (halves(volts) if volts.dtype == F32 else (volts,)))
    picked = jnp.zeros((SCEN, OWN), F32)
    for n in range(ROWS):
        picked += jnp.where(hi == paired_sender(n), found[n * SCEN : (n + 1) * SCEN, :], 0.0)
    return (rows_ref[1:2, :] * picked).astype(BF16)


def update(k, drive, open_ref, inv, volt, curr, breaker_ref, gain_ref):
    volt_next = open_ref[k] + dot(drive[:, k * PORTS : (k + 1) * PORTS], inv)
    closed = breaker_ref[k].astype(F32)
    return volt_next, closed * (curr + gain_ref[k : k + 1, :] * (volt_next + volt))


def paired_sender(place):
    return CORES[place // (ROWS // 2)][place % (ROWS // 2)]


def middle_kernel(time_ref, node_ref, recv_ref, prev_ref, volt_ref, curr_ref, breaker_ref, gain_ref, tie_ref, right_ref, rows_ref, inv_ref, volt_out, curr_out, open_ref, send_ref):
    drive = driven(recv_ref, right_ref, rows_ref)
    volts, currs = zip(*(update(k, drive, prev_ref, inv_ref[k, :PORTS, :], volt_ref[k], curr_ref[k], breaker_ref, gain_ref) for k in range(SUBS)))
    for k in range(SUBS):
        volt_out[k], curr_out[k] = volts[k], currs[k]
    open_circuit(1, volts, currs, breaker_ref, gain_ref, None, inv_ref, time_ref, node_ref, tie_ref, open_ref, send_ref)


def last_kernel(recv_ref, prev_ref, volt_ref, curr_ref, breaker_ref, gain_ref, right_ref, rows_ref, face_ref, inv_ref, volt_out, curr_out, face_out):
    face_out[...] = face_ref[...]
    drive = driven(recv_ref, right_ref, rows_ref)
    for k in range(SUBS):
        volt_out[k], curr_out[k] = update(k, drive, prev_ref, inv_ref[k, :PORTS, :], volt_ref[k], curr_ref[k], breaker_ref, gain_ref)


SMEM = pl.BlockSpec(memory_space=pltpu.SMEM)
VMEM = pl.BlockSpec(memory_space=pltpu.VMEM)
HBM = pl.BlockSpec(memory_space=pltpu.HBM)

STATE = ((SUBS, SCEN, NODES), F32)
RHS = ((COLS, SCEN, LANES), BF16)
MAPS = ((ROWS, MAP_ROWS, LANES), F32)
FACE = (ROWS, SCEN, BLOCK)
GIGA = 1_000_000_000


def held(*shapes):
    return [pltpu.VMEM(*shape) for shape in shapes]


def copies_of(count):
    return [pltpu.SemaphoreType.DMA((count,))]


GAIN, TIE = held(((SUBS, NODES), F32), ((SUBS, PORTS), F32))
BREAKER = held(((SUBS, SCEN, NODES), jnp.int32))
INVERSE = held(((SUBS, NODES, NODES), BF16))
PICK = [((BLOCK, OWN), BF16), ((8, OWN), F32)]


def call(body, ins, outs, scratch, flops, moved, vmem=VMEM_BYTES):
    return pl.pallas_call(
        body,
        out_shape=[jax.ShapeDtypeStruct(shape, kind) for shape, kind in outs],
        in_specs=ins,
        out_specs=[VMEM] * len(outs),
        scratch_shapes=scratch,
        compiler_params=pltpu.CompilerParams(vmem_limit_bytes=vmem),
        cost_estimate=pl.CostEstimate(flops=flops, bytes_accessed=moved, transcendentals=0),
    )


first = call(
    first_kernel,
    [SMEM] * 2 + [HBM] * 7,
    [STATE, ((ROWS // 2, VALUE_ROWS + MAP_ROWS, LANES), F32)] + PICK,
    held(((SUBS, PORTS), jnp.int32)) + [GAIN, TIE] + held(STATE, STATE) + BREAKER + INVERSE + copies_of(6 + SUBS),
    GIGA,
    4 << 20,
    ALL_VMEM,
)
join = call(join_kernel, [VMEM] * 5, [((2, 2, BLOCK, LANES), BF16)] * 2, [], 100_000 * GIGA, 1 << 20, 8 << 20)
summed = call(rhs_kernel, [VMEM], [RHS, MAPS], [], GIGA, 1 << 20)
product = call(product_kernel, [VMEM] * 9, [((ROWS // 2, SCEN, BLOCK), F32)], [], GIGA, 3 << 20)
interface = call(interface_kernel, [VMEM] * 10, [(FACE[1:], F32), ((ROWS // 2, SCEN, BLOCK), BF16)], held(RHS), GIGA, 3 << 20)
middle = call(middle_kernel, [SMEM] * 2 + [VMEM] * 10, [STATE, STATE, STATE, ((ROWS // 2, VALUE_ROWS, LANES), BF16)], [], GIGA, 4 << 20)
last = call(
    last_kernel,
    [VMEM] * 10,
    [STATE, STATE, (FACE[1:], F32)],
    [],
    GIGA,
    2 << 20,
)


def along_z(block, flip):
    return lax.ppermute(block, "col", [(c, c ^ flip) for c in range(COLS)])


def along_y(block, steps):
    return lax.ppermute(block, "col", [(c, (c + 8 * steps) % COLS) for c in range(COLS)])


def exchange(send, groups):
    return lax.all_to_all(send, "row", 0, 0, axis_index_groups=groups)


def paired_exchange(send):
    both = lax.all_gather(exchange(send, CORES), "row", axis_index_groups=PAIRS)
    return both.reshape(ROWS, *send.shape[1:])


def local(volt, curr, local_inverse, schur_inverse, ind_gain, tie, port_map, breaker, fault_time, fault_node):
    with jax.named_scope("schur_z"):
        across = along_z(schur_inverse, 4)
    opened, send, *pick = first(fault_time, fault_node, volt, curr, breaker, ind_gain, tie, port_map, local_inverse)
    across, send = lax.optimization_barrier((across, send))
    with jax.named_scope("schur_z"):
        pair = jnp.stack([schur_inverse, across])
        low, high = join(schur_inverse, across, *(along_z(pair, x) for x in (1, 2, 3)))
    with jax.named_scope("schur_y"):
        back, ahead = along_y(low, 1), along_y(high, -1)
        schur_rows = low, high, back, along_y(high, 1), along_y(back, 1), along_y(ahead, -1), along_y(low, -1), ahead
    rhs, maps = summed(paired_exchange(send))
    (send,) = product(rhs, *schur_rows)
    volt, curr, opened, send = middle(fault_time, fault_node, paired_exchange(send), opened, volt, curr, breaker, ind_gain, tie, *pick, local_inverse)
    face, send = interface(paired_exchange(send), maps, *schur_rows)
    return tuple(last(paired_exchange(send), opened, volt, curr, breaker, ind_gain, *pick, face, local_inverse))


def solution(mesh):
    placed = (
        P("row", "col", None),
        P("row", "col", None),
        P("row", None, None),
        P("row", "col"),
        P("row", None),
        P("row", None),
        P("row", None),
        P("row", "col", None),
        P("col"),
        P("col"),
    )
    return jax.shard_map(
        local,
        mesh=mesh,
        in_specs=placed,
        out_specs=(P("row", "col", None), P("row", "col", None), P("col", "row")),
        check_vma=False,
    )
```
